128 devices in a mesh: group: 16 (over y, z), local: 8 (over x, core).
Axes of the slice: x: 4, y: 4, z: 4, core: 2. Of those that a mesh axis runs over, the one named last changes fastest.
Arguments:
- features: float32 [131072, 512], P(('group', 'local'))
- aggregated: float32 [131072, 512], P(('group', 'local')), may hold values from -6 to 6
- preact: float32 [131072, 512], P(('group', 'local')), may hold values from -6 to 6
- grad_out: float32 [131072, 512], P(('group', 'local')), may hold values from -6 to 6
- w_self: float32 [512, 512], replicated, may hold values from -0.25 to 0.25
- w_neigh: float32 [512, 512], replicated, may hold values from -0.25 to 0.25
- tile_vals: float32 [8192, 128, 128], P(('group', 'local')), as said below
- tile_col: int32 [8192], P(('group', 'local')), may hold values from 0 to 39, as said below
- halo_count: int32 [16, 16], replicated, may hold values from 0 to 2, as said below
- halo_target: int32 [16, 32], replicated, may hold values from 0 to 63, as said below
Outputs:
- node_grad: float32 [131072, 512], P(('group', 'local'))
- self_grad: float32 [512, 512], replicated
- neigh_grad: float32 [512, 512], replicated
The draws below stay inside these ranges and needn't reach their ends.
Inputs may be any that keep to these rules, and one draw needn't show every extreme that they name: `halo_count`: no partition sends to itself; for every partition some owner receives 2 slots from it, and one owner partition receives 2 slots from every other partition. `halo_target`: entries of slots that are not live are in range but unused. `tile_col`: A tile's column names a row block of its own device (0 to 7) or 8 plus a live halo slot of its own partition. `tile_vals`: each tile is sparse with nonnegative weights; a row's weights over its 8 tiles sum to about one.
All inputs are finite; a program needn't handle non-finite values.
Results may differ from the reference program's by a relative error of at most 0.0003.
Values sent between devices are 32-bit elements; how exact they have to be, the bound alone decides.
No kernel may reach another device: no remote copies, remote signals or barrier semaphores. Data moves between devices by JAX's collectives and lax.ppermute only.
A program may use at most 192 MiB of HBM per device.

```python
import jax
import jax.numpy as jnp
from jax import lax

F = 512
TILES_ROW = 8
CAP = 2
GROUPS = 16
MEMBERS = 8
ROW_BLOCKS = 8
GROUP_BLOCKS = 64
SLOTS = 32
NODES = 131072
TILES = 8192


def send_counts(key):
    key_one, key_two = jax.random.split(key)
    base = jax.random.randint(key_one, (GROUPS, GROUPS), 0, CAP + 1)
    star = jax.random.randint(key_two, (), 0, GROUPS)
    group_ids = jnp.arange(GROUPS)
    full = (group_ids[None, :] == star) | (group_ids[None, :] == (group_ids[:, None] + 1) % GROUPS)
    counts = jnp.where(full, CAP, base)
    return jnp.where(group_ids[:, None] == group_ids[None, :], 0, counts).astype(jnp.int32)


def draw_halo_count(key, part):
    return send_counts(key)


def draw_halo_target(key, part):
    key = jax.random.fold_in(key, 5)
    key_one, key_two = jax.random.split(key)
    targets = jax.random.randint(key_one, (GROUPS * SLOTS,), 0, GROUP_BLOCKS)
    spots = jax.random.randint(key_two, (2,), 0, GROUPS * SLOTS)
    targets = targets.at[spots[0]].set(GROUP_BLOCKS - 1).at[spots[1]].set(0)
    return targets.reshape(GROUPS, SLOTS).astype(jnp.int32)


def draw_tile_col(key, part):
    counts = send_counts(key)
    key = jax.random.fold_in(key, 7)
    key_one, key_two, key_three = jax.random.split(key, 3)
    tile_ids = jnp.arange(TILES)
    group_ids = tile_ids // (ROW_BLOCKS * TILES_ROW * MEMBERS)
    slot_pick = jax.random.randint(key_one, (TILES,), 0, SLOTS)
    own_block = jax.random.randint(key_two, (TILES,), 0, ROW_BLOCKS)
    choose = jax.random.randint(key_three, (TILES,), 0, 10) < 6
    live_slot = slot_pick % CAP < counts[group_ids, slot_pick // CAP]
    return jnp.where(choose & live_slot, ROW_BLOCKS + slot_pick, own_block).astype(jnp.int32)


def draw_tile_vals(key, part):
    key = jax.random.fold_in(key, 11)
    key_one, key_two = jax.random.split(key)
    degree = 8.0 * TILES_ROW
    keep_mask = (jax.random.randint(key_one, (TILES, 128, 128), 0, 16) == 0).astype(jnp.float32)
    values = jax.random.uniform(key_two, (TILES, 128, 128), jnp.float32, 0.0, 2.0)
    return (keep_mask * values / degree).astype(jnp.float32)


def draw_features(key, part):
    key = jax.random.fold_in(key, 13)
    key_one = jax.random.fold_in(key, 0)
    row_scale = 1.0 + 2.0 * jnp.arange(NODES, dtype=jnp.float32)[:, None] / NODES
    values = jax.random.normal(key_one, (NODES, F), jnp.float32)
    return (values * row_scale).astype(jnp.float32)


def block_levels(key, dims, cuts, smallest, top_value):
    def one(position, parts):
        steps = jax.random.uniform(jax.random.fold_in(jax.random.fold_in(key, 6), position), (parts,), jnp.float32, smallest / len(cuts), top_value / len(cuts))
        return jnp.repeat(jnp.exp(steps), dims[position] // parts).reshape((-1,) + (1,) * (len(dims) - position - 1))

    factor_of = one(*cuts[0])
    for cut in cuts[1:]:
        factor_of = factor_of * one(*cut)
    return factor_of


def centred(key, extent, scale, limit, cuts=(), kind=jnp.bfloat16):
    entries = jax.random.normal(key, extent, jnp.float32) * scale
    if len(cuts) > 0:
        entries = block_levels(key, extent, cuts, -0.22, 0.18) * entries
    return jnp.clip(entries, min=-limit, max=limit).astype(kind)


def setup_inputs(seed: int = 0) -> dict:
    keys = jax.random.split(jax.random.key(seed), 11)
    features = draw_features(jax.random.fold_in(keys[10], 71), 0)
    aggregated = centred(keys[1], (NODES, F), 1.0, 6.0, ((0, 128),), jnp.float32)
    preact = centred(keys[2], (NODES, F), 1.0, 6.0, ((0, 128),), jnp.float32)
    grad_out = centred(keys[3], (NODES, F), 1.0, 6.0, ((0, 128),), jnp.float32)
    w_self = centred(keys[4], (F, F), F ** -0.5, 0.25, (), jnp.float32)
    w_neigh = centred(keys[5], (F, F), F ** -0.5, 0.25, (), jnp.float32)
    tile_vals = draw_tile_vals(jax.random.fold_in(keys[10], 71), 0)
    tile_col = draw_tile_col(jax.random.fold_in(keys[10], 71), 0)
    halo_count = draw_halo_count(jax.random.fold_in(keys[10], 71), 0)
    halo_target = draw_halo_target(jax.random.fold_in(keys[10], 71), 0)
    return dict(features=features, aggregated=aggregated, preact=preact, grad_out=grad_out, w_self=w_self, w_neigh=w_neigh, tile_vals=tile_vals, tile_col=tile_col, halo_count=halo_count, halo_target=halo_target)


def reference(features, aggregated, preact, grad_out, w_self, w_neigh, tile_vals, tile_col, halo_count, halo_target):
    precise = lax.Precision.HIGHEST
    pre_grad = jnp.where(preact > 0, grad_out, jnp.zeros_like(grad_out))
    neigh_rows = jnp.dot(pre_grad, w_neigh.T, precision=precise, preferred_element_type=jnp.float32)
    device_count = GROUPS * MEMBERS
    rows_dev = neigh_rows.reshape(device_count, ROW_BLOCKS, 128, F)
    tiles_dev = tile_vals.reshape(device_count, ROW_BLOCKS, TILES_ROW, 128, 128)
    cols_dev = tile_col.reshape(device_count, ROW_BLOCKS * TILES_ROW)
    slot_ids = jnp.arange(SLOTS, dtype=jnp.int32)

    def per_device(halo_acc, inputs):
        row_block, tile_block, columns, device = inputs
        contrib = jnp.einsum('rkab,raf->rkbf', tile_block, row_block, precision=precise).reshape(-1, 128, F)
        own_pick = (columns[:, None] == jnp.arange(ROW_BLOCKS, dtype=jnp.int32)[None, :]).astype(jnp.float32)
        local_sum = jnp.einsum('tr,tbf->rbf', own_pick, contrib, precision=precise)
        halo_pick = ((columns[:, None] - ROW_BLOCKS) == slot_ids[None, :]).astype(jnp.float32)
        halo_part = jnp.einsum('ts,tbf->sbf', halo_pick, contrib, precision=precise)
        group_id = device // MEMBERS
        current = lax.dynamic_index_in_dim(halo_acc, group_id, 0, keepdims=False)
        halo_acc = lax.dynamic_update_index_in_dim(halo_acc, current + halo_part, group_id, 0)
        return halo_acc, local_sum

    start = jnp.zeros((GROUPS, SLOTS, 128, F), jnp.float32)
    halo_acc, local_sums = lax.scan(per_device, start, (rows_dev, tiles_dev, cols_dev, jnp.arange(device_count, dtype=jnp.int32)))
    owner_group = slot_ids // CAP
    live_mask = ((slot_ids[None, :] % CAP) < halo_count[:, owner_group]).astype(jnp.float32)
    halo_acc = halo_acc * live_mask[:, :, None, None]
    destination = (owner_group[None, :] * GROUP_BLOCKS + halo_target).reshape(-1).astype(jnp.int32)
    blocks = local_sums.reshape(device_count * ROW_BLOCKS, 128, F)
    blocks = blocks.at[destination].add(halo_acc.reshape(-1, 128, F))
    node_grad = jnp.dot(pre_grad, w_self.T, precision=precise, preferred_element_type=jnp.float32) + blocks.reshape(NODES, F)
    scale = float(NODES) ** -0.5
    self_grad = jnp.dot(features.T, pre_grad, precision=precise, preferred_element_type=jnp.float32) * scale
    neigh_grad = jnp.dot(aggregated.T, pre_grad, precision=precise, preferred_element_type=jnp.float32) * scale
    return node_grad, self_grad, neigh_grad
```

```python
import functools

import jax
import jax.numpy as jnp
from jax import lax
from jax.experimental import pallas as pl
from jax.experimental.pallas import tpu as pltpu
from jax.sharding import PartitionSpec as P

F32 = jnp.float32
BF16 = jnp.bfloat16
BLOCK = 128


def split(x):
    high = x.astype(BF16)
    low = (x - high.astype(F32)).astype(BF16)
    return high, low


def tile_kernel(blocks, col_ref, tiles_ref, rows_ref, local_ref, halo_ref, left, product):
    step = pl.program_id(0)
    tiles_row = tiles_ref.shape[0]

    @pl.when(step == 0)
    def _():
        local_ref[...] = jnp.zeros_like(local_ref)
        halo_ref[...] = jnp.zeros_like(halo_ref)

    for k in range(tiles_row):
        high, low = split(tiles_ref[k].T)
        rows = pl.ds(k * BLOCK, BLOCK)
        left[rows, 0:BLOCK] = high
        left[rows, BLOCK : 2 * BLOCK] = high
        left[rows, 2 * BLOCK : 3 * BLOCK] = low
    high, low = split(rows_ref[...])
    right = jnp.concatenate([high, low, high], axis=0)
    product[...] = jnp.dot(left[...], right, preferred_element_type=F32)
    for k in range(tiles_row):
        col = col_ref[step * tiles_row + k]
        rows = pl.ds(k * BLOCK, BLOCK)

        @pl.when(col < blocks)
        def _():
            local_ref[col] += product[rows, :]

        @pl.when(col >= blocks)
        def _():
            halo_ref[col - blocks] += product[rows, :]


def tile_sums(tile_col, tile_vals, neigh_rows, slot_count):
    node_rows, width = neigh_rows.shape
    blocks = node_rows // BLOCK
    tiles_row = tile_vals.shape[0] // blocks
    return pl.pallas_call(
        functools.partial(tile_kernel, blocks),
        out_shape=(
            jax.ShapeDtypeStruct((blocks, BLOCK, width), F32),
            jax.ShapeDtypeStruct((slot_count, BLOCK, width), F32),
        ),
        grid_spec=pltpu.PrefetchScalarGridSpec(
            num_scalar_prefetch=1,
            grid=(blocks,),
            in_specs=[
                pl.BlockSpec((tiles_row, BLOCK, BLOCK), lambda r, col: (r, 0, 0)),
                pl.BlockSpec((BLOCK, width), lambda r, col: (r, 0)),
            ],
            out_specs=[
                pl.BlockSpec((blocks, BLOCK, width), lambda r, col: (0, 0, 0)),
                pl.BlockSpec((slot_count, BLOCK, width), lambda r, col: (0, 0, 0)),
            ],
            scratch_shapes=[
                pltpu.VMEM((tiles_row * BLOCK, 3 * BLOCK), BF16),
                pltpu.VMEM((tiles_row * BLOCK, width), F32),
            ],
        ),
        compiler_params=pltpu.CompilerParams(
            dimension_semantics=("arbitrary",), vmem_limit_bytes=48 * 1024 * 1024
        ),
        cost_estimate=pl.CostEstimate(
            flops=6 * tile_vals.size * width, bytes_accessed=16 * 1024 * 1024, transcendentals=0
        ),
        name="tile_sums",
    )(tile_col, tile_vals, neigh_rows)


def on_device(
    features,
    aggregated,
    preact,
    grad_out,
    w_self,
    w_neigh,
    tile_vals,
    tile_col,
    halo_count,
    halo_target,
):
    high = lax.Precision.HIGH
    node_rows, width = features.shape
    blocks = node_rows // BLOCK
    groups = lax.axis_size("group")
    members = lax.axis_size("local")
    slot_count = halo_target.shape[1]
    capacity = slot_count // groups
    group_id = lax.axis_index("group")
    core = lax.axis_index("local") % 2

    pre_grad = jnp.where(preact > 0, grad_out, jnp.zeros_like(grad_out))
    neigh_rows = jnp.dot(pre_grad, w_neigh.T, precision=high, preferred_element_type=F32)
    local_sum, halo_terms = tile_sums(tile_col, tile_vals, neigh_rows, slot_count)

    slot_ids = jnp.arange(slot_count, dtype=jnp.int32)
    source = slot_ids // capacity
    offset = slot_ids % capacity
    recv_target = halo_target[source, group_id * capacity + offset]
    recv_live = offset < halo_count[source, group_id]
    group_blocks = blocks * members
    place_table = (
        (recv_target[:, None] == jnp.arange(group_blocks, dtype=jnp.int32)[None, :])
        & recv_live[:, None]
    ).astype(F32)
    row_parts = lax.psum_scatter(halo_terms, "local", scatter_dimension=1, tiled=True)
    arrived = lax.all_to_all(row_parts, "group", split_axis=0, concat_axis=0, tiled=True)
    gathered_rows = jnp.einsum("sb,srf->brf", place_table, arrived, precision=high)
    incoming = lax.all_to_all(gathered_rows, "local", split_axis=0, concat_axis=1, tiled=True)

    contract = (((0,), (0,)), ((), ()))
    self_term = lax.dot_general(
        features, pre_grad, contract, precision=high, preferred_element_type=F32
    )
    neigh_term = lax.dot_general(
        aggregated, pre_grad, contract, precision=high, preferred_element_type=F32
    )
    swap = [(i, i ^ 1) for i in range(members)]
    first = core == 0
    mine = jnp.where(first, self_term, neigh_term) + lax.ppermute(
        jnp.where(first, neigh_term, self_term), "local", swap
    )
    shares = lax.all_to_all(
        mine.reshape(groups, -1, width), "group", split_axis=0, concat_axis=0, tiled=True
    )
    total = jnp.sum(shares, axis=0)
    pairs = [(i, i ^ 2) for i in range(members)]
    total = total + lax.ppermute(total, "local", pairs)
    across = [(i, members - 2 - (i - i % 2) + i % 2) for i in range(members)]
    total = total + lax.ppermute(total, "local", across)
    scale = float(node_rows * groups * members) ** (-0.5)
    whole = lax.all_gather(total * scale, "group", tiled=True)
    other = lax.ppermute(whole, "local", swap)
    self_grad = jnp.where(first, whole, other)
    neigh_grad = jnp.where(first, other, whole)

    node_grad = jnp.dot(pre_grad, w_self.T, precision=high, preferred_element_type=F32)
    node_grad = (
        node_grad + local_sum.reshape(node_rows, width) + incoming.reshape(node_rows, width)
    )
    return (node_grad, self_grad, neigh_grad)


def solution(mesh):
    in_specs = (
        P(("group", "local"), None),
        P(("group", "local"), None),
        P(("group", "local"), None),
        P(("group", "local"), None),
        P(),
        P(),
        P(("group", "local"), None, None),
        P(("group", "local")),
        P(),
        P(),
    )
    out_specs = (P(("group", "local"), None), P(), P())
    return jax.shard_map(
        on_device, mesh=mesh, in_specs=in_specs, out_specs=out_specs, check_vma=False
    )
```

```python
import functools

import jax
import jax.numpy as jnp
from jax import lax
from jax.experimental import pallas as pl
from jax.experimental.pallas import tpu as pltpu
from jax.sharding import PartitionSpec as P

F32 = jnp.float32
BF16 = jnp.bfloat16
BLOCK = 128


def split(x):
    high = x.astype(BF16)
    low = (x - high.astype(F32)).astype(BF16)
    return high, low


def tile_kernel(
    blocks,
    want_rows,
    info_ref,
    preact_ref,
    grad_ref,
    weight_ref,
    tiles_ref,
    local_ref,
    keep_ref,
    send_ref,
    *rest,
):
    if want_rows:
        pre_ref, *rest = rest
    left, product, halo, weight, sems = rest
    step = pl.program_id(0)
    tiles_row = 8
    step_rows = preact_ref.shape[0]
    width = weight_ref.shape[0]

    @pl.when(step == 0)
    def _():
        local_ref[...] = jnp.zeros_like(local_ref)
        halo[...] = jnp.zeros_like(halo)
        high, low = split(weight_ref[...])
        weight[0] = high
        weight[1] = low

    pre_grad = jnp.where(preact_ref[...] > 0, grad_ref[...], 0.0)
    if want_rows:
        pre_ref[...] = pre_grad
    pre_high, pre_low = split(pre_grad)
    contract = (((1,), (1,)), ((), ()))
    rows = lax.dot_general(pre_high, weight[0], contract, preferred_element_type=F32)
    rows += lax.dot_general(pre_high, weight[1], contract, preferred_element_type=F32)
    rows += lax.dot_general(pre_low, weight[0], contract, preferred_element_type=F32)
    row_high, row_low = split(rows)
    for r in range(step_rows // BLOCK):
        for k in range(tiles_row):
            high, low = split(tiles_ref[r * tiles_row + k].T)
            at = pl.ds(k * BLOCK, BLOCK)
            left[at, 0:BLOCK] = high
            left[at, BLOCK : 2 * BLOCK] = high
            left[at, 2 * BLOCK : 3 * BLOCK] = low
        mine = slice(r * BLOCK, (r + 1) * BLOCK)
        right = jnp.concatenate([row_high[mine], row_low[mine], row_high[mine]], axis=0)
        product[...] = jnp.dot(left[...], right, preferred_element_type=F32)
        for k in range(tiles_row):
            col = info_ref[step * tiles_ref.shape[0] + r * tiles_row + k]
            at = pl.ds(k * BLOCK, BLOCK)

            @pl.when(col < blocks)
            def _():
                local_ref[col] += product[at, :]

            @pl.when(col >= blocks)
            def _():
                halo[col - blocks] += product[at, :]

    @pl.when(step == pl.num_programs(0) - 1)
    def _():
        half = BLOCK // 2
        core = info_ref[info_ref.shape[0] - 1]
        own = pl.ds(pl.multiple_of(core * half, half), half)
        other = pl.ds(pl.multiple_of((1 - core) * half, half), half)
        out = pltpu.make_async_copy(halo.at[:, other], send_ref, sems.at[0])
        stay = pltpu.make_async_copy(halo.at[:, own], keep_ref, sems.at[1])
        out.start()
        stay.start()
        out.wait()
        stay.wait()


def tile_sums(info, preact, grad_out, weight, tile_vals, slot_count, part, parts, want_rows):
    node_rows, feat = preact.shape
    width = weight.shape[0] // parts
    blocks = node_rows // BLOCK
    tiles_row = tile_vals.shape[0] // blocks
    steps = 4
    step_rows = node_rows // steps
    step_tiles = tile_vals.shape[0] // steps
    out_shape = [
        jax.ShapeDtypeStruct((blocks, BLOCK, width), F32),
        jax.ShapeDtypeStruct((slot_count, BLOCK // 2, width), F32),
        jax.ShapeDtypeStruct((slot_count, BLOCK // 2, width), F32),
    ]
    out_specs = [
        pl.BlockSpec((blocks, BLOCK, width), lambda i, info: (0, 0, 0)),
        pl.BlockSpec(memory_space=pl.ANY),
        pl.BlockSpec(memory_space=pl.ANY),
    ]
    if want_rows:
        out_shape.append(jax.ShapeDtypeStruct((node_rows, feat), F32))
        out_specs.append(pl.BlockSpec((step_rows, feat), lambda i, info: (i, 0)))
    return pl.pallas_call(
        functools.partial(tile_kernel, blocks, want_rows),
        out_shape=out_shape,
        grid_spec=pltpu.PrefetchScalarGridSpec(
            num_scalar_prefetch=1,
            grid=(steps,),
            in_specs=[
                pl.BlockSpec((step_rows, feat), lambda i, info: (i, 0)),
                pl.BlockSpec((step_rows, feat), lambda i, info: (i, 0)),
                pl.BlockSpec((width, feat), lambda i, info: (part, 0)),
                pl.BlockSpec((step_tiles, BLOCK, BLOCK), lambda i, info: (i, 0, 0)),
            ],
            out_specs=out_specs,
            scratch_shapes=[
                pltpu.VMEM((tiles_row * BLOCK, 3 * BLOCK), BF16),
                pltpu.VMEM((tiles_row * BLOCK, width), F32),
                pltpu.VMEM((slot_count, BLOCK, width), F32),
                pltpu.VMEM((2, width, feat), BF16),
                pltpu.SemaphoreType.DMA((2,)),
            ],
        ),
        compiler_params=pltpu.CompilerParams(
            dimension_semantics=("arbitrary",), vmem_limit_bytes=40 * 1024 * 1024
        ),
        cost_estimate=pl.CostEstimate(
            flops=6 * (tile_vals.size + node_rows * feat) * width,
            bytes_accessed=14 * 1024 * 1024,
            transcendentals=0,
        ),
        name="tile_sums",
    )(info, preact, grad_out, weight, tile_vals)


ROWS = 16


def first_kernel(info_ref, keep_ref, recv_ref, keep_a, send_a, keep_b, send_b):
    p = info_ref[1]
    q = info_ref[2]
    for p_at in range(2):
        for q_at, out in ((q, keep_a), (1 - q, send_a)):
            at = pl.ds(pl.multiple_of(p_at * 2 * ROWS + q_at * ROWS, ROWS), ROWS)
            out[:, p_at] = keep_ref[0, :, at] + recv_ref[0, :, at]
    for q_at in range(2):
        for p_at, out in ((p, keep_b), (1 - p, send_b)):
            at = pl.ds(pl.multiple_of(p_at * 2 * ROWS + q_at * ROWS, ROWS), ROWS)
            out[:, q_at] = keep_ref[1, :, at] + recv_ref[1, :, at]


def first_sums(info, keep, recv):
    slots, rows, width = keep.shape
    half = slots // 2
    step = half // 4
    piece = jax.ShapeDtypeStruct((half, 2, ROWS, width), F32)
    whole_spec = pl.BlockSpec((2, step, rows, width), lambda i, info: (0, i, 0, 0))
    piece_spec = pl.BlockSpec((step, 2, ROWS, width), lambda i, info: (i, 0, 0, 0))
    return pl.pallas_call(
        first_kernel,
        out_shape=[piece] * 4,
        grid_spec=pltpu.PrefetchScalarGridSpec(
            num_scalar_prefetch=1,
            grid=(4,),
            in_specs=[whole_spec] * 2,
            out_specs=[piece_spec] * 4,
        ),
        cost_estimate=pl.CostEstimate(
            flops=keep.size, bytes_accessed=12 * keep.size, transcendentals=0
        ),
        name="first_sums",
    )(info, keep.reshape(2, half, rows, width), recv.reshape(2, half, rows, width))


def second_kernel(info_ref, keep_a, recv_a, keep_b, recv_b, out_keep, out_send_a, out_send_b):
    p = info_ref[1]
    q = info_ref[2]
    out_keep[0] = keep_a[:, p] + recv_a[:, p]
    out_send_a[...] = keep_a[:, 1 - p] + recv_a[:, 1 - p]
    out_keep[1] = keep_b[:, q] + recv_b[:, q]
    out_send_b[...] = keep_b[:, 1 - q] + recv_b[:, 1 - q]


def second_sums(info, keep_a, recv_a, keep_b, recv_b):
    half, _, rows, width = keep_a.shape
    step = half // 2
    piece_spec = pl.BlockSpec((step, 2, rows, width), lambda i, info: (i, 0, 0, 0))
    send_spec = pl.BlockSpec((step, rows, width), lambda i, info: (i, 0, 0))
    send = jax.ShapeDtypeStruct((half, rows, width), F32)
    return pl.pallas_call(
        second_kernel,
        out_shape=[jax.ShapeDtypeStruct((2, half, rows, width), F32), send, send],
        grid_spec=pltpu.PrefetchScalarGridSpec(
            num_scalar_prefetch=1,
            grid=(2,),
            in_specs=[piece_spec] * 4,
            out_specs=[
                pl.BlockSpec((2, step, rows, width), lambda i, info: (0, i, 0, 0)),
                send_spec,
                send_spec,
            ],
        ),
        cost_estimate=pl.CostEstimate(
            flops=keep_a.size, bytes_accessed=24 * keep_a.size, transcendentals=0
        ),
        name="second_sums",
    )(info, keep_a, recv_a, keep_b, recv_b)


def third_kernel(keep_ref, recv_a, recv_b, out_ref):
    out_ref[0] = keep_ref[0] + recv_a[...]
    out_ref[1] = keep_ref[1] + recv_b[...]


def third_sums(keep, recv_a, recv_b):
    return pl.pallas_call(
        third_kernel,
        out_shape=jax.ShapeDtypeStruct(keep.shape, F32),
        cost_estimate=pl.CostEstimate(
            flops=keep.size, bytes_accessed=12 * keep.size, transcendentals=0
        ),
        name="third_sums",
    )(keep, recv_a, recv_b)


def place_kernel(target_ref, arrived_ref, out_ref):
    out_ref[...] = jnp.zeros_like(out_ref)

    @pl.loop(0, arrived_ref.shape[0])
    def _(s):
        target = target_ref[s]

        @pl.when(target >= 0)
        def _():
            out_ref[target] += arrived_ref[s]


def place(target, arrived, group_blocks):
    _, rows, width = arrived.shape
    return pl.pallas_call(
        place_kernel,
        out_shape=jax.ShapeDtypeStruct((group_blocks, rows, width), F32),
        grid_spec=pltpu.PrefetchScalarGridSpec(
            num_scalar_prefetch=1,
            grid=(1,),
            in_specs=[pl.BlockSpec(arrived.shape, lambda i, t: (0, 0, 0))],
            out_specs=pl.BlockSpec((group_blocks, rows, width), lambda i, t: (0, 0, 0)),
        ),
        cost_estimate=pl.CostEstimate(
            flops=arrived.size, bytes_accessed=12 * arrived.size, transcendentals=0
        ),
        name="place",
    )(target, arrived)


QUARTER = (0, 1, 3, 2)


def finish_kernel(base_ref, *rest):
    *parts, out_ref = rest
    width = out_ref.shape[1] // len(parts)
    for h, part in enumerate(parts):
        for member in range(part.shape[0]):
            start = (member % 2) * (BLOCK // 2) + QUARTER[member // 2] * ROWS
            at = (slice(start, start + ROWS), slice(h * width, (h + 1) * width))
            out_ref[at] = base_ref[at] + part[member, 0]


def finish(base, parts):
    node_rows, feat = base.shape
    members, blocks, rows, width = parts[0].shape
    part_spec = pl.BlockSpec((members, 1, rows, width), lambda i: (0, i, 0, 0))
    row_spec = pl.BlockSpec((BLOCK, feat), lambda i: (i, 0))
    return pl.pallas_call(
        finish_kernel,
        out_shape=jax.ShapeDtypeStruct((node_rows, feat), F32),
        grid=(blocks,),
        in_specs=[row_spec] + [part_spec] * len(parts),
        out_specs=row_spec,
        cost_estimate=pl.CostEstimate(
            flops=base.size, bytes_accessed=12 * base.size, transcendentals=0
        ),
        name="finish",
    )(base, *parts)


PARTS = 2


def on_device(
    features,
    aggregated,
    preact,
    grad_out,
    w_self,
    w_neigh,
    tile_vals,
    tile_col,
    halo_count,
    halo_target,
):
    high = lax.Precision.HIGH
    node_rows, width = features.shape
    blocks = node_rows // BLOCK
    groups = lax.axis_size("group")
    members = lax.axis_size("local")
    slot_count = halo_target.shape[1]
    capacity = slot_count // groups
    group_id = lax.axis_index("group")
    core = lax.axis_index("local") % 2

    member = lax.axis_index("local")
    chip = member // 2
    side = chip // 2
    pair = (chip % 2) ^ side
    place_info = jnp.stack([core, side, pair]).astype(jnp.int32)
    tile_info = jnp.concatenate([tile_col, core[None].astype(jnp.int32)])
    swap = [(i, i ^ 1) for i in range(members)]
    pairs = [(i, i ^ 2) for i in range(members)]
    across = [(i, members - 2 - (i - i % 2) + i % 2) for i in range(members)]

    slot_ids = jnp.arange(slot_count, dtype=jnp.int32)
    source = slot_ids // capacity
    offset = slot_ids % capacity
    recv_target = halo_target[source, group_id * capacity + offset]
    recv_live = offset < halo_count[source, group_id]
    target = jnp.where(recv_live, recv_target, -1)
    group_blocks = blocks * members

    local_parts = []
    incoming = []
    for part in range(PARTS):
        local_part, keep, send, *rows = tile_sums(
            tile_info, preact, grad_out, w_neigh, tile_vals, slot_count, part, PARTS, part == 0
        )
        if part == 0:
            pre_grad = rows[0]
        local_parts.append(local_part.reshape(node_rows, -1))
        recv = lax.ppermute(send, "local", swap)
        keep_a, send_a, keep_b, send_b = first_sums(place_info, keep, recv)
        recv_a = lax.ppermute(send_a, "local", pairs)
        recv_b = lax.ppermute(send_b, "local", across)
        keep, send_a, send_b = second_sums(place_info, keep_a, recv_a, keep_b, recv_b)
        recv_a = lax.ppermute(send_a, "local", across)
        recv_b = lax.ppermute(send_b, "local", pairs)
        row_part = third_sums(keep, recv_a, recv_b).reshape(slot_count, ROWS, -1)
        arrived = lax.all_to_all(row_part, "group", split_axis=0, concat_axis=0, tiled=True)
        placed = place(target, arrived, group_blocks)
        received = lax.all_to_all(placed, "local", split_axis=0, concat_axis=0, tiled=True)
        incoming.append(received.reshape(members, blocks, ROWS, -1))

    contract = (((0,), (0,)), ((), ()))
    self_term = lax.dot_general(
        features, pre_grad, contract, precision=high, preferred_element_type=F32
    )
    neigh_term = lax.dot_general(
        aggregated, pre_grad, contract, precision=high, preferred_element_type=F32
    )
    first = core == 0
    mine = jnp.where(first, self_term, neigh_term) + lax.ppermute(
        jnp.where(first, neigh_term, self_term), "local", swap
    )
    shares = lax.all_to_all(
        mine.reshape(groups, -1, width), "group", split_axis=0, concat_axis=0, tiled=True
    )
    total = jnp.sum(shares, axis=0)
    total = total + lax.ppermute(total, "local", pairs)
    total = total + lax.ppermute(total, "local", across)
    scale = float(node_rows * groups * members) ** (-0.5)
    whole = lax.all_gather(total * scale, "group", tiled=True)
    other = lax.ppermute(whole, "local", swap)
    self_grad = jnp.where(first, whole, other)
    neigh_grad = jnp.where(first, other, whole)

    base = jnp.dot(pre_grad, w_self.T, precision=high, preferred_element_type=F32)
    base = base + jnp.concatenate(local_parts, axis=1)
    node_grad = finish(base, incoming)
    return (node_grad, self_grad, neigh_grad)


def solution(mesh):
    in_specs = (
        P(("group", "local"), None),
        P(("group", "local"), None),
        P(("group", "local"), None),
        P(("group", "local"), None),
        P(),
        P(),
        P(("group", "local"), None, None),
        P(("group", "local")),
        P(),
        P(),
    )
    out_specs = (P(("group", "local"), None), P(), P())
    return jax.shard_map(
        on_device, mesh=mesh, in_specs=in_specs, out_specs=out_specs, check_vma=False
    )
```

```python
import functools

import jax
import jax.numpy as jnp
from jax import lax
from jax.experimental import pallas as pl
from jax.experimental.pallas import tpu as pltpu
from jax.sharding import PartitionSpec as P

F32 = jnp.float32
BF16 = jnp.bfloat16
BLOCK = 128
CHUNKS = 2
MAIN = 26
QUARTER = (0, 1, 3, 2)
LIMIT = 24


def split(x):
    high = x.astype(BF16)
    low = (x - high.astype(F32)).astype(BF16)
    return high, low


def whereabouts():
    member = lax.axis_index("local")
    chip = member // 2
    side = chip // 2
    return member % 2, side, (chip + side) % 2


def slot_places(count_ref, places):
    slots = places.shape[0]
    owners = count_ref.shape[1]
    capacity = slots // owners
    group = lax.axis_index("group")

    def owner(o, carry):
        live, dead = carry
        count = count_ref[group, o]
        for j in range(capacity):
            is_live = j < count
            places[o * capacity + j] = jnp.where(is_live, live, slots - 1 - dead)
            live = live + is_live.astype(jnp.int32)
            dead = dead + 1 - is_live.astype(jnp.int32)
        return live, dead

    zero = jnp.int32(0)
    lax.fori_loop(0, owners, owner, (zero, zero))


def tile_kernel(own, blocks, main, over, col_ref, count_ref, *rest):
    if own:
        pre_hbm, weight_hbm, tiles_hbm, recv_ref, local_ref, over_ref, *rest = rest
        keep_a, send_a, keep_b, send_b, pre, weight, tiles, sums, places, column, sems = rest
    else:
        pre_hbm, grad_hbm, weight_hbm, tiles_hbm, pre_ref, local_ref, over_ref, *rest = rest
        send_ref, pre, grad, weight, tiles, sums, places, column, sems = rest
    width = weight.shape[0]
    rows = pre.shape[0] // CHUNKS
    count = tiles.shape[0] // CHUNKS
    core, p, q = whereabouts()
    half = core if own else 1 - core
    some = pl.ds(pl.multiple_of(half * width, width), width)
    weight_copy = pltpu.make_async_copy(weight_hbm.at[some], weight, sems.at[0])
    weight_copy.start()
    if own:
        main_sums = sums.at[pl.ds(blocks, main)]
        recv_copy = pltpu.make_async_copy(recv_ref, main_sums, sems.at[1])
        recv_copy.start()
    chunks = []
    for i in range(CHUNKS):
        at = pl.ds(i * rows, rows)
        copies = [pltpu.make_async_copy(pre_hbm.at[at], pre.at[at], sems.at[2 + 3 * i])]
        if not own:
            copies.append(pltpu.make_async_copy(grad_hbm.at[at], grad.at[at], sems.at[3 + 3 * i]))
        some_tiles = pl.ds(i * count, count)
        copies.append(
            pltpu.make_async_copy(tiles_hbm.at[some_tiles], tiles.at[some_tiles], sems.at[4 + 3 * i])
        )
        for copy in copies:
            copy.start()
        chunks.append(copies)
    sums[0:blocks] = jnp.zeros((blocks,) + sums.shape[1:], F32)
    sums[blocks + main :] = jnp.zeros((over,) + sums.shape[1:], F32)
    if not own:
        sums[blocks : blocks + main] = jnp.zeros((main,) + sums.shape[1:], F32)
    slot_places(count_ref, places)

    def place_tile(t, _):
        col = col_ref[t]
        slot = jnp.maximum(col - blocks, 0)
        column[t] = jnp.where(col < blocks, col, blocks + places[slot])
        return 0

    lax.fori_loop(0, tiles.shape[0], place_tile, 0)
    weight_copy.wait()
    weight_high, weight_low = split(weight[...])
    contract = (((1,), (1,)), ((), ()))
    for i in range(CHUNKS):
        at = pl.ds(i * rows, rows)
        *copies, tiles_copy = chunks[i]
        for copy in copies:
            copy.wait()
        if own:
            pre_grad = pre[at]
        else:
            pre_grad = jnp.where(pre[at] > 0, grad[at], 0.0)
            grad[at] = pre_grad
        pre_high, pre_low = split(pre_grad)
        part = lax.dot_general(weight_high, pre_high, contract, preferred_element_type=F32)
        part += lax.dot_general(weight_high, pre_low, contract, preferred_element_type=F32)
        part += lax.dot_general(weight_low, pre_high, contract, preferred_element_type=F32)
        row_high, row_low = split(part)
        tiles_copy.wait()
        if own and i == 0:
            recv_copy.wait()
        for r in range(rows // BLOCK):
            mine = slice(r * BLOCK, (r + 1) * BLOCK)
            high = row_high[:, mine]
            left = jnp.concatenate([high, high, row_low[:, mine]], axis=1)
            each = count * BLOCK // rows
            for k in range(0, each, 2):
                t = i * count + r * each + k
                first_high, first_low = split(tiles[t])
                next_high, next_low = split(tiles[t + 1])
                high = jnp.concatenate([first_high, next_high], axis=1)
                low = jnp.concatenate([first_low, next_low], axis=1)
                right = jnp.concatenate([high, low, high], axis=0)
                product = jnp.dot(left, right, preferred_element_type=F32)
                sums[column[t]] += product[:, :BLOCK]
                sums[column[t + 1]] += product[:, BLOCK:]

    copies = []

    def out(source, target):
        copy = pltpu.make_async_copy(source, target, sems.at[2 + len(copies)])
        copy.start()
        copies.append(copy)

    if own:
        some = main // 2
        share = width // 4

        def piece(first, p_at, q_at, target):
            share_rows = pl.ds(pl.multiple_of((p_at * 2 + q_at) * share, share), share)
            out(sums.at[pl.ds(blocks + first, some), share_rows], target)

        for k in range(2):
            piece(0, k, 1 - q, send_a.at[k])
            piece(some, 1 - p, k, send_b.at[k])
        for k in range(2):
            piece(0, k, q, keep_a.at[k])
            piece(some, p, k, keep_b.at[k])
    else:
        out(sums.at[pl.ds(blocks, main)], send_ref)
        out(grad, pre_ref)
    out(sums.at[pl.ds(0, blocks)], local_ref)
    out(sums.at[pl.ds(blocks + main, over)], over_ref)
    for copy in copies:
        copy.wait()


def tile_sums(
    tile_col, halo_count, weight, tile_vals, main, over, preact=None, grad_out=None,
    pre_grad=None, recv=None,
):
    own = recv is not None
    node_rows, feat = (pre_grad if own else preact).shape
    width = weight.shape[0] // 2
    blocks = node_rows // BLOCK
    some = main // 2
    anywhere = pl.BlockSpec(memory_space=pl.ANY)
    local = jax.ShapeDtypeStruct((blocks, width, BLOCK), F32)
    over_shape = jax.ShapeDtypeStruct((over, width, BLOCK), F32)
    piece = jax.ShapeDtypeStruct((2, some, width // 4, BLOCK), F32)
    if own:
        args = [pre_grad, weight, tile_vals, recv]
        out_shape = [local, over_shape] + [piece] * 4
    else:
        args = [preact, grad_out, weight, tile_vals]
        out_shape = [
            jax.ShapeDtypeStruct((node_rows, feat), F32),
            local,
            over_shape,
            jax.ShapeDtypeStruct((main, width, BLOCK), F32),
        ]
    scratch = [pltpu.VMEM((node_rows, feat), F32)]
    if not own:
        scratch.append(pltpu.VMEM((node_rows, feat), F32))
    scratch += [
        pltpu.VMEM((width, feat), F32),
        pltpu.VMEM(tile_vals.shape, F32),
        pltpu.VMEM((blocks + main + over, width, BLOCK), F32),
        pltpu.SMEM((main + over,), jnp.int32),
        pltpu.SMEM((tile_vals.shape[0],), jnp.int32),
        pltpu.SemaphoreType.DMA((12,)),
    ]
    return pl.pallas_call(
        functools.partial(tile_kernel, own, blocks, main, over),
        out_shape=out_shape,
        in_specs=[pl.BlockSpec(memory_space=pltpu.SMEM)] * 2 + [anywhere] * len(args),
        out_specs=[anywhere] * len(out_shape),
        scratch_shapes=scratch,
        compiler_params=pltpu.CompilerParams(vmem_limit_bytes=LIMIT * 1024 * 1024),
        cost_estimate=pl.CostEstimate(
            flops=6 * (tile_vals.size + node_rows * feat) * width,
            bytes_accessed=14 * 1024 * 1024,
            transcendentals=0,
        ),
        name="own_tile_sums" if own else "other_tile_sums",
    )(tile_col, halo_count, *args)


IN_VMEM = pl.BlockSpec(memory_space=pltpu.VMEM)
IN_SMEM = pl.BlockSpec(memory_space=pltpu.SMEM)


def second_kernel(keep_a, recv_a, keep_b, recv_b, keep, send_a, send_b):
    _, p, q = whereabouts()
    send_a[...] = keep_a[1 - p] + recv_a[1 - p]
    send_b[...] = keep_b[1 - q] + recv_b[1 - q]
    keep[0] = keep_a[p] + recv_a[p]
    keep[1] = keep_b[q] + recv_b[q]


def second_sums(keep_a, recv_a, keep_b, recv_b):
    send = jax.ShapeDtypeStruct(keep_a.shape[1:], F32)
    return pl.pallas_call(
        second_kernel,
        out_shape=[jax.ShapeDtypeStruct(keep_a.shape, F32), send, send],
        in_specs=[IN_VMEM] * 4,
        out_specs=[IN_VMEM] * 3,
        cost_estimate=pl.CostEstimate(
            flops=2 * keep_a.size, bytes_accessed=24 * keep_a.size, transcendentals=0
        ),
        name="second_sums",
    )(keep_a, recv_a, keep_b, recv_b)


def third_kernel(count_ref, keep, recv_a, recv_b, over, out, total, places):
    half = recv_a.shape[0]
    main = 2 * half
    total[0:half] = keep[0] + recv_a[...]
    total[half:main] = keep[1] + recv_b[...]
    total[main:] = over[...]
    slot_places(count_ref, places)

    @pl.loop(0, out.shape[0])
    def _(slot):
        out[slot] = total[places[slot]]


def third_sums(halo_count, keep, recv_a, recv_b, over):
    slots = 2 * recv_a.shape[0] + over.shape[0]
    shape = (slots,) + recv_a.shape[1:]
    return pl.pallas_call(
        third_kernel,
        out_shape=jax.ShapeDtypeStruct(shape, F32),
        in_specs=[IN_SMEM] + [IN_VMEM] * 4,
        out_specs=IN_VMEM,
        scratch_shapes=[pltpu.VMEM(shape, F32), pltpu.SMEM((slots,), jnp.int32)],
        cost_estimate=pl.CostEstimate(
            flops=keep.size, bytes_accessed=16 * keep.size, transcendentals=0
        ),
        name="third_sums",
    )(halo_count, keep, recv_a, recv_b, over)


def place_kernel(count_ref, target_ref, arrived, out):
    group = lax.axis_index("group")
    sources = count_ref.shape[0]
    capacity = arrived.shape[0] // sources
    out[...] = jnp.zeros_like(out)

    @pl.loop(0, sources)
    def _(source):
        for j in range(capacity):

            @pl.when(j < count_ref[source, group])
            def _():
                out[target_ref[source, group * capacity + j]] += arrived[source * capacity + j]


def place(halo_count, halo_target, arrived, group_blocks):
    return pl.pallas_call(
        place_kernel,
        out_shape=jax.ShapeDtypeStruct((group_blocks,) + arrived.shape[1:], F32),
        in_specs=[IN_SMEM] * 2 + [IN_VMEM],
        out_specs=IN_VMEM,
        cost_estimate=pl.CostEstimate(
            flops=arrived.size, bytes_accessed=12 * arrived.size, transcendentals=0
        ),
        name="place",
    )(halo_count, halo_target, arrived)


def finish_kernel(base, other_local, own_local, received, out, total):
    core, _, _ = whereabouts()
    width = other_local.shape[1]
    share = received.shape[2]
    total[pl.ds(pl.multiple_of(core * width, width), width)] = own_local[0]
    total[pl.ds(pl.multiple_of((1 - core) * width, width), width)] = other_local[0]
    for member in range(received.shape[0]):
        start = (member % 2) * width + QUARTER[member // 2] * share
        total[start : start + share] += received[member, 0]
    out[...] = base[...] + total[...].T


def finish(base, other_local, own_local, received):
    node_rows, feat = base.shape
    blocks, width, _ = other_local.shape
    row_spec = pl.BlockSpec((BLOCK, feat), lambda i: (i, 0))
    local_spec = pl.BlockSpec((1, width, BLOCK), lambda i: (i, 0, 0))
    shape = (received.shape[0], 1) + received.shape[2:]
    return pl.pallas_call(
        finish_kernel,
        out_shape=jax.ShapeDtypeStruct(base.shape, F32),
        grid=(blocks,),
        in_specs=[row_spec, local_spec, local_spec, pl.BlockSpec(shape, lambda i: (0, i, 0, 0))],
        out_specs=row_spec,
        scratch_shapes=[pltpu.VMEM((feat, BLOCK), F32)],
        cost_estimate=pl.CostEstimate(
            flops=2 * base.size, bytes_accessed=16 * base.size, transcendentals=0
        ),
        name="finish",
    )(base, other_local, own_local, received)


def on_device(
    features,
    aggregated,
    preact,
    grad_out,
    w_self,
    w_neigh,
    tile_vals,
    tile_col,
    halo_count,
    halo_target,
):
    high = lax.Precision.HIGH
    node_rows, width = features.shape
    blocks = node_rows // BLOCK
    groups = lax.axis_size("group")
    members = lax.axis_size("local")
    slot_count = halo_target.shape[1]
    over = slot_count - MAIN
    member = lax.axis_index("local")
    swap = [(i, i ^ 1) for i in range(members)]
    pairs = [(i, i ^ 2) for i in range(members)]
    across = [(i, members - 2 - (i - i % 2) + i % 2) for i in range(members)]

    pre_grad, other_local, other_over, send = tile_sums(
        tile_col, halo_count, w_neigh, tile_vals, MAIN, over, preact=preact, grad_out=grad_out
    )
    recv = lax.ppermute(send, "local", swap)
    own_local, own_over, keep_a, send_a, keep_b, send_b = tile_sums(
        tile_col, halo_count, w_neigh, tile_vals, MAIN, over, pre_grad=pre_grad, recv=recv
    )
    recv_a = lax.ppermute(send_a, "local", pairs)
    recv_b = lax.ppermute(send_b, "local", across)
    keep, send_a, send_b = second_sums(keep_a, recv_a, keep_b, recv_b)
    recv_a = lax.ppermute(send_a, "local", across)
    recv_b = lax.ppermute(send_b, "local", pairs)

    def more():
        sums = own_over + lax.ppermute(other_over, "local", swap)
        shares = sums.reshape(over, 4, -1, BLOCK)
        quarters = jnp.array(QUARTER, dtype=jnp.int32)
        chip = member // 2
        total = lax.dynamic_index_in_dim(shares, quarters[chip], 1, keepdims=False)
        for away in range(1, 4):
            theirs = lax.dynamic_index_in_dim(
                shares, quarters[(chip + away) % 4], 1, keepdims=False
            )
            steps = [(i, (i + 2 * away) % members) for i in range(members)]
            total = total + lax.ppermute(theirs, "local", steps)
        return total

    def none():
        return jnp.zeros((over,) + recv_a.shape[1:], F32)

    most = jnp.max(jnp.sum(halo_count, axis=1))
    over_share = lax.cond(most > MAIN, more, none)
    shares = third_sums(halo_count, keep, recv_a, recv_b, over_share)
    arrived = lax.all_to_all(shares, "group", split_axis=0, concat_axis=0, tiled=True)
    placed = place(halo_count, halo_target, arrived, blocks * members)
    received = lax.all_to_all(placed, "local", split_axis=0, concat_axis=0, tiled=True)
    received = received.reshape((members, blocks) + received.shape[1:])

    contract = (((0,), (0,)), ((), ()))
    self_term = lax.dot_general(
        features, pre_grad, contract, precision=high, preferred_element_type=F32
    )
    neigh_term = lax.dot_general(
        aggregated, pre_grad, contract, precision=high, preferred_element_type=F32
    )
    first = member % 2 == 0
    mine = jnp.where(first, self_term, neigh_term) + lax.ppermute(
        jnp.where(first, neigh_term, self_term), "local", swap
    )
    parts = lax.all_to_all(
        mine.reshape(groups, -1, width), "group", split_axis=0, concat_axis=0, tiled=True
    )
    total = jnp.sum(parts, axis=0)
    total = total + lax.ppermute(total, "local", pairs)
    total = total + lax.ppermute(total, "local", across)
    scale = float(node_rows * groups * members) ** (-0.5)
    whole = lax.all_gather(total * scale, "group", tiled=True)
    other = lax.ppermute(whole, "local", swap)
    self_grad = jnp.where(first, whole, other)
    neigh_grad = jnp.where(first, other, whole)

    base = jnp.dot(pre_grad, w_self.T, precision=high, preferred_element_type=F32)
    node_grad = finish(base, other_local, own_local, received)
    return (node_grad, self_grad, neigh_grad)


def solution(mesh):
    in_specs = (
        P(("group", "local"), None),
        P(("group", "local"), None),
        P(("group", "local"), None),
        P(("group", "local"), None),
        P(),
        P(),
        P(("group", "local"), None, None),
        P(("group", "local")),
        P(),
        P(),
    )
    out_specs = (P(("group", "local"), None), P(), P())
    return jax.shard_map(
        on_device, mesh=mesh, in_specs=in_specs, out_specs=out_specs, check_vma=False
    )
```

```python
import functools

import jax
import jax.numpy as jnp
from jax import lax
from jax.experimental import pallas as pl
from jax.experimental.pallas import tpu as pltpu
from jax.sharding import PartitionSpec as P

F32 = jnp.float32
BF16 = jnp.bfloat16
BLOCK = 128
CHUNKS = 2
MAIN = 26
QUARTER = (0, 1, 3, 2)
LIMIT_OTHER = 55
LIMIT_OWN = 20
LIMIT_SMALL = 6


def split(x):
    high = x.astype(BF16)
    low = (x - high.astype(F32)).astype(BF16)
    return high, low


def limit(mebibytes):
    return pltpu.CompilerParams(vmem_limit_bytes=mebibytes * 1024 * 1024)


def whereabouts():
    member = lax.axis_index("local")
    chip = member // 2
    side = chip // 2
    return member % 2, side, (chip + side) % 2


def slot_places(count_ref, places):
    slots = places.shape[0]
    owners = count_ref.shape[1]
    capacity = slots // owners
    group = lax.axis_index("group")

    def owner(o, carry):
        live, dead = carry
        count = count_ref[group, o]
        for j in range(capacity):
            is_live = j < count
            places[o * capacity + j] = jnp.where(is_live, live, slots - 1 - dead)
            live = live + is_live.astype(jnp.int32)
            dead = dead + 1 - is_live.astype(jnp.int32)
        return live, dead

    zero = jnp.int32(0)
    lax.fori_loop(0, owners, owner, (zero, zero))


def tile_kernel(own, blocks, main, over, col_ref, count_ref, *rest):
    if own:
        pre_hbm, weight_hbm, tiles_hbm, recv_ref, local_ref, over_ref, flag_ref, *rest = rest
        keep_a, send_a, keep_b, send_b, pre, weight, tiles, sums, places, column, sems = rest
    else:
        pre_hbm, grad_hbm, weight_hbm, tiles_hbm, pre_ref, local_ref, over_ref, *rest = rest
        send_ref, pre, grad, weight, tiles, sums, places, column, sems = rest
    width = weight.shape[0]
    rows = pre.shape[0] // CHUNKS
    count = tiles.shape[0] // CHUNKS
    core, p, q = whereabouts()
    half = core if own else 1 - core
    some = pl.ds(pl.multiple_of(half * width, width), width)
    weight_copy = pltpu.make_async_copy(weight_hbm.at[some], weight, sems.at[0])
    weight_copy.start()
    if own:
        flag_ref[0] = core
        main_sums = sums.at[pl.ds(blocks, main)]
        recv_copy = pltpu.make_async_copy(recv_ref, main_sums, sems.at[1])
        recv_copy.start()
    chunks = []
    for i in range(CHUNKS):
        at = pl.ds(i * rows, rows)
        copies = [pltpu.make_async_copy(pre_hbm.at[at], pre.at[at], sems.at[2 + 3 * i])]
        if not own:
            copies.append(pltpu.make_async_copy(grad_hbm.at[at], grad.at[at], sems.at[3 + 3 * i]))
        some_tiles = pl.ds(i * count, count)
        copies.append(
            pltpu.make_async_copy(tiles_hbm.at[some_tiles], tiles.at[some_tiles], sems.at[4 + 3 * i])
        )
        for copy in copies:
            copy.start()
        chunks.append(copies)
    sums[0:blocks] = jnp.zeros((blocks,) + sums.shape[1:], F32)
    sums[blocks + main :] = jnp.zeros((over,) + sums.shape[1:], F32)
    if not own:
        sums[blocks : blocks + main] = jnp.zeros((main,) + sums.shape[1:], F32)
    slot_places(count_ref, places)

    def place_tile(t, _):
        col = col_ref[t]
        slot = jnp.maximum(col - blocks, 0)
        column[t] = jnp.where(col < blocks, col, blocks + places[slot])
        return 0

    lax.fori_loop(0, tiles.shape[0], place_tile, 0)
    weight_copy.wait()
    weight_high, weight_low = split(weight[...])
    contract = (((1,), (1,)), ((), ()))
    pre_copies = []
    for i in range(CHUNKS):
        at = pl.ds(i * rows, rows)
        *copies, tiles_copy = chunks[i]
        for copy in copies:
            copy.wait()
        if own:
            pre_grad = pre[at]
        else:
            pre_grad = jnp.where(pre[at] > 0, grad[at], 0.0)
            grad[at] = pre_grad
            pre_copy = pltpu.make_async_copy(grad.at[at], pre_ref.at[at], sems.at[2 + 3 * i])
            pre_copy.start()
            pre_copies.append(pre_copy)
        pre_high, pre_low = split(pre_grad)
        part = lax.dot_general(weight_high, pre_high, contract, preferred_element_type=F32)
        part += lax.dot_general(weight_high, pre_low, contract, preferred_element_type=F32)
        part += lax.dot_general(weight_low, pre_high, contract, preferred_element_type=F32)
        row_high, row_low = split(part)
        tiles_copy.wait()
        if own and i == 0:
            recv_copy.wait()
        for r in range(rows // BLOCK):
            mine = slice(r * BLOCK, (r + 1) * BLOCK)
            high = row_high[:, mine]
            left = jnp.concatenate([high, high, row_low[:, mine]], axis=1)
            each = count * BLOCK // rows
            for k in range(0, each, 2):
                t = i * count + r * each + k
                first_high, first_low = split(tiles[t])
                next_high, next_low = split(tiles[t + 1])
                high = jnp.concatenate([first_high, next_high], axis=1)
                low = jnp.concatenate([first_low, next_low], axis=1)
                right = jnp.concatenate([high, low, high], axis=0)
                product = jnp.dot(left, right, preferred_element_type=F32)
                sums[column[t]] += product[:, :BLOCK]
                sums[column[t + 1]] += product[:, BLOCK:]

    copies = []

    def out(source, target):
        copy = pltpu.make_async_copy(source, target, sems.at[2 + 3 * CHUNKS + len(copies)])
        copy.start()
        copies.append(copy)

    if own:
        some = main // 2
        share = width // 4

        def piece(first, p_at, q_at, target):
            share_rows = pl.ds(pl.multiple_of((p_at * 2 + q_at) * share, share), share)
            out(sums.at[pl.ds(blocks + first, some), share_rows], target)

        for k in range(2):
            piece(0, k, 1 - q, send_a.at[k])
            piece(some, 1 - p, k, send_b.at[k])
        for k in range(2):
            piece(0, k, q, keep_a.at[k])
            piece(some, p, k, keep_b.at[k])
    else:
        out(sums.at[pl.ds(blocks, main)], send_ref)
    out(sums.at[pl.ds(0, blocks)], local_ref)
    out(sums.at[pl.ds(blocks + main, over)], over_ref)
    for copy in pre_copies + copies:
        copy.wait()


def tile_sums(
    tile_col, halo_count, weight, tile_vals, main, over, preact=None, grad_out=None,
    pre_grad=None, recv=None,
):
    own = recv is not None
    node_rows, feat = (pre_grad if own else preact).shape
    width = weight.shape[0] // 2
    blocks = node_rows // BLOCK
    some = main // 2
    anywhere = pl.BlockSpec(memory_space=pl.ANY)
    local = jax.ShapeDtypeStruct((blocks, width, BLOCK), F32)
    over_shape = jax.ShapeDtypeStruct((over, width, BLOCK), F32)
    piece = jax.ShapeDtypeStruct((2, some, width // 4, BLOCK), F32)
    if own:
        args = [pre_grad, weight, tile_vals, recv]
        flag = jax.ShapeDtypeStruct((1,), jnp.int32)
        out_shape = [local, over_shape, flag] + [piece] * 4
    else:
        args = [preact, grad_out, weight, tile_vals]
        out_shape = [
            jax.ShapeDtypeStruct((node_rows, feat), F32),
            local,
            over_shape,
            jax.ShapeDtypeStruct((main, width, BLOCK), F32),
        ]
    scratch = [pltpu.VMEM((node_rows, feat), F32)]
    if not own:
        scratch.append(pltpu.VMEM((node_rows, feat), F32))
    scratch += [
        pltpu.VMEM((width, feat), F32),
        pltpu.VMEM(tile_vals.shape, F32),
        pltpu.VMEM((blocks + main + over, width, BLOCK), F32),
        pltpu.SMEM((main + over,), jnp.int32),
        pltpu.SMEM((tile_vals.shape[0],), jnp.int32),
        pltpu.SemaphoreType.DMA((2 + 3 * CHUNKS + 10,)),
    ]
    return pl.pallas_call(
        functools.partial(tile_kernel, own, blocks, main, over),
        out_shape=out_shape,
        in_specs=[pl.BlockSpec(memory_space=pltpu.SMEM)] * 2 + [anywhere] * len(args),
        out_specs=[
            pl.BlockSpec(memory_space=pltpu.SMEM) if x.dtype == jnp.int32 else anywhere
            for x in out_shape
        ],
        scratch_shapes=scratch,
        compiler_params=limit(LIMIT_OWN if own else LIMIT_OTHER),
        cost_estimate=pl.CostEstimate(
            flops=6 * (tile_vals.size + node_rows * feat) * width,
            bytes_accessed=14 * 1024 * 1024,
            transcendentals=0,
        ),
        name="own_tile_sums" if own else "other_tile_sums",
    )(tile_col, halo_count, *args)


IN_VMEM = pl.BlockSpec(memory_space=pltpu.VMEM)
IN_SMEM = pl.BlockSpec(memory_space=pltpu.SMEM)


def second_kernel(keep_a, recv_a, keep_b, recv_b, keep, send_a, send_b):
    _, p, q = whereabouts()
    send_a[...] = keep_a[1 - p] + recv_a[1 - p]
    send_b[...] = keep_b[1 - q] + recv_b[1 - q]
    keep[0] = keep_a[p] + recv_a[p]
    keep[1] = keep_b[q] + recv_b[q]


def second_sums(keep_a, recv_a, keep_b, recv_b):
    send = jax.ShapeDtypeStruct(keep_a.shape[1:], F32)
    return pl.pallas_call(
        second_kernel,
        out_shape=[jax.ShapeDtypeStruct(keep_a.shape, F32), send, send],
        in_specs=[IN_VMEM] * 4,
        out_specs=[IN_VMEM] * 3,
        cost_estimate=pl.CostEstimate(
            flops=2 * keep_a.size, bytes_accessed=24 * keep_a.size, transcendentals=0
        ),
        compiler_params=limit(LIMIT_SMALL),
        name="second_sums",
    )(keep_a, recv_a, keep_b, recv_b)


def third_kernel(count_ref, keep, recv_a, recv_b, over, out, total, places):
    half = recv_a.shape[0]
    main = 2 * half
    total[0:half] = keep[0] + recv_a[...]
    total[half:main] = keep[1] + recv_b[...]
    total[main:] = over[...]
    slot_places(count_ref, places)

    @pl.loop(0, out.shape[0])
    def _(slot):
        out[slot] = total[places[slot]]


def third_sums(halo_count, keep, recv_a, recv_b, over):
    slots = 2 * recv_a.shape[0] + over.shape[0]
    shape = (slots,) + recv_a.shape[1:]
    return pl.pallas_call(
        third_kernel,
        out_shape=jax.ShapeDtypeStruct(shape, F32),
        in_specs=[IN_SMEM] + [IN_VMEM] * 4,
        out_specs=IN_VMEM,
        scratch_shapes=[pltpu.VMEM(shape, F32), pltpu.SMEM((slots,), jnp.int32)],
        cost_estimate=pl.CostEstimate(
            flops=keep.size, bytes_accessed=16 * keep.size, transcendentals=0
        ),
        compiler_params=limit(LIMIT_SMALL),
        name="third_sums",
    )(halo_count, keep, recv_a, recv_b, over)


def part_kernel(parts, after, out):
    del after
    total = parts[0]
    for k in range(1, parts.shape[0]):
        total += parts[k]
    out[...] = total


def part_sum(parts, after):
    return pl.pallas_call(
        part_kernel,
        out_shape=jax.ShapeDtypeStruct(parts.shape[1:], F32),
        in_specs=[IN_VMEM, pl.BlockSpec(memory_space=pl.ANY)],
        out_specs=IN_VMEM,
        cost_estimate=pl.CostEstimate(
            flops=parts.size, bytes_accessed=4 * parts.size, transcendentals=0
        ),
        compiler_params=limit(LIMIT_SMALL),
        name="part_sum",
    )(parts, after)


def place_kernel(count_ref, target_ref, arrived, out):
    group = lax.axis_index("group")
    sources = count_ref.shape[0]
    capacity = arrived.shape[0] // sources
    out[...] = jnp.zeros_like(out)

    @pl.loop(0, sources)
    def _(source):
        for j in range(capacity):

            @pl.when(j < count_ref[source, group])
            def _():
                out[target_ref[source, group * capacity + j]] += arrived[source * capacity + j]


def place(halo_count, halo_target, arrived, group_blocks):
    return pl.pallas_call(
        place_kernel,
        out_shape=jax.ShapeDtypeStruct((group_blocks,) + arrived.shape[1:], F32),
        in_specs=[IN_SMEM] * 2 + [IN_VMEM],
        out_specs=IN_VMEM,
        cost_estimate=pl.CostEstimate(
            flops=arrived.size, bytes_accessed=12 * arrived.size, transcendentals=0
        ),
        compiler_params=limit(LIMIT_SMALL),
        name="place",
    )(halo_count, halo_target, arrived)


def finish_kernel(base, other_local, own_local, received, out, total):
    core, _, _ = whereabouts()
    width = other_local.shape[1]
    share = received.shape[2]
    total[pl.ds(pl.multiple_of(core * width, width), width)] = own_local[0]
    total[pl.ds(pl.multiple_of((1 - core) * width, width), width)] = other_local[0]
    for member in range(received.shape[0]):
        start = (member % 2) * width + QUARTER[member // 2] * share
        total[start : start + share] += received[member, 0]
    out[...] = base[...] + total[...].T


def finish(base, other_local, own_local, received):
    node_rows, feat = base.shape
    blocks, width, _ = other_local.shape
    row_spec = pl.BlockSpec((BLOCK, feat), lambda i: (i, 0))
    local_spec = pl.BlockSpec((1, width, BLOCK), lambda i: (i, 0, 0))
    shape = (received.shape[0], 1) + received.shape[2:]
    return pl.pallas_call(
        finish_kernel,
        out_shape=jax.ShapeDtypeStruct(base.shape, F32),
        grid=(blocks,),
        in_specs=[row_spec, local_spec, local_spec, pl.BlockSpec(shape, lambda i: (0, i, 0, 0))],
        out_specs=row_spec,
        scratch_shapes=[pltpu.VMEM((feat, BLOCK), F32)],
        cost_estimate=pl.CostEstimate(
            flops=2 * base.size, bytes_accessed=16 * base.size, transcendentals=0
        ),
        compiler_params=limit(LIMIT_SMALL),
        name="finish",
    )(base, other_local, own_local, received)


def on_device(
    features,
    aggregated,
    preact,
    grad_out,
    w_self,
    w_neigh,
    tile_vals,
    tile_col,
    halo_count,
    halo_target,
):
    high = lax.Precision.HIGH
    node_rows, width = features.shape
    blocks = node_rows // BLOCK
    groups = lax.axis_size("group")
    members = lax.axis_size("local")
    slot_count = halo_target.shape[1]
    over = slot_count - MAIN
    member = lax.axis_index("local")
    swap = [(i, i ^ 1) for i in range(members)]
    pairs = [(i, i ^ 2) for i in range(members)]
    across = [(i, members - 2 - (i - i % 2) + i % 2) for i in range(members)]

    pre_grad, other_local, other_over, send = tile_sums(
        tile_col, halo_count, w_neigh, tile_vals, MAIN, over, preact=preact, grad_out=grad_out
    )
    recv = lax.ppermute(send, "local", swap)
    own_local, own_over, flag, keep_a, send_a, keep_b, send_b = tile_sums(
        tile_col, halo_count, w_neigh, tile_vals, MAIN, over, pre_grad=pre_grad, recv=recv
    )
    recv_a = lax.ppermute(send_a, "local", pairs)
    recv_b = lax.ppermute(send_b, "local", across)
    keep, send_a, send_b = second_sums(keep_a, recv_a, keep_b, recv_b)
    recv_a = lax.ppermute(send_a, "local", across)
    recv_b = lax.ppermute(send_b, "local", pairs)

    def more():
        sums = own_over + lax.ppermute(other_over, "local", swap)
        shares = sums.reshape(over, 4, -1, BLOCK)
        quarters = jnp.array(QUARTER, dtype=jnp.int32)
        chip = member // 2
        total = lax.dynamic_index_in_dim(shares, quarters[chip], 1, keepdims=False)
        for away in range(1, 4):
            theirs = lax.dynamic_index_in_dim(
                shares, quarters[(chip + away) % 4], 1, keepdims=False
            )
            steps = [(i, (i + 2 * away) % members) for i in range(members)]
            total = total + lax.ppermute(theirs, "local", steps)
        return total

    def none():
        return jnp.zeros((over,) + recv_a.shape[1:], F32)

    most = jnp.max(jnp.sum(halo_count, axis=1))
    over_share = lax.cond(most > MAIN, more, none)
    shares = third_sums(halo_count, keep, recv_a, recv_b, over_share)
    arrived = lax.all_to_all(shares, "group", split_axis=0, concat_axis=0, tiled=True)
    placed = place(halo_count, halo_target, arrived, blocks * members)
    received = lax.all_to_all(placed, "local", split_axis=0, concat_axis=0, tiled=True)
    received = received.reshape((members, blocks) + received.shape[1:])

    contract = (((0,), (0,)), ((), ()))
    self_term = lax.dot_general(
        features, pre_grad, contract, precision=high, preferred_element_type=F32
    )
    neigh_term = lax.dot_general(
        aggregated, pre_grad, contract, precision=high, preferred_element_type=F32
    )
    first = flag[0] == 0
    mine = jnp.where(first, self_term, neigh_term) + lax.ppermute(
        jnp.where(first, neigh_term, self_term), "local", swap
    )
    parts = lax.all_to_all(
        mine.reshape(groups, -1, width), "group", split_axis=0, concat_axis=0, tiled=True
    )
    total = part_sum(parts, send_a)
    total = total + lax.ppermute(total, "local", pairs)
    total = total + lax.ppermute(total, "local", across)
    scale = float(node_rows * groups * members) ** (-0.5)
    whole = lax.all_gather(total * scale, "group", tiled=True)
    other = lax.ppermute(whole, "local", swap)
    self_grad = jnp.where(first, whole, other)
    neigh_grad = jnp.where(first, other, whole)

    base = jnp.dot(pre_grad, w_self.T, precision=high, preferred_element_type=F32)
    node_grad = finish(base, other_local, own_local, received)
    return (node_grad, self_grad, neigh_grad)


def solution(mesh):
    in_specs = (
        P(("group", "local"), None),
        P(("group", "local"), None),
        P(("group", "local"), None),
        P(("group", "local"), None),
        P(),
        P(),
        P(("group", "local"), None, None),
        P(("group", "local")),
        P(),
        P(),
    )
    out_specs = (P(("group", "local"), None), P(), P())
    return jax.shard_map(
        on_device, mesh=mesh, in_specs=in_specs, out_specs=out_specs, check_vma=False
    )
```

```python
import functools

import jax
import jax.numpy as jnp
from jax import lax
from jax.experimental import pallas as pl
from jax.experimental.pallas import tpu as pltpu
from jax.sharding import PartitionSpec as P

F32 = jnp.float32
BF16 = jnp.bfloat16
BLOCK = 128
CHUNKS = 2
MAIN = 26
QUARTER = (0, 1, 3, 2)
LIMIT_OTHER = 55
LIMIT_OWN = 20
LIMIT_SMALL = 6
PARTS = 2


def split(x):
    high = x.astype(BF16)
    low = (x - high.astype(F32)).astype(BF16)
    return high, low


def limit(mebibytes):
    return pltpu.CompilerParams(vmem_limit_bytes=mebibytes * 1024 * 1024)


def whereabouts():
    member = lax.axis_index("local")
    chip = member // 2
    side = chip // 2
    return member % 2, side, (chip + side) % 2


def slot_places(count_ref, places):
    slots = places.shape[0]
    owners = count_ref.shape[1]
    capacity = slots // owners
    group = lax.axis_index("group")

    def owner(o, carry):
        live, dead = carry
        count = count_ref[group, o]
        for j in range(capacity):
            is_live = j < count
            places[o * capacity + j] = jnp.where(is_live, live, slots - 1 - dead)
            live = live + is_live.astype(jnp.int32)
            dead = dead + 1 - is_live.astype(jnp.int32)
        return live, dead

    zero = jnp.int32(0)
    lax.fori_loop(0, owners, owner, (zero, zero))


def tile_kernel(own, blocks, main, over, col_ref, count_ref, *rest):
    if own:
        pre_hbm, weight_hbm, tiles_hbm, recv_ref, local_ref, over_ref, flag_ref, *rest = rest
        keep_a, send_a, keep_b, send_b, pre, weight, tiles, sums, places, column, sems = rest
    else:
        pre_hbm, grad_hbm, weight_hbm, tiles_hbm, pre_ref, local_ref, over_ref, *rest = rest
        send_ref, pre, grad, weight, tiles, sums, places, column, sems = rest
    width = weight.shape[0]
    rows = pre.shape[0] // CHUNKS
    count = tiles.shape[0] // CHUNKS
    core, p, q = whereabouts()
    half = core if own else 1 - core
    some = pl.ds(pl.multiple_of(half * width, width), width)
    weight_copy = pltpu.make_async_copy(weight_hbm.at[some], weight, sems.at[0])
    weight_copy.start()
    if own:
        flag_ref[0] = core
        main_sums = sums.at[pl.ds(blocks, main)]
        recv_copy = pltpu.make_async_copy(recv_ref, main_sums, sems.at[1])
        recv_copy.start()
    chunks = []
    for i in range(CHUNKS):
        at = pl.ds(i * rows, rows)
        copies = [pltpu.make_async_copy(pre_hbm.at[at], pre.at[at], sems.at[2 + 3 * i])]
        if not own:
            copies.append(pltpu.make_async_copy(grad_hbm.at[at], grad.at[at], sems.at[3 + 3 * i]))
        some_tiles = pl.ds(i * count, count)
        copies.append(
            pltpu.make_async_copy(tiles_hbm.at[some_tiles], tiles.at[some_tiles], sems.at[4 + 3 * i])
        )
        for copy in copies:
            copy.start()
        chunks.append(copies)
    sums[0:blocks] = jnp.zeros((blocks,) + sums.shape[1:], F32)
    sums[blocks + main :] = jnp.zeros((over,) + sums.shape[1:], F32)
    if not own:
        sums[blocks : blocks + main] = jnp.zeros((main,) + sums.shape[1:], F32)
    slot_places(count_ref, places)

    def place_tile(t, _):
        col = col_ref[t]
        slot = jnp.maximum(col - blocks, 0)
        column[t] = jnp.where(col < blocks, col, blocks + places[slot])
        return 0

    lax.fori_loop(0, tiles.shape[0], place_tile, 0)
    weight_copy.wait()
    weight_high, weight_low = split(weight[...])
    contract = (((1,), (1,)), ((), ()))
    pre_copies = []
    for i in range(CHUNKS):
        at = pl.ds(i * rows, rows)
        *copies, tiles_copy = chunks[i]
        for copy in copies:
            copy.wait()
        if own:
            pre_grad = pre[at]
        else:
            pre_grad = jnp.where(pre[at] > 0, grad[at], 0.0)
            grad[at] = pre_grad
            pre_copy = pltpu.make_async_copy(grad.at[at], pre_ref.at[at], sems.at[2 + 3 * i])
            pre_copy.start()
            pre_copies.append(pre_copy)
        pre_high, pre_low = split(pre_grad)
        part = lax.dot_general(weight_high, pre_high, contract, preferred_element_type=F32)
        part += lax.dot_general(weight_high, pre_low, contract, preferred_element_type=F32)
        part += lax.dot_general(weight_low, pre_high, contract, preferred_element_type=F32)
        row_high, row_low = split(part)
        tiles_copy.wait()
        if own and i == 0:
            recv_copy.wait()
        for r in range(rows // BLOCK):
            mine = slice(r * BLOCK, (r + 1) * BLOCK)
            high = row_high[:, mine]
            left = jnp.concatenate([high, high, row_low[:, mine]], axis=1)
            each = count * BLOCK // rows
            for k in range(0, each, 2):
                t = i * count + r * each + k
                first_high, first_low = split(tiles[t])
                next_high, next_low = split(tiles[t + 1])
                high = jnp.concatenate([first_high, next_high], axis=1)
                low = jnp.concatenate([first_low, next_low], axis=1)
                right = jnp.concatenate([high, low, high], axis=0)
                product = jnp.dot(left, right, preferred_element_type=F32)
                sums[column[t]] += product[:, :BLOCK]
                sums[column[t + 1]] += product[:, BLOCK:]

    copies = []

    def out(source, target):
        copy = pltpu.make_async_copy(source, target, sems.at[2 + 3 * CHUNKS + len(copies)])
        copy.start()
        copies.append(copy)

    if own:
        some = main // 2
        share = width // 4

        def piece(first, p_at, q_at, target):
            share_rows = pl.ds(pl.multiple_of((p_at * 2 + q_at) * share, share), share)
            out(sums.at[pl.ds(blocks + first, some), share_rows], target)

        for k in range(2):
            piece(0, k, 1 - q, send_a.at[k])
            piece(some, 1 - p, k, send_b.at[k])
        for k in range(2):
            piece(0, k, q, keep_a.at[k])
            piece(some, p, k, keep_b.at[k])
    else:
        out(sums.at[pl.ds(blocks, main)], send_ref)
    out(sums.at[pl.ds(0, blocks)], local_ref)
    out(sums.at[pl.ds(blocks + main, over)], over_ref)
    for copy in pre_copies + copies:
        copy.wait()


def tile_sums(
    tile_col, halo_count, weight, tile_vals, main, over, preact=None, grad_out=None,
    pre_grad=None, recv=None,
):
    own = recv is not None
    node_rows, feat = (pre_grad if own else preact).shape
    width = weight.shape[0] // 2
    blocks = node_rows // BLOCK
    some = main // 2
    anywhere = pl.BlockSpec(memory_space=pl.ANY)
    local = jax.ShapeDtypeStruct((blocks, width, BLOCK), F32)
    over_shape = jax.ShapeDtypeStruct((over, width, BLOCK), F32)
    piece = jax.ShapeDtypeStruct((2, some, width // 4, BLOCK), F32)
    if own:
        args = [pre_grad, weight, tile_vals, recv]
        flag = jax.ShapeDtypeStruct((1,), jnp.int32)
        out_shape = [local, over_shape, flag] + [piece] * 4
    else:
        args = [preact, grad_out, weight, tile_vals]
        out_shape = [
            jax.ShapeDtypeStruct((node_rows, feat), F32),
            local,
            over_shape,
            jax.ShapeDtypeStruct((main, width, BLOCK), F32),
        ]
    scratch = [pltpu.VMEM((node_rows, feat), F32)]
    if not own:
        scratch.append(pltpu.VMEM((node_rows, feat), F32))
    scratch += [
        pltpu.VMEM((width, feat), F32),
        pltpu.VMEM(tile_vals.shape, F32),
        pltpu.VMEM((blocks + main + over, width, BLOCK), F32),
        pltpu.SMEM((main + over,), jnp.int32),
        pltpu.SMEM((tile_vals.shape[0],), jnp.int32),
        pltpu.SemaphoreType.DMA((2 + 3 * CHUNKS + 10,)),
    ]
    return pl.pallas_call(
        functools.partial(tile_kernel, own, blocks, main, over),
        out_shape=out_shape,
        in_specs=[pl.BlockSpec(memory_space=pltpu.SMEM)] * 2 + [anywhere] * len(args),
        out_specs=[
            pl.BlockSpec(memory_space=pltpu.SMEM) if x.dtype == jnp.int32 else anywhere
            for x in out_shape
        ],
        scratch_shapes=scratch,
        compiler_params=limit(LIMIT_OWN if own else LIMIT_OTHER),
        cost_estimate=pl.CostEstimate(
            flops=6 * (tile_vals.size + node_rows * feat) * width,
            bytes_accessed=14 * 1024 * 1024,
            transcendentals=0,
        ),
        name="own_tile_sums" if own else "other_tile_sums",
    )(tile_col, halo_count, *args)


IN_VMEM = pl.BlockSpec(memory_space=pltpu.VMEM)
IN_SMEM = pl.BlockSpec(memory_space=pltpu.SMEM)


def second_kernel(keep_a, recv_a, keep_b, recv_b, parts, keep, send_a, send_b, share):
    _, p, q = whereabouts()
    half = keep_a.shape[1]
    total = parts[0]
    for k in range(1, parts.shape[0]):
        total += parts[k]
    rows = total.shape[1]
    for k in range(total.shape[0]):
        at = (k * rows // share.shape[1], pl.ds(k * rows % share.shape[1], rows))
        share[at] = total[k]
    send_a[0:half] = keep_a[1 - p] + recv_a[1 - p]
    send_b[0:half] = keep_b[1 - q] + recv_b[1 - q]
    send_a[half:] = share[...]
    send_b[half:] = share[...]
    keep[0] = keep_a[p] + recv_a[p]
    keep[1] = keep_b[q] + recv_b[q]


def second_sums(keep_a, recv_a, keep_b, recv_b, parts):
    _, half, share, _ = keep_a.shape
    extra = parts[0].size // (share * BLOCK)
    send = jax.ShapeDtypeStruct((half + extra, share, BLOCK), F32)
    return pl.pallas_call(
        second_kernel,
        out_shape=[
            jax.ShapeDtypeStruct(keep_a.shape, F32),
            send,
            send,
            jax.ShapeDtypeStruct((extra, share, BLOCK), F32),
        ],
        in_specs=[IN_VMEM] * 5,
        out_specs=[IN_VMEM] * 4,
        cost_estimate=pl.CostEstimate(
            flops=2 * keep_a.size, bytes_accessed=24 * keep_a.size, transcendentals=0
        ),
        compiler_params=limit(LIMIT_SMALL),
        name="second_sums",
    )(keep_a, recv_a, keep_b, recv_b, parts)


def third_kernel(scale, count_ref, keep, recv_a, recv_b, over, share, recv_share, *rest):
    *outs, weight, total, places = rest
    half = keep.shape[1]
    main = 2 * half
    total[0:half] = keep[0] + recv_a[0:half]
    total[half:main] = keep[1] + recv_b[0:half]
    total[main:] = over[...]
    weight[...] = ((share[...] + recv_b[half:]) + (recv_a[half:] + recv_share[...])) * scale
    slot_places(count_ref, places)
    rows = outs[0].shape[1]

    @pl.loop(0, total.shape[0])
    def _(slot):
        for h, out in enumerate(outs):
            out[slot] = total[places[slot], h * rows : (h + 1) * rows]


def third_sums(halo_count, keep, recv_a, recv_b, over, share, recv_share, scale):
    _, half, rows, _ = keep.shape
    slots = 2 * half + over.shape[0]
    return pl.pallas_call(
        functools.partial(third_kernel, scale),
        out_shape=[jax.ShapeDtypeStruct((slots, rows // PARTS, BLOCK), F32)] * PARTS
        + [jax.ShapeDtypeStruct(share.shape, F32)],
        in_specs=[IN_SMEM] + [IN_VMEM] * 6,
        out_specs=[IN_VMEM] * (PARTS + 1),
        scratch_shapes=[pltpu.VMEM((slots, rows, BLOCK), F32), pltpu.SMEM((slots,), jnp.int32)],
        cost_estimate=pl.CostEstimate(
            flops=keep.size, bytes_accessed=16 * keep.size, transcendentals=0
        ),
        compiler_params=limit(LIMIT_SMALL),
        name="third_sums",
    )(halo_count, keep, recv_a, recv_b, over, share, recv_share)


def small(kernel, out_shape, args, name, specs=None, out_specs=None):
    size = max(x.size for x in args)
    return pl.pallas_call(
        kernel,
        out_shape=out_shape,
        in_specs=specs or [IN_VMEM] * len(args),
        out_specs=out_specs or jax.tree.map(lambda _: IN_VMEM, out_shape),
        cost_estimate=pl.CostEstimate(flops=size, bytes_accessed=12 * size, transcendentals=0),
        compiler_params=limit(LIMIT_SMALL),
        name=name,
    )(*args)


def sort_kernel(self_term, neigh_term, keep, send):
    core, _, _ = whereabouts()
    pieces, columns, rows, _ = keep.shape

    def copy(source, target):
        for g in range(pieces):
            for c in range(columns):
                some = (slice(g * rows, (g + 1) * rows), slice(c * BLOCK, (c + 1) * BLOCK))
                target[g, c] = source[some]

    @pl.when(core == 0)
    def _():
        copy(self_term, keep)
        copy(neigh_term, send)

    @pl.when(core != 0)
    def _():
        copy(neigh_term, keep)
        copy(self_term, send)


def grads_kernel(whole, other, self_grad, neigh_grad):
    core, _, _ = whereabouts()
    pieces, columns, rows, _ = whole.shape

    def copy(source, target):
        for g in range(pieces):
            for c in range(columns):
                some = (slice(g * rows, (g + 1) * rows), slice(c * BLOCK, (c + 1) * BLOCK))
                target[some] = source[g, c]

    @pl.when(core == 0)
    def _():
        copy(whole, self_grad)
        copy(other, neigh_grad)

    @pl.when(core != 0)
    def _():
        copy(other, self_grad)
        copy(whole, neigh_grad)


def add_kernel(one, two, after, out):
    del after
    out[...] = one[...] + two[...]


def place_kernel(count_ref, target_ref, arrived, out):
    group = lax.axis_index("group")
    sources = count_ref.shape[0]
    capacity = arrived.shape[0] // sources
    out[...] = jnp.zeros_like(out)

    @pl.loop(0, sources)
    def _(source):
        for j in range(capacity):

            @pl.when(j < count_ref[source, group])
            def _():
                out[target_ref[source, group * capacity + j]] += arrived[source * capacity + j]


def place(halo_count, halo_target, arrived, group_blocks):
    return pl.pallas_call(
        place_kernel,
        out_shape=jax.ShapeDtypeStruct((group_blocks,) + arrived.shape[1:], F32),
        in_specs=[IN_SMEM] * 2 + [IN_VMEM],
        out_specs=IN_VMEM,
        cost_estimate=pl.CostEstimate(
            flops=arrived.size, bytes_accessed=12 * arrived.size, transcendentals=0
        ),
        compiler_params=limit(LIMIT_SMALL),
        name="place",
    )(halo_count, halo_target, arrived)


def finish_kernel(base, other_local, own_local, *rest):
    *received, out, total, rows, sems = rest
    core, _, _ = whereabouts()
    blocks, width, _ = other_local.shape
    members, _, part, _ = received[0].shape
    share = part * len(received)
    own = pl.ds(pl.multiple_of(core * width, width), width)
    other = pl.ds(pl.multiple_of((1 - core) * width, width), width)
    copies = []
    for b in range(blocks):
        total[b, own] = own_local[b]
        total[b, other] = other_local[b]
        for member in range(members):
            start = (member % 2) * width + QUARTER[member // 2] * share
            for h, some in enumerate(received):
                total[b, start + h * part : start + (h + 1) * part] += some[member, b]
        at = slice(b * BLOCK, (b + 1) * BLOCK)
        rows[at] = base[at] + total[b].T
        copy = pltpu.make_async_copy(rows.at[at], out.at[at], sems.at[b])
        copy.start()
        copies.append(copy)
    for copy in copies:
        copy.wait()


def finish(base, other_local, own_local, received):
    node_rows, feat = base.shape
    blocks = other_local.shape[0]
    return pl.pallas_call(
        finish_kernel,
        out_shape=jax.ShapeDtypeStruct(base.shape, F32),
        in_specs=[IN_VMEM] * (3 + len(received)),
        out_specs=pl.BlockSpec(memory_space=pl.ANY),
        scratch_shapes=[
            pltpu.VMEM((blocks, feat, BLOCK), F32),
            pltpu.VMEM((node_rows, feat), F32),
            pltpu.SemaphoreType.DMA((blocks,)),
        ],
        cost_estimate=pl.CostEstimate(
            flops=2 * base.size, bytes_accessed=16 * base.size, transcendentals=0
        ),
        compiler_params=limit(8),
        name="finish",
    )(base, other_local, own_local, *received)


def on_device(
    features,
    aggregated,
    preact,
    grad_out,
    w_self,
    w_neigh,
    tile_vals,
    tile_col,
    halo_count,
    halo_target,
):
    high = lax.Precision.HIGH
    node_rows, width = features.shape
    blocks = node_rows // BLOCK
    groups = lax.axis_size("group")
    members = lax.axis_size("local")
    slot_count = halo_target.shape[1]
    over = slot_count - MAIN
    member = lax.axis_index("local")
    swap = [(i, i ^ 1) for i in range(members)]
    pairs = [(i, i ^ 2) for i in range(members)]
    across = [(i, members - 2 - (i - i % 2) + i % 2) for i in range(members)]

    pre_grad, other_local, other_over, send = tile_sums(
        tile_col, halo_count, w_neigh, tile_vals, MAIN, over, preact=preact, grad_out=grad_out
    )
    recv = lax.ppermute(send, "local", swap)
    own_local, own_over, flag, keep_a, send_a, keep_b, send_b = tile_sums(
        tile_col, halo_count, w_neigh, tile_vals, MAIN, over, pre_grad=pre_grad, recv=recv
    )
    recv_a = lax.ppermute(send_a, "local", pairs)
    recv_b = lax.ppermute(send_b, "local", across)

    contract = (((0,), (0,)), ((), ()))
    self_term = lax.dot_general(
        features, pre_grad, contract, precision=high, preferred_element_type=F32
    )
    neigh_term = lax.dot_general(
        aggregated, pre_grad, contract, precision=high, preferred_element_type=F32
    )
    pieces = jax.ShapeDtypeStruct(
        (groups, width // BLOCK, width // groups, BLOCK), F32
    )
    stay, leave = small(sort_kernel, [pieces] * 2, [self_term, neigh_term], "sort_terms")
    mine = small(
        add_kernel,
        pieces,
        [stay, lax.ppermute(leave, "local", swap), flag],
        "add_terms",
        [IN_VMEM, IN_VMEM, IN_SMEM],
    )
    parts = lax.all_to_all(mine, "group", split_axis=0, concat_axis=0, tiled=True)

    keep, send_a, send_b, share = second_sums(keep_a, recv_a, keep_b, recv_b, parts)
    recv_a = lax.ppermute(send_a, "local", across)
    recv_b = lax.ppermute(send_b, "local", pairs)
    recv_share = lax.ppermute(share, "local", [(i, i ^ 4) for i in range(members)])

    def more():
        sums = own_over + lax.ppermute(other_over, "local", swap)
        shares = sums.reshape(over, 4, -1, BLOCK)
        quarters = jnp.array(QUARTER, dtype=jnp.int32)
        chip = member // 2
        total = lax.dynamic_index_in_dim(shares, quarters[chip], 1, keepdims=False)
        for away in range(1, 4):
            theirs = lax.dynamic_index_in_dim(
                shares, quarters[(chip + away) % 4], 1, keepdims=False
            )
            steps = [(i, (i + 2 * away) % members) for i in range(members)]
            total = total + lax.ppermute(theirs, "local", steps)
        return total

    def none():
        return jnp.zeros((over,) + share.shape[1:], F32)

    most = jnp.max(jnp.sum(halo_count, axis=1))
    over_share = lax.cond(most > MAIN, more, none)
    scale = float(node_rows * groups * members) ** (-0.5)
    *shares, weight_share = third_sums(
        halo_count, keep, recv_a, recv_b, over_share, share, recv_share, scale
    )
    arrived = [
        lax.all_to_all(some, "group", split_axis=0, concat_axis=0, tiled=True) for some in shares
    ]
    received = []
    for some in arrived:
        placed = place(halo_count, halo_target, some, blocks * members)
        some = lax.all_to_all(placed, "local", split_axis=0, concat_axis=0, tiled=True)
        received.append(some.reshape((members, blocks) + some.shape[1:]))
    whole = lax.all_gather(weight_share, "group", tiled=True).reshape(pieces.shape)
    other = lax.ppermute(whole, "local", swap)
    square = jax.ShapeDtypeStruct(self_term.shape, F32)
    self_grad, neigh_grad = small(grads_kernel, [square] * 2, [whole, other], "sort_grads")

    base = jnp.dot(pre_grad, w_self.T, precision=high, preferred_element_type=F32)
    node_grad = finish(base, other_local, own_local, received)
    return (node_grad, self_grad, neigh_grad)


def solution(mesh):
    in_specs = (
        P(("group", "local"), None),
        P(("group", "local"), None),
        P(("group", "local"), None),
        P(("group", "local"), None),
        P(),
        P(),
        P(("group", "local"), None, None),
        P(("group", "local")),
        P(),
        P(),
    )
    out_specs = (P(("group", "local"), None), P(), P())
    return jax.shard_map(
        on_device, mesh=mesh, in_specs=in_specs, out_specs=out_specs, check_vma=False
    )
```

```python
import functools

import jax
import jax.numpy as jnp
from jax import lax
from jax.experimental import pallas as pl
from jax.experimental.pallas import tpu as pltpu
from jax.sharding import PartitionSpec as P

F32 = jnp.float32
BF16 = jnp.bfloat16
BLOCK = 128
CHUNKS = 2
MAIN = 30
LIMIT_OTHER = 55
LIMIT_OWN = 20
LIMIT_SMALL = 6


def split(x):
    high = x.astype(BF16)
    low = (x - high.astype(F32)).astype(BF16)
    return high, low


def limit(mebibytes):
    return pltpu.CompilerParams(vmem_limit_bytes=mebibytes * 1024 * 1024)


def whereabouts():
    member = lax.axis_index("local")
    chip = member // 2
    side = chip // 2
    return member % 2, side, (chip + side) % 2


def slot_places(count_ref, places):
    slots = places.shape[0]
    owners = count_ref.shape[1]
    capacity = slots // owners
    group = lax.axis_index("group")

    def owner(o, carry):
        live, dead = carry
        count = count_ref[group, o]
        for j in range(capacity):
            is_live = j < count
            places[o * capacity + j] = jnp.where(is_live, live, slots - 1 - dead)
            live = live + is_live.astype(jnp.int32)
            dead = dead + 1 - is_live.astype(jnp.int32)
        return live, dead

    zero = jnp.int32(0)
    lax.fori_loop(0, owners, owner, (zero, zero))


def tile_kernel(own, blocks, main, over, col_ref, count_ref, *rest):
    if own:
        pre_hbm, weight_hbm, tiles_hbm, recv_ref, local_ref, flag_ref, *rest = rest
        keep_a, send_a, keep_b, send_b, pre, weight, tiles, sums, places, column, sems = rest
    else:
        pre_hbm, grad_hbm, weight_hbm, tiles_hbm, pre_ref, local_ref, *rest = rest
        send_ref, pre, grad, weight, tiles, sums, places, column, sems = rest
    width = weight.shape[0]
    rows = pre.shape[0] // CHUNKS
    count = tiles.shape[0] // CHUNKS
    core, p, q = whereabouts()
    half = core if own else 1 - core
    some = pl.ds(pl.multiple_of(half * width, width), width)
    weight_copy = pltpu.make_async_copy(weight_hbm.at[some], weight, sems.at[0])
    weight_copy.start()
    if own:
        flag_ref[0] = core
        main_sums = sums.at[pl.ds(blocks, main)]
        recv_copy = pltpu.make_async_copy(recv_ref, main_sums, sems.at[1])
        recv_copy.start()
    chunks = []
    for i in range(CHUNKS):
        at = pl.ds(i * rows, rows)
        copies = [pltpu.make_async_copy(pre_hbm.at[at], pre.at[at], sems.at[2 + 3 * i])]
        if not own:
            copies.append(pltpu.make_async_copy(grad_hbm.at[at], grad.at[at], sems.at[3 + 3 * i]))
        some_tiles = pl.ds(i * count, count)
        copies.append(
            pltpu.make_async_copy(tiles_hbm.at[some_tiles], tiles.at[some_tiles], sems.at[4 + 3 * i])
        )
        for copy in copies:
            copy.start()
        chunks.append(copies)
    sums[0:blocks] = jnp.zeros((blocks,) + sums.shape[1:], F32)
    sums[blocks + main :] = jnp.zeros((over,) + sums.shape[1:], F32)
    if not own:
        sums[blocks : blocks + main] = jnp.zeros((main,) + sums.shape[1:], F32)
    slot_places(count_ref, places)

    def place_tile(t, _):
        col = col_ref[t]
        slot = jnp.maximum(col - blocks, 0)
        column[t] = jnp.where(col < blocks, col, blocks + places[slot])
        return 0

    lax.fori_loop(0, tiles.shape[0], place_tile, 0)
    weight_copy.wait()
    weight_high, weight_low = split(weight[...])
    contract = (((1,), (1,)), ((), ()))
    pre_copies = []
    for i in range(CHUNKS):
        at = pl.ds(i * rows, rows)
        *copies, tiles_copy = chunks[i]
        for copy in copies:
            copy.wait()
        if own:
            pre_grad = pre[at]
        else:
            pre_grad = jnp.where(pre[at] > 0, grad[at], 0.0)
            grad[at] = pre_grad
            pre_copy = pltpu.make_async_copy(grad.at[at], pre_ref.at[at], sems.at[2 + 3 * i])
            pre_copy.start()
            pre_copies.append(pre_copy)
        pre_high, pre_low = split(pre_grad)
        part = lax.dot_general(weight_high, pre_high, contract, preferred_element_type=F32)
        part += lax.dot_general(weight_high, pre_low, contract, preferred_element_type=F32)
        part += lax.dot_general(weight_low, pre_high, contract, preferred_element_type=F32)
        row_high, row_low = split(part)
        tiles_copy.wait()
        if own and i == 0:
            recv_copy.wait()
        for r in range(rows // BLOCK):
            mine = slice(r * BLOCK, (r + 1) * BLOCK)
            high = row_high[:, mine]
            left = jnp.concatenate([high, high, row_low[:, mine]], axis=1)
            each = count * BLOCK // rows
            for k in range(0, each, 2):
                t = i * count + r * each + k
                first_high, first_low = split(tiles[t])
                next_high, next_low = split(tiles[t + 1])
                high = jnp.concatenate([first_high, next_high], axis=1)
                low = jnp.concatenate([first_low, next_low], axis=1)
                right = jnp.concatenate([high, low, high], axis=0)
                product = jnp.dot(left, right, preferred_element_type=F32)
                sums[column[t]] += product[:, :BLOCK]
                sums[column[t + 1]] += product[:, BLOCK:]

    copies = []

    def out(source, target):
        copy = pltpu.make_async_copy(source, target, sems.at[2 + 3 * CHUNKS + len(copies)])
        copy.start()
        copies.append(copy)

    if own:
        some = main // 2
        share = width // 4

        def piece(first, p_at, q_at, target):
            share_rows = pl.ds(pl.multiple_of((p_at * 2 + q_at) * share, share), share)
            out(sums.at[pl.ds(blocks + first, some), share_rows], target)

        for k in range(2):
            piece(0, k, 1 - q, send_a.at[k])
            piece(some, 1 - p, k, send_b.at[k])
        for k in range(2):
            piece(0, k, q, keep_a.at[k])
            piece(some, p, k, keep_b.at[k])
    else:
        out(sums.at[pl.ds(blocks, main)], send_ref)
    out(sums.at[pl.ds(0, blocks)], local_ref)
    for copy in pre_copies + copies:
        copy.wait()


def tile_sums(
    tile_col, halo_count, weight, tile_vals, main, over, preact=None, grad_out=None,
    pre_grad=None, recv=None,
):
    own = recv is not None
    node_rows, feat = (pre_grad if own else preact).shape
    width = weight.shape[0] // 2
    blocks = node_rows // BLOCK
    some = main // 2
    anywhere = pl.BlockSpec(memory_space=pl.ANY)
    local = jax.ShapeDtypeStruct((blocks, width, BLOCK), F32)
    piece = jax.ShapeDtypeStruct((2, some, width // 4, BLOCK), F32)
    if own:
        args = [pre_grad, weight, tile_vals, recv]
        flag = jax.ShapeDtypeStruct((1,), jnp.int32)
        out_shape = [local, flag] + [piece] * 4
    else:
        args = [preact, grad_out, weight, tile_vals]
        out_shape = [
            jax.ShapeDtypeStruct((node_rows, feat), F32),
            local,
            jax.ShapeDtypeStruct((main, width, BLOCK), F32),
        ]
    scratch = [pltpu.VMEM((node_rows, feat), F32)]
    if not own:
        scratch.append(pltpu.VMEM((node_rows, feat), F32))
    scratch += [
        pltpu.VMEM((width, feat), F32),
        pltpu.VMEM(tile_vals.shape, F32),
        pltpu.VMEM((blocks + main + over, width, BLOCK), F32),
        pltpu.SMEM((main + over,), jnp.int32),
        pltpu.SMEM((tile_vals.shape[0],), jnp.int32),
        pltpu.SemaphoreType.DMA((2 + 3 * CHUNKS + 10,)),
    ]
    return pl.pallas_call(
        functools.partial(tile_kernel, own, blocks, main, over),
        out_shape=out_shape,
        in_specs=[pl.BlockSpec(memory_space=pltpu.SMEM)] * 2 + [anywhere] * len(args),
        out_specs=[
            pl.BlockSpec(memory_space=pltpu.SMEM) if x.dtype == jnp.int32 else anywhere
            for x in out_shape
        ],
        scratch_shapes=scratch,
        compiler_params=limit(LIMIT_OWN if own else LIMIT_OTHER),
        cost_estimate=pl.CostEstimate(
            flops=6 * (tile_vals.size + node_rows * feat) * width,
            bytes_accessed=14 * 1024 * 1024,
            transcendentals=0,
        ),
        name="own_tile_sums" if own else "other_tile_sums",
    )(tile_col, halo_count, *args)


IN_VMEM = pl.BlockSpec(memory_space=pltpu.VMEM)
IN_SMEM = pl.BlockSpec(memory_space=pltpu.SMEM)


def second_kernel(keep_a, recv_a, keep_b, recv_b, *rest):
    *parts, keep, send_a, send_b, share = rest
    _, p, q = whereabouts()
    half = keep_a.shape[1]
    rows = parts[0].shape[1]
    for k in range(parts[0].shape[0]):
        at = (k * rows // share.shape[1], pl.ds(k * rows % share.shape[1], rows))
        total = parts[0][k]
        for part in parts[1:]:
            total += part[k]
        share[at] = total
    send_a[0:half] = keep_a[1 - p] + recv_a[1 - p]
    send_b[0:half] = keep_b[1 - q] + recv_b[1 - q]
    send_a[half:] = share[...]
    send_b[half:] = share[...]
    keep[0] = keep_a[p] + recv_a[p]
    keep[1] = keep_b[q] + recv_b[q]


def second_sums(keep_a, recv_a, keep_b, recv_b, parts):
    _, half, share, _ = keep_a.shape
    extra = parts[0].size // (share * BLOCK)
    send = jax.ShapeDtypeStruct((half + extra, share, BLOCK), F32)
    weight_share = jax.ShapeDtypeStruct((extra, share, BLOCK), F32)
    out_shape = [jax.ShapeDtypeStruct(keep_a.shape, F32), send, send, weight_share]
    return small(second_kernel, out_shape, [keep_a, recv_a, keep_b, recv_b, *parts], "second_sums")


def third_kernel(scale, count_ref, keep, recv_a, recv_b, share, recv_share, out, weight, places):
    half = keep.shape[1]
    weight[...] = ((share[...] + recv_b[half:]) + (recv_a[half:] + recv_share[...])) * scale
    slot_places(count_ref, places)

    @pl.loop(0, out.shape[0])
    def _(slot):
        place = places[slot]

        @pl.when(place < half)
        def _():
            out[slot] = keep[0, place] + recv_a[place]

        @pl.when((place >= half) & (place < 2 * half))
        def _():
            out[slot] = keep[1, place - half] + recv_b[place - half]

        @pl.when(place >= 2 * half)
        def _():
            out[slot] = jnp.zeros_like(out[slot])


def third_sums(halo_count, keep, recv_a, recv_b, share, recv_share, slots, scale):
    return small(
        functools.partial(third_kernel, scale),
        [
            jax.ShapeDtypeStruct((slots,) + keep.shape[2:], F32),
            jax.ShapeDtypeStruct(share.shape, F32),
        ],
        [halo_count, keep, recv_a, recv_b, share, recv_share],
        "third_sums",
        [IN_SMEM] + [IN_VMEM] * 5,
        scratch=[pltpu.SMEM((slots,), jnp.int32)],
    )


def small(kernel, out_shape, args, name, specs=None, scratch=()):
    size = max(x.size for x in args)
    return pl.pallas_call(
        kernel,
        out_shape=out_shape,
        in_specs=specs or [IN_VMEM] * len(args),
        out_specs=jax.tree.map(lambda _: IN_VMEM, out_shape),
        scratch_shapes=scratch,
        cost_estimate=pl.CostEstimate(flops=size, bytes_accessed=12 * size, transcendentals=0),
        compiler_params=limit(LIMIT_SMALL),
        name=name,
    )(*args)


def sort_kernel(self_term, neigh_term, keep, send):
    core, _, _ = whereabouts()
    pieces, columns, rows, _ = keep.shape

    def copy(source, target):
        for g in range(pieces):
            for c in range(columns):
                some = (slice(g * rows, (g + 1) * rows), slice(c * BLOCK, (c + 1) * BLOCK))
                target[g, c] = source[some]

    @pl.when(core == 0)
    def _():
        copy(self_term, keep)
        copy(neigh_term, send)

    @pl.when(core != 0)
    def _():
        copy(neigh_term, keep)
        copy(self_term, send)


def grads_kernel(whole, other, self_grad, neigh_grad):
    core, _, _ = whereabouts()
    pieces, columns, rows, _ = whole.shape

    def copy(source, target):
        for g in range(pieces):
            for c in range(columns):
                some = (slice(g * rows, (g + 1) * rows), slice(c * BLOCK, (c + 1) * BLOCK))
                target[some] = source[g, c]

    @pl.when(core == 0)
    def _():
        copy(whole, self_grad)
        copy(other, neigh_grad)

    @pl.when(core != 0)
    def _():
        copy(other, self_grad)
        copy(whole, neigh_grad)


def scatter_kernel(axis_of, count, *rest):
    terms = rest[:count]
    outs = rest[-4:]
    me = axis_of(lax.axis_index("group"))
    for away, out in enumerate(outs):
        at = lax.rem(me + away, 4)
        total = terms[0][at]
        for term in terms[1:]:
            total += term[at]
        out[...] = total


def scatter(axis_of, terms, name, after=()):
    piece = jax.ShapeDtypeStruct(terms[0].shape[1:], F32)
    return small(
        functools.partial(scatter_kernel, axis_of, len(terms)),
        [piece] * 4,
        [*terms, *after],
        name,
        [IN_VMEM] * len(terms) + [IN_SMEM] * len(after),
    )


def place_kernel(count_ref, target_ref, arrived, send, *keeps):
    core, _, _ = whereabouts()
    chip = lax.axis_index("local") // 2
    group = lax.axis_index("group")
    sources = count_ref.shape[0]
    capacity = arrived.shape[0] // sources
    blocks = send.shape[1]
    for out in (send, *keeps):
        out[...] = jnp.zeros_like(out)

    @pl.loop(0, sources)
    def _(source):
        for j in range(capacity):
            target = target_ref[source, group * capacity + j]
            live = j < count_ref[source, group]
            member = target // blocks
            block = target - member * blocks
            away = (member // 2 - chip + 4) % 4
            mine = member % 2 == core

            @pl.when(live & jnp.logical_not(mine))
            def _():
                send[away, block] += arrived[source * capacity + j]

            for k, keep in enumerate(keeps):

                @pl.when(live & mine & (away == k))
                def _():
                    keep[block] += arrived[source * capacity + j]


def place(halo_count, halo_target, arrived, blocks):
    keep = jax.ShapeDtypeStruct((blocks,) + arrived.shape[1:], F32)
    send = jax.ShapeDtypeStruct((4,) + keep.shape, F32)
    specs = [IN_SMEM, IN_SMEM, IN_VMEM]
    return small(
        place_kernel, [send] + [keep] * 4, [halo_count, halo_target, arrived], "place", specs
    )


def finish_kernel(base, other_local, own_local, *rest):
    *received, out, total, rows, sems = rest
    core, _, _ = whereabouts()
    chip = lax.axis_index("local") // 2
    blocks, width, _ = other_local.shape
    share = received[0].shape[1]
    own = pl.ds(pl.multiple_of(core * width, width), width)
    other = pl.ds(pl.multiple_of((1 - core) * width, width), width)
    copies = []
    for b in range(blocks):
        total[b, own] = own_local[b]
        total[b, other] = other_local[b]
        for k, some in enumerate(received):
            source = lax.rem(chip - k // 2 + 4, 4)
            side = source // 2
            quarter = side * 2 + lax.rem(source + side, 2)
            first = core if k % 2 == 0 else 1 - core
            start = pl.multiple_of(first * width + quarter * share, share)
            total[b, pl.ds(start, share)] += some[b]
        at = slice(b * BLOCK, (b + 1) * BLOCK)
        rows[at] = base[at] + total[b].T
        copy = pltpu.make_async_copy(rows.at[at], out.at[at], sems.at[b])
        copy.start()
        copies.append(copy)
    for copy in copies:
        copy.wait()


def finish(base, other_local, own_local, received):
    node_rows, feat = base.shape
    blocks = other_local.shape[0]
    return pl.pallas_call(
        finish_kernel,
        out_shape=jax.ShapeDtypeStruct(base.shape, F32),
        in_specs=[IN_VMEM] * (3 + len(received)),
        out_specs=pl.BlockSpec(memory_space=pl.ANY),
        scratch_shapes=[
            pltpu.VMEM((blocks, feat, BLOCK), F32),
            pltpu.VMEM((node_rows, feat), F32),
            pltpu.SemaphoreType.DMA((blocks,)),
        ],
        cost_estimate=pl.CostEstimate(
            flops=2 * base.size, bytes_accessed=16 * base.size, transcendentals=0
        ),
        compiler_params=limit(8),
        name="finish",
    )(base, other_local, own_local, *received)


def on_device(
    features,
    aggregated,
    preact,
    grad_out,
    w_self,
    w_neigh,
    tile_vals,
    tile_col,
    halo_count,
    halo_target,
):
    high = lax.Precision.HIGH
    node_rows, width = features.shape
    blocks = node_rows // BLOCK
    groups = lax.axis_size("group")
    members = lax.axis_size("local")
    slot_count = halo_target.shape[1]
    dead = slot_count - MAIN
    swap = [(i, i ^ 1) for i in range(members)]
    pairs = [(i, i ^ 2) for i in range(members)]
    across = [(i, members - 2 - (i - i % 2) + i % 2) for i in range(members)]
    along_x = [[(i, (i + 2 * k) % members) for i in range(members)] for k in range(4)]
    along_y = [[(i, (i + 4 * k) % groups) for i in range(groups)] for k in range(4)]
    along_z = [[(i, i // 4 * 4 + (i + k) % 4) for i in range(groups)] for k in range(4)]

    pre_grad, other_local, send = tile_sums(
        tile_col, halo_count, w_neigh, tile_vals, MAIN, dead, preact=preact, grad_out=grad_out
    )
    recv = lax.ppermute(send, "local", swap)
    own_local, flag, keep_a, send_a, keep_b, send_b = tile_sums(
        tile_col, halo_count, w_neigh, tile_vals, MAIN, dead, pre_grad=pre_grad, recv=recv
    )
    recv_a = lax.ppermute(send_a, "local", pairs)
    recv_b = lax.ppermute(send_b, "local", across)

    contract = (((0,), (0,)), ((), ()))
    self_term = lax.dot_general(
        features, pre_grad, contract, precision=high, preferred_element_type=F32
    )
    neigh_term = lax.dot_general(
        aggregated, pre_grad, contract, precision=high, preferred_element_type=F32
    )
    pieces = jax.ShapeDtypeStruct((groups, width // BLOCK, width // groups, BLOCK), F32)
    stay, leave = small(sort_kernel, [pieces] * 2, [self_term, neigh_term], "sort_terms")
    by_y = (4, groups // 4) + pieces.shape[1:]
    stay, leave = stay.reshape(by_y), lax.ppermute(leave, "local", swap).reshape(by_y)
    mine, *sends = scatter(lambda g: g // 4, [stay, leave], "sum_cores", [flag])
    terms = [mine] + [
        lax.ppermute(some, "group", along_y[k + 1]) for k, some in enumerate(sends)
    ]
    mine, *sends = scatter(lambda g: lax.rem(g, 4), terms, "sum_y")
    terms = [mine] + [
        lax.ppermute(some, "group", along_z[k + 1]) for k, some in enumerate(sends)
    ]

    keep, send_a, send_b, share = second_sums(keep_a, recv_a, keep_b, recv_b, terms)
    recv_a = lax.ppermute(send_a, "local", across)
    recv_b = lax.ppermute(send_b, "local", pairs)
    recv_share = lax.ppermute(share, "local", along_x[2])
    scale = float(node_rows * groups * members) ** (-0.5)
    shares, weight_share = third_sums(
        halo_count, keep, recv_a, recv_b, share, recv_share, slot_count, scale
    )
    arrived = lax.all_to_all(shares, "group", split_axis=0, concat_axis=0, tiled=True)
    send, *keeps = place(halo_count, halo_target, arrived, blocks)
    swapped = lax.ppermute(send, "local", swap)
    received = []
    for k in range(4):
        pair = [keeps[k], swapped[k]]
        if k > 0:
            pair = [lax.ppermute(some, "local", along_x[k]) for some in pair]
        received += pair

    whole = lax.all_gather(weight_share, "group", tiled=True).reshape(pieces.shape)
    other = lax.ppermute(whole, "local", swap)
    square = jax.ShapeDtypeStruct(self_term.shape, F32)
    self_grad, neigh_grad = small(grads_kernel, [square] * 2, [whole, other], "sort_grads")

    base = jnp.dot(pre_grad, w_self.T, precision=high, preferred_element_type=F32)
    node_grad = finish(base, other_local, own_local, received)
    return (node_grad, self_grad, neigh_grad)


def solution(mesh):
    in_specs = (
        P(("group", "local"), None),
        P(("group", "local"), None),
        P(("group", "local"), None),
        P(("group", "local"), None),
        P(),
        P(),
        P(("group", "local"), None, None),
        P(("group", "local")),
        P(),
        P(),
    )
    out_specs = (P(("group", "local"), None), P(), P())
    return jax.shard_map(
        on_device, mesh=mesh, in_specs=in_specs, out_specs=out_specs, check_vma=False
    )
```

```python
import functools

import jax
import jax.numpy as jnp
from jax import lax
from jax.experimental import pallas as pl
from jax.experimental.pallas import tpu as pltpu
from jax.sharding import PartitionSpec as P

F32 = jnp.float32
BF16 = jnp.bfloat16
BLOCK = 128
CHUNKS = 2
MAIN = 30
LIMIT_OTHER = 55
LIMIT_OWN = 20
LIMIT_SMALL = 6


def split(x):
    high = x.astype(BF16)
    low = (x - high.astype(F32)).astype(BF16)
    return high, low


def limit(mebibytes):
    return pltpu.CompilerParams(vmem_limit_bytes=mebibytes * 1024 * 1024)


def whereabouts():
    member = lax.axis_index("local")
    chip = member >> 1
    side = chip >> 1
    return member & 1, side, (chip + side) & 1


def slot_places(count_ref, places):
    slots = places.shape[0]
    owners = count_ref.shape[1]
    capacity = slots // owners
    group = lax.axis_index("group")

    def owner(o, carry):
        live, dead = carry
        count = count_ref[group, o]
        for j in range(capacity):
            is_live = j < count
            places[o * capacity + j] = jnp.where(is_live, live, slots - 1 - dead)
            live = live + is_live.astype(jnp.int32)
            dead = dead + 1 - is_live.astype(jnp.int32)
        return live, dead

    zero = jnp.int32(0)
    lax.fori_loop(0, owners, owner, (zero, zero))


def tile_kernel(own, blocks, main, over, col_ref, count_ref, *rest):
    if own:
        pre_hbm, weight_hbm, tiles_hbm, recv_ref, local_ref, flag_ref, *rest = rest
        keep_a, send_a, keep_b, send_b, pre, weight, tiles, sums, places, column, sems = rest
    else:
        pre_hbm, grad_hbm, weight_hbm, tiles_hbm, pre_ref, local_ref, *rest = rest
        send_ref, pre, grad, weight, tiles, sums, places, column, sems = rest
    width = weight.shape[0]
    rows = pre.shape[0] // CHUNKS
    count = tiles.shape[0] // CHUNKS
    core, p, q = whereabouts()
    half = core if own else 1 - core
    some = pl.ds(pl.multiple_of(half * width, width), width)
    weight_copy = pltpu.make_async_copy(weight_hbm.at[some], weight, sems.at[0])
    weight_copy.start()
    if own:
        flag_ref[0] = core
        main_sums = sums.at[pl.ds(blocks, main)]
        recv_copy = pltpu.make_async_copy(recv_ref, main_sums, sems.at[1])
        recv_copy.start()
    chunks = []
    for i in range(CHUNKS):
        at = pl.ds(i * rows, rows)
        copies = [pltpu.make_async_copy(pre_hbm.at[at], pre.at[at], sems.at[2 + 3 * i])]
        if not own:
            copies.append(pltpu.make_async_copy(grad_hbm.at[at], grad.at[at], sems.at[3 + 3 * i]))
        some_tiles = pl.ds(i * count, count)
        copies.append(
            pltpu.make_async_copy(tiles_hbm.at[some_tiles], tiles.at[some_tiles], sems.at[4 + 3 * i])
        )
        for copy in copies:
            copy.start()
        chunks.append(copies)
    sums[0:blocks] = jnp.zeros((blocks,) + sums.shape[1:], F32)
    sums[blocks + main :] = jnp.zeros((over,) + sums.shape[1:], F32)
    if not own:
        sums[blocks : blocks + main] = jnp.zeros((main,) + sums.shape[1:], F32)
    slot_places(count_ref, places)

    def place_tile(t, _):
        col = col_ref[t]
        slot = jnp.maximum(col - blocks, 0)
        column[t] = jnp.where(col < blocks, col, blocks + places[slot])
        return 0

    lax.fori_loop(0, tiles.shape[0], place_tile, 0)
    weight_copy.wait()
    weight_high, weight_low = split(weight[...])
    contract = (((1,), (1,)), ((), ()))
    pre_copies = []
    for i in range(CHUNKS):
        at = pl.ds(i * rows, rows)
        *copies, tiles_copy = chunks[i]
        for copy in copies:
            copy.wait()
        if own:
            pre_grad = pre[at]
        else:
            pre_grad = jnp.where(pre[at] > 0, grad[at], 0.0)
            grad[at] = pre_grad
            pre_copy = pltpu.make_async_copy(grad.at[at], pre_ref.at[at], sems.at[2 + 3 * i])
            pre_copy.start()
            pre_copies.append(pre_copy)
        pre_high, pre_low = split(pre_grad)
        part = lax.dot_general(weight_high, pre_high, contract, preferred_element_type=F32)
        part += lax.dot_general(weight_high, pre_low, contract, preferred_element_type=F32)
        part += lax.dot_general(weight_low, pre_high, contract, preferred_element_type=F32)
        row_high, row_low = split(part)
        tiles_copy.wait()
        if own and i == 0:
            recv_copy.wait()
        for r in range(rows // BLOCK):
            mine = slice(r * BLOCK, (r + 1) * BLOCK)
            high = row_high[:, mine]
            left = jnp.concatenate([high, high, row_low[:, mine]], axis=1)
            each = count * BLOCK // rows
            for k in range(0, each, 2):
                t = i * count + r * each + k
                first_high, first_low = split(tiles[t])
                next_high, next_low = split(tiles[t + 1])
                high = jnp.concatenate([first_high, next_high], axis=1)
                low = jnp.concatenate([first_low, next_low], axis=1)
                right = jnp.concatenate([high, low, high], axis=0)
                product = jnp.dot(left, right, preferred_element_type=F32)
                sums[column[t]] += product[:, :BLOCK]
                sums[column[t + 1]] += product[:, BLOCK:]

    copies = []

    def out(source, target):
        copy = pltpu.make_async_copy(source, target, sems.at[2 + 3 * CHUNKS + len(copies)])
        copy.start()
        copies.append(copy)

    if own:
        some = main // 2
        share = width // 4

        def piece(first, p_at, q_at, target):
            share_rows = pl.ds(pl.multiple_of((p_at * 2 + q_at) * share, share), share)
            out(sums.at[pl.ds(blocks + first, some), share_rows], target)

        for k in range(2):
            piece(0, k, 1 - q, send_a.at[k])
            piece(some, 1 - p, k, send_b.at[k])
        for k in range(2):
            piece(0, k, q, keep_a.at[k])
            piece(some, p, k, keep_b.at[k])
    else:
        out(sums.at[pl.ds(blocks, main)], send_ref)
    out(sums.at[pl.ds(0, blocks)], local_ref)
    for copy in pre_copies + copies:
        copy.wait()


def tile_sums(
    tile_col, halo_count, weight, tile_vals, main, over, preact=None, grad_out=None,
    pre_grad=None, recv=None,
):
    own = recv is not None
    node_rows, feat = (pre_grad if own else preact).shape
    width = weight.shape[0] // 2
    blocks = node_rows // BLOCK
    some = main // 2
    anywhere = pl.BlockSpec(memory_space=pl.ANY)
    local = jax.ShapeDtypeStruct((blocks, width, BLOCK), F32)
    piece = jax.ShapeDtypeStruct((2, some, width // 4, BLOCK), F32)
    if own:
        args = [pre_grad, weight, tile_vals, recv]
        flag = jax.ShapeDtypeStruct((1,), jnp.int32)
        out_shape = [local, flag] + [piece] * 4
    else:
        args = [preact, grad_out, weight, tile_vals]
        out_shape = [
            jax.ShapeDtypeStruct((node_rows, feat), F32),
            local,
            jax.ShapeDtypeStruct((main, width, BLOCK), F32),
        ]
    scratch = [pltpu.VMEM((node_rows, feat), F32)]
    if not own:
        scratch.append(pltpu.VMEM((node_rows, feat), F32))
    scratch += [
        pltpu.VMEM((width, feat), F32),
        pltpu.VMEM(tile_vals.shape, F32),
        pltpu.VMEM((blocks + main + over, width, BLOCK), F32),
        pltpu.SMEM((main + over,), jnp.int32),
        pltpu.SMEM((tile_vals.shape[0],), jnp.int32),
        pltpu.SemaphoreType.DMA((2 + 3 * CHUNKS + 10,)),
    ]
    return pl.pallas_call(
        functools.partial(tile_kernel, own, blocks, main, over),
        out_shape=out_shape,
        in_specs=[pl.BlockSpec(memory_space=pltpu.SMEM)] * 2 + [anywhere] * len(args),
        out_specs=[
            pl.BlockSpec(memory_space=pltpu.SMEM) if x.dtype == jnp.int32 else anywhere
            for x in out_shape
        ],
        scratch_shapes=scratch,
        compiler_params=limit(LIMIT_OWN if own else LIMIT_OTHER),
        cost_estimate=pl.CostEstimate(
            flops=6 * (tile_vals.size + node_rows * feat) * width,
            bytes_accessed=14 * 1024 * 1024,
            transcendentals=0,
        ),
        name="own_tile_sums" if own else "other_tile_sums",
    )(tile_col, halo_count, *args)


IN_VMEM = pl.BlockSpec(memory_space=pltpu.VMEM)
IN_SMEM = pl.BlockSpec(memory_space=pltpu.SMEM)
ANYWHERE = pl.BlockSpec(memory_space=pl.ANY)


def second_kernel(keep_a, recv_a, keep_b, recv_b, after, keep, send_a, send_b):
    del after
    _, p, q = whereabouts()
    send_a[...] = keep_a[1 - p] + recv_a[1 - p]
    send_b[...] = keep_b[1 - q] + recv_b[1 - q]
    keep[0] = keep_a[p] + recv_a[p]
    keep[1] = keep_b[q] + recv_b[q]


def second_sums(keep_a, recv_a, keep_b, recv_b, after):
    send = jax.ShapeDtypeStruct(keep_a.shape[1:], F32)
    out_shape = [jax.ShapeDtypeStruct(keep_a.shape, F32), send, send]
    return small(
        second_kernel,
        out_shape,
        [keep_a, recv_a, keep_b, recv_b, after],
        "second_sums",
        [IN_VMEM] * 4 + [ANYWHERE],
    )


def third_kernel(count_ref, keep, recv_a, recv_b, after, out, total, places):
    del after
    half = recv_a.shape[0]
    main = 2 * half
    total[0:half] = keep[0] + recv_a[...]
    total[half:main] = keep[1] + recv_b[...]
    total[main:] = jnp.zeros_like(total[main:])
    slot_places(count_ref, places)
    for slot in range(out.shape[0]):
        out[slot] = total[places[slot]]


def third_sums(halo_count, keep, recv_a, recv_b, after, slots):
    shape = (slots,) + keep.shape[2:]
    return small(
        third_kernel,
        jax.ShapeDtypeStruct(shape, F32),
        [halo_count, keep, recv_a, recv_b, after],
        "third_sums",
        [IN_SMEM] + [IN_VMEM] * 3 + [ANYWHERE],
        scratch=[pltpu.VMEM(shape, F32), pltpu.SMEM((slots,), jnp.int32)],
    )


def small(
    kernel, out_shape, args, name, specs=None, scratch=(), mebibytes=LIMIT_SMALL, flops=None
):
    size = max(x.size for x in args)
    return pl.pallas_call(
        kernel,
        out_shape=out_shape,
        in_specs=specs or [IN_VMEM] * len(args),
        out_specs=jax.tree.map(lambda _: IN_VMEM, out_shape),
        scratch_shapes=scratch,
        cost_estimate=pl.CostEstimate(
            flops=flops or size, bytes_accessed=12 * size, transcendentals=0
        ),
        compiler_params=limit(mebibytes),
        name=name,
    )(*args)


def sort_kernel(self_term, neigh_term, keep, send):
    core, _, _ = whereabouts()
    pieces, columns, rows, _ = keep.shape

    def copy(source, target):
        for g in range(pieces):
            for c in range(columns):
                some = (slice(g * rows, (g + 1) * rows), slice(c * BLOCK, (c + 1) * BLOCK))
                target[g, c] = source[some]

    @pl.when(core == 0)
    def _():
        copy(self_term, keep)
        copy(neigh_term, send)

    @pl.when(core != 0)
    def _():
        copy(neigh_term, keep)
        copy(self_term, send)


def grads_kernel(whole, other, self_grad, neigh_grad):
    core, _, _ = whereabouts()
    pieces, columns, rows, _ = whole.shape

    def copy(source, target):
        for g in range(pieces):
            for c in range(columns):
                some = (slice(g * rows, (g + 1) * rows), slice(c * BLOCK, (c + 1) * BLOCK))
                target[some] = source[g, c]

    @pl.when(core == 0)
    def _():
        copy(whole, self_grad)
        copy(other, neigh_grad)

    @pl.when(core != 0)
    def _():
        copy(other, self_grad)
        copy(whole, neigh_grad)


def scatter_kernel(axis_of, count, *rest):
    terms = rest[:count]
    outs = rest[-4:]
    me = axis_of(lax.axis_index("group"))
    for away, out in enumerate(outs):
        at = (me + away) & 3
        total = terms[0][at]
        for term in terms[1:]:
            total += term[at]
        out[...] = total


def scatter(axis_of, terms, name, after=()):
    piece = jax.ShapeDtypeStruct(terms[0].shape[1:], F32)
    return small(
        functools.partial(scatter_kernel, axis_of, len(terms)),
        [piece] * 4,
        [*terms, *after],
        name,
        [IN_VMEM] * len(terms) + [IN_SMEM] * len(after),
    )


def sum_kernel(*rest):
    *terms, _, out = rest
    total = terms[0][...]
    for term in terms[1:]:
        total += term[...]
    out[...] = total


def chips_kernel(scale, mine, pair, far_one, far_two, out):
    out[...] = ((mine[...] + pair[...]) + (far_one[...] + far_two[...])) * scale


def late_kernel(whole, *rest):
    rest[-1][...] = whole[...]


def place_kernel(count_ref, target_ref, arrived, after, send, *keeps):
    del after
    core, _, _ = whereabouts()
    chip = lax.axis_index("local") >> 1
    group = lax.axis_index("group")
    sources = count_ref.shape[0]
    capacity = arrived.shape[0] // sources
    blocks = send.shape[1]
    shift = blocks.bit_length() - 1
    for out in (send, *keeps):
        out[...] = jnp.zeros_like(out)

    @pl.loop(0, sources)
    def _(source):
        count = count_ref[source, group]
        for j in range(capacity):
            target = target_ref[source, group * capacity + j]
            member = lax.shift_right_logical(target, shift)
            block = target & (blocks - 1)
            away = (lax.shift_right_logical(member, 1) - chip) & 3
            mine = (member & 1) == core

            @pl.when(j < count)
            def _():
                @pl.when(jnp.logical_not(mine))
                def _():
                    send[away, block] += arrived[source * capacity + j]

                @pl.when(mine)
                def _():
                    for k, keep in enumerate(keeps):

                        @pl.when(away == k)
                        def _():
                            keep[block] += arrived[source * capacity + j]


def place(halo_count, halo_target, arrived, after, blocks):
    keep = jax.ShapeDtypeStruct((blocks,) + arrived.shape[1:], F32)
    send = jax.ShapeDtypeStruct((4,) + keep.shape, F32)
    specs = [IN_SMEM, IN_SMEM, IN_VMEM, ANYWHERE]
    args = [halo_count, halo_target, arrived, after]
    return small(place_kernel, [send] + [keep] * 4, args, "place", specs)


def self_kernel(pre_grad, weight, after, out):
    del after
    contract = (((1,), (1,)), ((), ()))
    weight_high, weight_low = split(weight[...])
    rows = out.shape[0] // 4
    for i in range(4):
        at = slice(i * rows, (i + 1) * rows)
        high, low = split(pre_grad[at])
        total = lax.dot_general(high, weight_high, contract, preferred_element_type=F32)
        total += lax.dot_general(high, weight_low, contract, preferred_element_type=F32)
        total += lax.dot_general(low, weight_high, contract, preferred_element_type=F32)
        out[at] = total


def finish_kernel(base, other_local, own_local, *rest):
    *received, out, total, rows, sems = rest
    core, _, _ = whereabouts()
    chip = lax.axis_index("local") >> 1
    blocks, width, _ = other_local.shape
    share = received[0].shape[1]
    own = pl.ds(pl.multiple_of(core * width, width), width)
    other = pl.ds(pl.multiple_of((1 - core) * width, width), width)
    copies = []
    for b in range(blocks):
        total[b, own] = own_local[b]
        total[b, other] = other_local[b]
        for k, some in enumerate(received):
            source = (chip - k // 2) & 3
            side = source >> 1
            quarter = side * 2 + ((source + side) & 1)
            first = core if k % 2 == 0 else 1 - core
            start = pl.multiple_of(first * width + quarter * share, share)
            total[b, pl.ds(start, share)] += some[b]
        at = slice(b * BLOCK, (b + 1) * BLOCK)
        rows[at] = base[at] + total[b].T
        copy = pltpu.make_async_copy(rows.at[at], out.at[at], sems.at[b])
        copy.start()
        copies.append(copy)
    for copy in copies:
        copy.wait()


def finish(base, other_local, own_local, received):
    node_rows, feat = base.shape
    blocks = other_local.shape[0]
    return pl.pallas_call(
        finish_kernel,
        out_shape=jax.ShapeDtypeStruct(base.shape, F32),
        in_specs=[IN_VMEM] * (3 + len(received)),
        out_specs=pl.BlockSpec(memory_space=pl.ANY),
        scratch_shapes=[
            pltpu.VMEM((blocks, feat, BLOCK), F32),
            pltpu.VMEM((node_rows, feat), F32),
            pltpu.SemaphoreType.DMA((blocks,)),
        ],
        cost_estimate=pl.CostEstimate(
            flops=2 * base.size, bytes_accessed=16 * base.size, transcendentals=0
        ),
        compiler_params=limit(8),
        name="finish",
    )(base, other_local, own_local, *received)


def on_device(
    features,
    aggregated,
    preact,
    grad_out,
    w_self,
    w_neigh,
    tile_vals,
    tile_col,
    halo_count,
    halo_target,
):
    high = lax.Precision.HIGH
    node_rows, width = features.shape
    blocks = node_rows // BLOCK
    groups = lax.axis_size("group")
    members = lax.axis_size("local")
    slot_count = halo_target.shape[1]
    dead = slot_count - MAIN
    swap = [(i, i ^ 1) for i in range(members)]
    pairs = [(i, i ^ 2) for i in range(members)]
    across = [(i, members - 2 - (i - i % 2) + i % 2) for i in range(members)]
    along_x = [[(i, (i + 2 * k) % members) for i in range(members)] for k in range(4)]
    along_y = [[(i, (i + 4 * k) % groups) for i in range(groups)] for k in range(4)]
    along_z = [[(i, i // 4 * 4 + (i + k) % 4) for i in range(groups)] for k in range(4)]

    pre_grad, other_local, send = tile_sums(
        tile_col, halo_count, w_neigh, tile_vals, MAIN, dead, preact=preact, grad_out=grad_out
    )
    recv = lax.ppermute(send, "local", swap)
    own_local, flag, keep_a, send_a, keep_b, send_b = tile_sums(
        tile_col, halo_count, w_neigh, tile_vals, MAIN, dead, pre_grad=pre_grad, recv=recv
    )
    recv_a = lax.ppermute(send_a, "local", pairs)
    recv_b = lax.ppermute(send_b, "local", across)

    contract = (((0,), (0,)), ((), ()))
    self_term = lax.dot_general(
        features, pre_grad, contract, precision=high, preferred_element_type=F32
    )
    neigh_term = lax.dot_general(
        aggregated, pre_grad, contract, precision=high, preferred_element_type=F32
    )
    pieces = jax.ShapeDtypeStruct((groups, width // BLOCK, width // groups, BLOCK), F32)
    stay, leave = small(sort_kernel, [pieces] * 2, [self_term, neigh_term], "sort_terms")
    by_y = (4, groups // 4) + pieces.shape[1:]
    stay, leave = stay.reshape(by_y), lax.ppermute(leave, "local", swap).reshape(by_y)
    mine, *sends = scatter(lambda g: g >> 2, [stay, leave], "sum_cores", [flag])
    terms = [mine] + [
        lax.ppermute(some, "group", along_y[k + 1]) for k, some in enumerate(sends)
    ]
    mine, *sends = scatter(lambda g: g & 3, terms, "sum_y")
    terms = [mine] + [
        lax.ppermute(some, "group", along_z[k + 1]) for k, some in enumerate(sends)
    ]

    keep, send_a, send_b = second_sums(keep_a, recv_a, keep_b, recv_b, mine)
    share_shape = jax.ShapeDtypeStruct(mine.shape, F32)
    share = small(sum_kernel, share_shape, [*terms, keep], "sum_z", [IN_VMEM] * 4 + [ANYWHERE])
    recv_a = lax.ppermute(send_a, "local", across)
    recv_b = lax.ppermute(send_b, "local", pairs)
    terms = [share] + [lax.ppermute(share, "local", p) for p in (pairs, across, along_x[2])]
    scale = float(node_rows * groups * members) ** (-0.5)
    share = small(functools.partial(chips_kernel, scale), share_shape, terms, "sum_chips")
    whole = lax.all_gather(share, "group", tiled=True)
    shares = third_sums(halo_count, keep, recv_a, recv_b, share, slot_count)
    base = small(
        self_kernel,
        jax.ShapeDtypeStruct(pre_grad.shape, F32),
        [pre_grad, w_self, shares],
        "self_rows",
        [IN_VMEM, IN_VMEM, ANYWHERE],
        mebibytes=16,
        flops=6 * pre_grad.size * width,
    )
    arrived = lax.all_to_all(shares, "group", split_axis=0, concat_axis=0, tiled=True)
    send, *keeps = place(halo_count, halo_target, arrived, base, blocks)
    swapped = lax.ppermute(send, "local", swap)
    received = []
    for k in range(4):
        pair = [keeps[k], swapped[k]]
        if k > 0:
            pair = [lax.ppermute(some, "local", along_x[k]) for some in pair]
        received += pair

    whole = small(
        late_kernel,
        pieces,
        [whole.reshape(pieces.shape), *received[2:]],
        "late",
        [IN_VMEM] + [ANYWHERE] * 6,
    )
    other = lax.ppermute(whole, "local", swap)
    square = jax.ShapeDtypeStruct(self_term.shape, F32)
    self_grad, neigh_grad = small(grads_kernel, [square] * 2, [whole, other], "sort_grads")

    node_grad = finish(base, other_local, own_local, received)
    return (node_grad, self_grad, neigh_grad)


def solution(mesh):
    in_specs = (
        P(("group", "local"), None),
        P(("group", "local"), None),
        P(("group", "local"), None),
        P(("group", "local"), None),
        P(),
        P(),
        P(("group", "local"), None, None),
        P(("group", "local")),
        P(),
        P(),
    )
    out_specs = (P(("group", "local"), None), P(), P())
    return jax.shard_map(
        on_device, mesh=mesh, in_specs=in_specs, out_specs=out_specs, check_vma=False
    )
```

```python
import functools

import jax
import jax.numpy as jnp
from jax import lax
from jax.experimental import pallas as pl
from jax.experimental.pallas import tpu as pltpu
from jax.sharding import PartitionSpec as P

F32 = jnp.float32
BF16 = jnp.bfloat16
BLOCK = 128
CHUNKS = 2
MAIN = 30
LIMIT_OTHER = 55
LIMIT_OWN = 20
LIMIT_SMALL = 6


def split(x):
    high = x.astype(BF16)
    low = (x - high.astype(F32)).astype(BF16)
    return high, low


def limit(mebibytes):
    return pltpu.CompilerParams(vmem_limit_bytes=mebibytes * 1024 * 1024)


def whereabouts():
    member = lax.axis_index("local")
    chip = member >> 1
    side = chip >> 1
    return member & 1, side, (chip + side) & 1


def slot_places(count_ref, places):
    slots = places.shape[0]
    owners = count_ref.shape[1]
    capacity = slots // owners
    group = lax.axis_index("group")

    def owner(o, carry):
        live, dead = carry
        count = count_ref[group, o]
        for j in range(capacity):
            is_live = j < count
            places[o * capacity + j] = jnp.where(is_live, live, slots - 1 - dead)
            live = live + is_live.astype(jnp.int32)
            dead = dead + 1 - is_live.astype(jnp.int32)
        return live, dead

    zero = jnp.int32(0)
    lax.fori_loop(0, owners, owner, (zero, zero))


def tile_kernel(own, blocks, main, over, col_ref, count_ref, *rest):
    if own:
        pre_hbm, weight_hbm, tiles_hbm, recv_ref, local_ref, flag_ref, *rest = rest
        keep_a, send_a, keep_b, send_b, pre, weight, tiles, sums, sems = rest
        column = col_ref
    else:
        pre_hbm, grad_hbm, weight_hbm, tiles_hbm, pre_ref, local_ref, send_ref, places, column, *rest = rest
        pre, grad, weight, tiles, sums, sems = rest
    width = weight.shape[0]
    rows = pre.shape[0] // CHUNKS
    count = tiles.shape[0] // CHUNKS
    core, p, q = whereabouts()
    half = core if own else 1 - core
    some = pl.ds(pl.multiple_of(half * width, width), width)
    weight_copy = pltpu.make_async_copy(weight_hbm.at[some], weight, sems.at[0])
    weight_copy.start()
    if own:
        flag_ref[0] = core
        main_sums = sums.at[pl.ds(blocks, main)]
        recv_copy = pltpu.make_async_copy(recv_ref, main_sums, sems.at[1])
        recv_copy.start()
    chunks = []
    for i in range(CHUNKS):
        at = pl.ds(i * rows, rows)
        copies = [pltpu.make_async_copy(pre_hbm.at[at], pre.at[at], sems.at[2 + 3 * i])]
        if not own:
            copies.append(pltpu.make_async_copy(grad_hbm.at[at], grad.at[at], sems.at[3 + 3 * i]))
        some_tiles = pl.ds(i * count, count)
        copies.append(
            pltpu.make_async_copy(tiles_hbm.at[some_tiles], tiles.at[some_tiles], sems.at[4 + 3 * i])
        )
        for copy in copies:
            copy.start()
        chunks.append(copies)
    sums[0:blocks] = jnp.zeros((blocks,) + sums.shape[1:], F32)
    sums[blocks + main :] = jnp.zeros((over,) + sums.shape[1:], F32)
    if not own:
        sums[blocks : blocks + main] = jnp.zeros((main,) + sums.shape[1:], F32)
    if not own:
        slot_places(count_ref, places)

        def place_tile(t, _):
            col = col_ref[t]
            slot = jnp.maximum(col - blocks, 0)
            column[t] = jnp.where(col < blocks, col, blocks + places[slot])
            return 0

        lax.fori_loop(0, tiles.shape[0], place_tile, 0)
    weight_copy.wait()
    weight_high, weight_low = split(weight[...])
    contract = (((1,), (1,)), ((), ()))
    pre_copies = []
    for i in range(CHUNKS):
        at = pl.ds(i * rows, rows)
        *copies, tiles_copy = chunks[i]
        for copy in copies:
            copy.wait()
        if own:
            pre_grad = pre[at]
        else:
            pre_grad = jnp.where(pre[at] > 0, grad[at], 0.0)
            grad[at] = pre_grad
            pre_copy = pltpu.make_async_copy(grad.at[at], pre_ref.at[at], sems.at[2 + 3 * i])
            pre_copy.start()
            pre_copies.append(pre_copy)
        pre_high, pre_low = split(pre_grad)
        part = lax.dot_general(weight_high, pre_high, contract, preferred_element_type=F32)
        part += lax.dot_general(weight_high, pre_low, contract, preferred_element_type=F32)
        part += lax.dot_general(weight_low, pre_high, contract, preferred_element_type=F32)
        row_high, row_low = split(part)
        tiles_copy.wait()
        if own and i == 0:
            recv_copy.wait()
        for r in range(rows // BLOCK):
            mine = slice(r * BLOCK, (r + 1) * BLOCK)
            high = row_high[:, mine]
            left = jnp.concatenate([high, high, row_low[:, mine]], axis=1)
            each = count * BLOCK // rows
            for k in range(0, each, 2):
                t = i * count + r * each + k
                first_high, first_low = split(tiles[t])
                next_high, next_low = split(tiles[t + 1])
                high = jnp.concatenate([first_high, next_high], axis=1)
                low = jnp.concatenate([first_low, next_low], axis=1)
                right = jnp.concatenate([high, low, high], axis=0)
                product = jnp.dot(left, right, preferred_element_type=F32)
                sums[column[t]] += product[:, :BLOCK]
                sums[column[t + 1]] += product[:, BLOCK:]

    copies = []

    def out(source, target):
        copy = pltpu.make_async_copy(source, target, sems.at[2 + 3 * CHUNKS + len(copies)])
        copy.start()
        copies.append(copy)

    if own:
        some = main // 2
        share = width // 4

        def piece(first, p_at, q_at, target):
            share_rows = pl.ds(pl.multiple_of((p_at * 2 + q_at) * share, share), share)
            out(sums.at[pl.ds(blocks + first, some), share_rows], target)

        for k in range(2):
            piece(0, k, 1 - q, send_a.at[k])
            piece(some, 1 - p, k, send_b.at[k])
        for k in range(2):
            piece(0, k, q, keep_a.at[k])
            piece(some, p, k, keep_b.at[k])
    else:
        out(sums.at[pl.ds(blocks, main)], send_ref)
    out(sums.at[pl.ds(0, blocks)], local_ref)
    for copy in pre_copies + copies:
        copy.wait()


def tile_sums(
    tile_col, halo_count, weight, tile_vals, main, over, preact=None, grad_out=None,
    pre_grad=None, recv=None,
):
    own = recv is not None
    node_rows, feat = (pre_grad if own else preact).shape
    width = weight.shape[0] // 2
    blocks = node_rows // BLOCK
    some = main // 2
    anywhere = pl.BlockSpec(memory_space=pl.ANY)
    local = jax.ShapeDtypeStruct((blocks, width, BLOCK), F32)
    piece = jax.ShapeDtypeStruct((2, some, width // 4, BLOCK), F32)
    if own:
        args = [pre_grad, weight, tile_vals, recv]
        flag = jax.ShapeDtypeStruct((1,), jnp.int32)
        out_shape = [local, flag] + [piece] * 4
    else:
        args = [preact, grad_out, weight, tile_vals]
        out_shape = [
            jax.ShapeDtypeStruct((node_rows, feat), F32),
            local,
            jax.ShapeDtypeStruct((main, width, BLOCK), F32),
            jax.ShapeDtypeStruct((main + over,), jnp.int32),
            jax.ShapeDtypeStruct(tile_col.shape, jnp.int32),
        ]
    scratch = [pltpu.VMEM((node_rows, feat), F32)]
    if not own:
        scratch.append(pltpu.VMEM((node_rows, feat), F32))
    scratch += [
        pltpu.VMEM((width, feat), F32),
        pltpu.VMEM(tile_vals.shape, F32),
        pltpu.VMEM((blocks + main + over, width, BLOCK), F32),
        pltpu.SemaphoreType.DMA((2 + 3 * CHUNKS + 10,)),
    ]
    return pl.pallas_call(
        functools.partial(tile_kernel, own, blocks, main, over),
        out_shape=out_shape,
        in_specs=[pl.BlockSpec(memory_space=pltpu.SMEM)] * 2 + [anywhere] * len(args),
        out_specs=[
            pl.BlockSpec(memory_space=pltpu.SMEM) if x.dtype == jnp.int32 else anywhere
            for x in out_shape
        ],
        scratch_shapes=scratch,
        compiler_params=limit(LIMIT_OWN if own else LIMIT_OTHER),
        cost_estimate=pl.CostEstimate(
            flops=6 * (tile_vals.size + node_rows * feat) * width,
            bytes_accessed=14 * 1024 * 1024,
            transcendentals=0,
        ),
        name="own_tile_sums" if own else "other_tile_sums",
    )(tile_col, halo_count, *args)


IN_VMEM = pl.BlockSpec(memory_space=pltpu.VMEM)
IN_SMEM = pl.BlockSpec(memory_space=pltpu.SMEM)
ANYWHERE = pl.BlockSpec(memory_space=pl.ANY)


def second_kernel(keep_a, recv_a, keep_b, recv_b, after, keep, send_a, send_b):
    del after
    _, p, q = whereabouts()
    send_a[...] = keep_a[1 - p] + recv_a[1 - p]
    send_b[...] = keep_b[1 - q] + recv_b[1 - q]
    keep[0] = keep_a[p] + recv_a[p]
    keep[1] = keep_b[q] + recv_b[q]


def second_sums(keep_a, recv_a, keep_b, recv_b, after):
    send = jax.ShapeDtypeStruct(keep_a.shape[1:], F32)
    out_shape = [jax.ShapeDtypeStruct(keep_a.shape, F32), send, send]
    return small(
        second_kernel,
        out_shape,
        [keep_a, recv_a, keep_b, recv_b, after],
        "second_sums",
        [IN_VMEM] * 4 + [ANYWHERE],
    )


def third_kernel(places, keep, recv_a, recv_b, after, out, total):
    del after
    half = recv_a.shape[0]
    main = 2 * half
    total[0:half] = keep[0] + recv_a[...]
    total[half:main] = keep[1] + recv_b[...]
    total[main:] = jnp.zeros_like(total[main:])
    for slot in range(out.shape[0]):
        out[slot] = total[places[slot]]


def third_sums(places, keep, recv_a, recv_b, after):
    shape = (places.shape[0],) + keep.shape[2:]
    return small(
        third_kernel,
        jax.ShapeDtypeStruct(shape, F32),
        [places, keep, recv_a, recv_b, after],
        "third_sums",
        [IN_SMEM] + [IN_VMEM] * 3 + [ANYWHERE],
        scratch=[pltpu.VMEM(shape, F32)],
    )


def small(
    kernel, out_shape, args, name, specs=None, scratch=(), mebibytes=LIMIT_SMALL, flops=None
):
    size = max(x.size for x in args)
    return pl.pallas_call(
        kernel,
        out_shape=out_shape,
        in_specs=specs or [IN_VMEM] * len(args),
        out_specs=jax.tree.map(lambda _: IN_VMEM, out_shape),
        scratch_shapes=scratch,
        cost_estimate=pl.CostEstimate(
            flops=flops or size, bytes_accessed=12 * size, transcendentals=0
        ),
        compiler_params=limit(mebibytes),
        name=name,
    )(*args)


def sort_kernel(self_term, neigh_term, keep, send):
    core, _, _ = whereabouts()
    pieces, columns, rows, _ = keep.shape

    def copy(source, target):
        for g in range(pieces):
            for c in range(columns):
                some = (slice(g * rows, (g + 1) * rows), slice(c * BLOCK, (c + 1) * BLOCK))
                target[g, c] = source[some]

    @pl.when(core == 0)
    def _():
        copy(self_term, keep)
        copy(neigh_term, send)

    @pl.when(core != 0)
    def _():
        copy(neigh_term, keep)
        copy(self_term, send)


def grads_kernel(whole, other, self_grad, neigh_grad):
    core, _, _ = whereabouts()
    pieces, columns, rows, _ = whole.shape

    def copy(source, target):
        for g in range(pieces):
            for c in range(columns):
                some = (slice(g * rows, (g + 1) * rows), slice(c * BLOCK, (c + 1) * BLOCK))
                target[some] = source[g, c]

    @pl.when(core == 0)
    def _():
        copy(whole, self_grad)
        copy(other, neigh_grad)

    @pl.when(core != 0)
    def _():
        copy(other, self_grad)
        copy(whole, neigh_grad)


def scatter_kernel(axis_of, count, *rest):
    terms = rest[:count]
    outs = rest[-4:]
    me = axis_of(lax.axis_index("group"))
    for away, out in enumerate(outs):
        at = (me + away) & 3
        total = terms[0][at]
        for term in terms[1:]:
            total += term[at]
        out[...] = total


def scatter(axis_of, terms, name, after=()):
    piece = jax.ShapeDtypeStruct(terms[0].shape[1:], F32)
    return small(
        functools.partial(scatter_kernel, axis_of, len(terms)),
        [piece] * 4,
        [*terms, *after],
        name,
        [IN_VMEM] * len(terms) + [IN_SMEM] * len(after),
    )


def sum_kernel(*rest):
    *terms, _, out = rest
    total = terms[0][...]
    for term in terms[1:]:
        total += term[...]
    out[...] = total


def chips_kernel(scale, mine, pair, far_one, far_two, out):
    out[...] = ((mine[...] + pair[...]) + (far_one[...] + far_two[...])) * scale


def pass_kernel(value, *rest):
    rest[-1][...] = value[...]


def gather_kernel(axis_of, *rest):
    pieces = rest[:4]
    out = rest[-1]
    me = axis_of(lax.axis_index("group"))
    for away, piece in enumerate(pieces):
        out[(me - away) & 3] = piece[...]


def gather(axis_of, pieces, name):
    whole = jax.ShapeDtypeStruct((4,) + pieces[0].shape, F32)
    return small(functools.partial(gather_kernel, axis_of), whole, pieces, name)


def place_kernel(count_ref, target_ref, arrived, after, send, *keeps):
    del after
    core, _, _ = whereabouts()
    chip = lax.axis_index("local") >> 1
    group = lax.axis_index("group")
    sources = count_ref.shape[0]
    capacity = arrived.shape[0] // sources
    blocks = send.shape[1]
    shift = blocks.bit_length() - 1
    for out in (send, *keeps):
        out[...] = jnp.zeros_like(out)

    @pl.loop(0, sources)
    def _(source):
        count = count_ref[source, group]
        for j in range(capacity):
            target = target_ref[source, group * capacity + j]
            member = lax.shift_right_logical(target, shift)
            block = target & (blocks - 1)
            away = (lax.shift_right_logical(member, 1) - chip) & 3
            mine = (member & 1) == core

            @pl.when(j < count)
            def _():
                @pl.when(jnp.logical_not(mine))
                def _():
                    send[away, block] += arrived[source * capacity + j]

                @pl.when(mine)
                def _():
                    for k, keep in enumerate(keeps):

                        @pl.when(away == k)
                        def _():
                            keep[block] += arrived[source * capacity + j]


def place(halo_count, halo_target, arrived, after, blocks):
    keep = jax.ShapeDtypeStruct((blocks,) + arrived.shape[1:], F32)
    send = jax.ShapeDtypeStruct((4,) + keep.shape, F32)
    specs = [IN_SMEM, IN_SMEM, IN_VMEM, ANYWHERE]
    args = [halo_count, halo_target, arrived, after]
    return small(place_kernel, [send] + [keep] * 4, args, "place", specs)


def self_kernel(pre_grad, weight, after, out):
    del after
    contract = (((1,), (1,)), ((), ()))
    weight_high, weight_low = split(weight[...])
    rows = out.shape[0] // 4
    for i in range(4):
        at = slice(i * rows, (i + 1) * rows)
        high, low = split(pre_grad[at])
        total = lax.dot_general(high, weight_high, contract, preferred_element_type=F32)
        total += lax.dot_general(high, weight_low, contract, preferred_element_type=F32)
        total += lax.dot_general(low, weight_high, contract, preferred_element_type=F32)
        out[at] = total


def finish_kernel(base, other_local, own_local, *rest):
    *received, out, total, rows, sems = rest
    core, _, _ = whereabouts()
    chip = lax.axis_index("local") >> 1
    blocks, width, _ = other_local.shape
    share = received[0].shape[1]
    own = pl.ds(pl.multiple_of(core * width, width), width)
    other = pl.ds(pl.multiple_of((1 - core) * width, width), width)
    copies = []
    for b in range(blocks):
        total[b, own] = own_local[b]
        total[b, other] = other_local[b]
        for k, some in enumerate(received):
            source = (chip - k // 2) & 3
            side = source >> 1
            quarter = side * 2 + ((source + side) & 1)
            first = core if k % 2 == 0 else 1 - core
            start = pl.multiple_of(first * width + quarter * share, share)
            total[b, pl.ds(start, share)] += some[b]
        at = slice(b * BLOCK, (b + 1) * BLOCK)
        rows[at] = base[at] + total[b].T
        copy = pltpu.make_async_copy(rows.at[at], out.at[at], sems.at[b])
        copy.start()
        copies.append(copy)
    for copy in copies:
        copy.wait()


def finish(base, other_local, own_local, received):
    node_rows, feat = base.shape
    blocks = other_local.shape[0]
    return pl.pallas_call(
        finish_kernel,
        out_shape=jax.ShapeDtypeStruct(base.shape, F32),
        in_specs=[IN_VMEM] * (3 + len(received)),
        out_specs=pl.BlockSpec(memory_space=pl.ANY),
        scratch_shapes=[
            pltpu.VMEM((blocks, feat, BLOCK), F32),
            pltpu.VMEM((node_rows, feat), F32),
            pltpu.SemaphoreType.DMA((blocks,)),
        ],
        cost_estimate=pl.CostEstimate(
            flops=2 * base.size, bytes_accessed=16 * base.size, transcendentals=0
        ),
        compiler_params=limit(8),
        name="finish",
    )(base, other_local, own_local, *received)


def on_device(
    features,
    aggregated,
    preact,
    grad_out,
    w_self,
    w_neigh,
    tile_vals,
    tile_col,
    halo_count,
    halo_target,
):
    high = lax.Precision.HIGH
    node_rows, width = features.shape
    blocks = node_rows // BLOCK
    groups = lax.axis_size("group")
    members = lax.axis_size("local")
    slot_count = halo_target.shape[1]
    dead = slot_count - MAIN
    swap = [(i, i ^ 1) for i in range(members)]
    pairs = [(i, i ^ 2) for i in range(members)]
    across = [(i, members - 2 - (i - i % 2) + i % 2) for i in range(members)]
    along_x = [[(i, (i + 2 * k) % members) for i in range(members)] for k in range(4)]
    along_y = [[(i, (i + 4 * k) % groups) for i in range(groups)] for k in range(4)]
    along_z = [[(i, i // 4 * 4 + (i + k) % 4) for i in range(groups)] for k in range(4)]

    pre_grad, other_local, send, places, column = tile_sums(
        tile_col, halo_count, w_neigh, tile_vals, MAIN, dead, preact=preact, grad_out=grad_out
    )
    recv = lax.ppermute(send, "local", swap)
    own_local, flag, keep_a, send_a, keep_b, send_b = tile_sums(
        column, halo_count, w_neigh, tile_vals, MAIN, dead, pre_grad=pre_grad, recv=recv
    )
    recv_a = lax.ppermute(send_a, "local", pairs)
    recv_b = lax.ppermute(send_b, "local", across)

    contract = (((0,), (0,)), ((), ()))
    self_term = lax.dot_general(
        features, pre_grad, contract, precision=high, preferred_element_type=F32
    )
    neigh_term = lax.dot_general(
        aggregated, pre_grad, contract, precision=high, preferred_element_type=F32
    )
    pieces = jax.ShapeDtypeStruct((groups, width // BLOCK, width // groups, BLOCK), F32)
    stay, leave = small(sort_kernel, [pieces] * 2, [self_term, neigh_term], "sort_terms")
    by_y = (4, groups // 4) + pieces.shape[1:]
    stay, leave = stay.reshape(by_y), lax.ppermute(leave, "local", swap).reshape(by_y)
    mine, *sends = scatter(lambda g: g >> 2, [stay, leave], "sum_cores", [flag])
    terms = [mine] + [
        lax.ppermute(some, "group", along_y[k + 1]) for k, some in enumerate(sends)
    ]
    mine, *sends = scatter(lambda g: g & 3, terms, "sum_y")
    terms = [mine] + [
        lax.ppermute(some, "group", along_z[k + 1]) for k, some in enumerate(sends)
    ]

    base = small(
        self_kernel,
        jax.ShapeDtypeStruct(pre_grad.shape, F32),
        [pre_grad, w_self, mine],
        "self_rows",
        [IN_VMEM, IN_VMEM, ANYWHERE],
        mebibytes=16,
        flops=6 * pre_grad.size * width,
    )
    keep, send_a, send_b = second_sums(keep_a, recv_a, keep_b, recv_b, base)
    recv_a = lax.ppermute(send_a, "local", across)
    recv_b = lax.ppermute(send_b, "local", pairs)
    share_shape = jax.ShapeDtypeStruct(mine.shape, F32)
    share = small(sum_kernel, share_shape, [*terms, keep], "sum_z", [IN_VMEM] * 4 + [ANYWHERE])
    shares = third_sums(places, keep, recv_a, recv_b, share)
    arrived = lax.all_to_all(shares, "group", split_axis=0, concat_axis=0, tiled=True)

    share = small(pass_kernel, share_shape, [share, shares], "pass", [IN_VMEM, ANYWHERE])
    terms = [share] + [lax.ppermute(share, "local", p) for p in (pairs, across, along_x[2])]
    scale = float(node_rows * groups * members) ** (-0.5)
    share = small(functools.partial(chips_kernel, scale), share_shape, terms, "sum_chips")
    terms = [share] + [lax.ppermute(share, "group", along_z[k]) for k in range(1, 4)]

    row = gather(lambda g: g & 3, terms, "gather_z")
    rows_of_y = [[z + 4 * y for y in range(4)] for z in range(4)]
    whole = lax.all_gather(row, "group", axis_index_groups=rows_of_y)

    send, *keeps = place(halo_count, halo_target, arrived, row, blocks)
    swapped = lax.ppermute(send, "local", swap)
    received = []
    for k in range(4):
        pair = [keeps[k], swapped[k]]
        if k > 0:
            pair = [lax.ppermute(some, "local", along_x[k]) for some in pair]
        received += pair

    whole = small(
        pass_kernel,
        pieces,
        [whole.reshape(pieces.shape), *received[2:]],
        "pass",
        [IN_VMEM] + [ANYWHERE] * 6,
    )
    other = lax.ppermute(whole, "local", swap)
    square = jax.ShapeDtypeStruct(self_term.shape, F32)
    self_grad, neigh_grad = small(grads_kernel, [square] * 2, [whole, other], "sort_grads")

    node_grad = finish(base, other_local, own_local, received)
    return (node_grad, self_grad, neigh_grad)


def solution(mesh):
    in_specs = (
        P(("group", "local"), None),
        P(("group", "local"), None),
        P(("group", "local"), None),
        P(("group", "local"), None),
        P(),
        P(),
        P(("group", "local"), None, None),
        P(("group", "local")),
        P(),
        P(),
    )
    out_specs = (P(("group", "local"), None), P(), P())
    return jax.shard_map(
        on_device, mesh=mesh, in_specs=in_specs, out_specs=out_specs, check_vma=False
    )
```

```python
import functools

import jax
import jax.numpy as jnp
from jax import lax
from jax.experimental import pallas as pl
from jax.experimental.pallas import tpu as pltpu
from jax.sharding import PartitionSpec as P

F32 = jnp.float32
BF16 = jnp.bfloat16
BLOCK = 128
CHUNKS = 2
MAIN = 30
LIMIT_OTHER = 55
LIMIT_OWN = 20
LIMIT_SMALL = 6


def split(x):
    high = x.astype(BF16)
    low = (x - high.astype(F32)).astype(BF16)
    return high, low


def limit(mebibytes):
    return pltpu.CompilerParams(vmem_limit_bytes=mebibytes * 1024 * 1024)


def whereabouts():
    member = lax.axis_index("local")
    chip = member >> 1
    side = chip >> 1
    return member & 1, side, (chip + side) & 1


def slot_places(count_ref, places):
    slots = places.shape[0]
    owners = count_ref.shape[1]
    capacity = slots // owners
    group = lax.axis_index("group")

    def owner(o, carry):
        live, dead = carry
        count = count_ref[group, o]
        for j in range(capacity):
            is_live = j < count
            places[o * capacity + j] = jnp.where(is_live, live, slots - 1 - dead)
            live = live + is_live.astype(jnp.int32)
            dead = dead + 1 - is_live.astype(jnp.int32)
        return live, dead

    zero = jnp.int32(0)
    lax.fori_loop(0, owners, owner, (zero, zero))


def tile_kernel(own, blocks, main, over, col_ref, count_ref, *rest):
    if own:
        pre_hbm, weight_hbm, tiles_hbm, recv_ref, local_ref, flag_ref, *rest = rest
        keep_a, send_a, keep_b, send_b, pre, weight, tiles, sums, sems = rest
        column = col_ref
    else:
        pre_hbm, grad_hbm, weight_hbm, tiles_hbm, pre_ref, local_ref, send_ref, places, column, *rest = rest
        pre, grad, weight, tiles, sums, sems = rest
    width = weight.shape[0]
    rows = pre.shape[0] // CHUNKS
    count = tiles.shape[0] // CHUNKS
    core, p, q = whereabouts()
    half = core if own else 1 - core
    some = pl.ds(pl.multiple_of(half * width, width), width)
    weight_copy = pltpu.make_async_copy(weight_hbm.at[some], weight, sems.at[0])
    weight_copy.start()
    if own:
        flag_ref[0] = core
        main_sums = sums.at[pl.ds(blocks, main)]
        recv_copy = pltpu.make_async_copy(recv_ref, main_sums, sems.at[1])
        recv_copy.start()
    chunks = []
    for i in range(CHUNKS):
        at = pl.ds(i * rows, rows)
        copies = [pltpu.make_async_copy(pre_hbm.at[at], pre.at[at], sems.at[2 + 3 * i])]
        if not own:
            copies.append(pltpu.make_async_copy(grad_hbm.at[at], grad.at[at], sems.at[3 + 3 * i]))
        some_tiles = pl.ds(i * count, count)
        copies.append(
            pltpu.make_async_copy(tiles_hbm.at[some_tiles], tiles.at[some_tiles], sems.at[4 + 3 * i])
        )
        for copy in copies:
            copy.start()
        chunks.append(copies)
    sums[0:blocks] = jnp.zeros((blocks,) + sums.shape[1:], F32)
    sums[blocks + main :] = jnp.zeros((over,) + sums.shape[1:], F32)
    if not own:
        sums[blocks : blocks + main] = jnp.zeros((main,) + sums.shape[1:], F32)
    if not own:
        slot_places(count_ref, places)

        def place_tile(t, _):
            col = col_ref[t]
            slot = jnp.maximum(col - blocks, 0)
            column[t] = jnp.where(col < blocks, col, blocks + places[slot])
            return 0

        lax.fori_loop(0, tiles.shape[0], place_tile, 0)
    weight_copy.wait()
    weight_high, weight_low = split(weight[...])
    contract = (((1,), (1,)), ((), ()))
    pre_copies = []
    for i in range(CHUNKS):
        at = pl.ds(i * rows, rows)
        *copies, tiles_copy = chunks[i]
        for copy in copies:
            copy.wait()
        if own:
            pre_grad = pre[at]
        else:
            pre_grad = jnp.where(pre[at] > 0, grad[at], 0.0)
            grad[at] = pre_grad
            pre_copy = pltpu.make_async_copy(grad.at[at], pre_ref.at[at], sems.at[2 + 3 * i])
            pre_copy.start()
            pre_copies.append(pre_copy)
        pre_high, pre_low = split(pre_grad)
        part = lax.dot_general(weight_high, pre_high, contract, preferred_element_type=F32)
        part += lax.dot_general(weight_high, pre_low, contract, preferred_element_type=F32)
        part += lax.dot_general(weight_low, pre_high, contract, preferred_element_type=F32)
        row_high, row_low = split(part)
        tiles_copy.wait()
        if own and i == 0:
            recv_copy.wait()
        for r in range(rows // BLOCK):
            mine = slice(r * BLOCK, (r + 1) * BLOCK)
            high = row_high[:, mine]
            left = jnp.concatenate([high, high, row_low[:, mine]], axis=1)
            each = count * BLOCK // rows
            for k in range(0, each, 2):
                t = i * count + r * each + k
                first_high, first_low = split(tiles[t])
                next_high, next_low = split(tiles[t + 1])
                high = jnp.concatenate([first_high, next_high], axis=1)
                low = jnp.concatenate([first_low, next_low], axis=1)
                right = jnp.concatenate([high, low, high], axis=0)
                product = jnp.dot(left, right, preferred_element_type=F32)
                sums[column[t]] += product[:, :BLOCK]
                sums[column[t + 1]] += product[:, BLOCK:]

    copies = []

    def out(source, target):
        copy = pltpu.make_async_copy(source, target, sems.at[2 + 3 * CHUNKS + len(copies)])
        copy.start()
        copies.append(copy)

    if own:
        some = main // 2
        share = width // 4

        def piece(first, p_at, q_at, target):
            share_rows = pl.ds(pl.multiple_of((p_at * 2 + q_at) * share, share), share)
            out(sums.at[pl.ds(blocks + first, some), share_rows], target)

        for k in range(2):
            piece(0, k, 1 - q, send_a.at[k])
            piece(some, 1 - p, k, send_b.at[k])
        for k in range(2):
            piece(0, k, q, keep_a.at[k])
            piece(some, p, k, keep_b.at[k])
    else:
        out(sums.at[pl.ds(blocks, main)], send_ref)
    out(sums.at[pl.ds(0, blocks)], local_ref)
    for copy in pre_copies + copies:
        copy.wait()


def tile_sums(
    tile_col, halo_count, weight, tile_vals, main, over, preact=None, grad_out=None,
    pre_grad=None, recv=None,
):
    own = recv is not None
    node_rows, feat = (pre_grad if own else preact).shape
    width = weight.shape[0] // 2
    blocks = node_rows // BLOCK
    some = main // 2
    anywhere = pl.BlockSpec(memory_space=pl.ANY)
    local = jax.ShapeDtypeStruct((blocks, width, BLOCK), F32)
    piece = jax.ShapeDtypeStruct((2, some, width // 4, BLOCK), F32)
    if own:
        args = [pre_grad, weight, tile_vals, recv]
        flag = jax.ShapeDtypeStruct((1,), jnp.int32)
        out_shape = [local, flag] + [piece] * 4
    else:
        args = [preact, grad_out, weight, tile_vals]
        out_shape = [
            jax.ShapeDtypeStruct((node_rows, feat), F32),
            local,
            jax.ShapeDtypeStruct((main, width, BLOCK), F32),
            jax.ShapeDtypeStruct((main + over,), jnp.int32),
            jax.ShapeDtypeStruct(tile_col.shape, jnp.int32),
        ]
    scratch = [pltpu.VMEM((node_rows, feat), F32)]
    if not own:
        scratch.append(pltpu.VMEM((node_rows, feat), F32))
    scratch += [
        pltpu.VMEM((width, feat), F32),
        pltpu.VMEM(tile_vals.shape, F32),
        pltpu.VMEM((blocks + main + over, width, BLOCK), F32),
        pltpu.SemaphoreType.DMA((2 + 3 * CHUNKS + 10,)),
    ]
    return pl.pallas_call(
        functools.partial(tile_kernel, own, blocks, main, over),
        out_shape=out_shape,
        in_specs=[pl.BlockSpec(memory_space=pltpu.SMEM)] * 2 + [anywhere] * len(args),
        out_specs=[
            pl.BlockSpec(memory_space=pltpu.SMEM) if x.dtype == jnp.int32 else anywhere
            for x in out_shape
        ],
        scratch_shapes=scratch,
        compiler_params=limit(LIMIT_OWN if own else LIMIT_OTHER),
        cost_estimate=pl.CostEstimate(
            flops=6 * (tile_vals.size + node_rows * feat) * width,
            bytes_accessed=14 * 1024 * 1024,
            transcendentals=0,
        ),
        name="own_tile_sums" if own else "other_tile_sums",
    )(tile_col, halo_count, *args)


IN_VMEM = pl.BlockSpec(memory_space=pltpu.VMEM)
IN_SMEM = pl.BlockSpec(memory_space=pltpu.SMEM)
ANYWHERE = pl.BlockSpec(memory_space=pl.ANY)


def second_kernel(keep_a, recv_a, keep_b, recv_b, *rest):
    keep, send_a, send_b = rest[-3:]
    _, p, q = whereabouts()
    send_a[...] = keep_a[1 - p] + recv_a[1 - p]
    send_b[...] = keep_b[1 - q] + recv_b[1 - q]
    keep[0] = keep_a[p] + recv_a[p]
    keep[1] = keep_b[q] + recv_b[q]


def second_sums(keep_a, recv_a, keep_b, recv_b, after):
    send = jax.ShapeDtypeStruct(keep_a.shape[1:], F32)
    out_shape = [jax.ShapeDtypeStruct(keep_a.shape, F32), send, send]
    return small(
        second_kernel,
        out_shape,
        [keep_a, recv_a, keep_b, recv_b, *after],
        "second_sums",
        [IN_VMEM] * 4 + [ANYWHERE] * len(after),
    )


def third_kernel(places, keep, recv_a, recv_b, after, out, total):
    del after
    half = recv_a.shape[0]
    main = 2 * half
    total[0:half] = keep[0] + recv_a[...]
    total[half:main] = keep[1] + recv_b[...]
    total[main:] = jnp.zeros_like(total[main:])
    for slot in range(out.shape[0]):
        out[slot] = total[places[slot]]


def third_sums(places, keep, recv_a, recv_b, after):
    shape = (places.shape[0],) + keep.shape[2:]
    return small(
        third_kernel,
        jax.ShapeDtypeStruct(shape, F32),
        [places, keep, recv_a, recv_b, after],
        "third_sums",
        [IN_SMEM] + [IN_VMEM] * 3 + [ANYWHERE],
        scratch=[pltpu.VMEM(shape, F32)],
    )


def small(
    kernel, out_shape, args, name, specs=None, scratch=(), mebibytes=LIMIT_SMALL, flops=None
):
    size = max(x.size for x in args)
    return pl.pallas_call(
        kernel,
        out_shape=out_shape,
        in_specs=specs or [IN_VMEM] * len(args),
        out_specs=jax.tree.map(lambda _: IN_VMEM, out_shape),
        scratch_shapes=scratch,
        cost_estimate=pl.CostEstimate(
            flops=flops or size, bytes_accessed=12 * size, transcendentals=0
        ),
        compiler_params=limit(mebibytes),
        name=name,
    )(*args)


def sort_kernel(self_term, neigh_term, keep, send):
    core, _, _ = whereabouts()
    pieces, columns, rows, _ = keep.shape

    def copy(source, target):
        for g in range(pieces):
            for c in range(columns):
                some = (slice(g * rows, (g + 1) * rows), slice(c * BLOCK, (c + 1) * BLOCK))
                target[g, c] = source[some]

    @pl.when(core == 0)
    def _():
        copy(self_term, keep)
        copy(neigh_term, send)

    @pl.when(core != 0)
    def _():
        copy(neigh_term, keep)
        copy(self_term, send)


def grads_kernel(whole, other, self_grad, neigh_grad):
    core, _, _ = whereabouts()
    pieces, columns, rows, _ = whole.shape

    def copy(source, target):
        for g in range(pieces):
            for c in range(columns):
                some = (slice(g * rows, (g + 1) * rows), slice(c * BLOCK, (c + 1) * BLOCK))
                target[some] = source[g, c]

    @pl.when(core == 0)
    def _():
        copy(whole, self_grad)
        copy(other, neigh_grad)

    @pl.when(core != 0)
    def _():
        copy(other, self_grad)
        copy(whole, neigh_grad)


def scatter_kernel(axis_of, count, *rest):
    terms = rest[:count]
    outs = rest[-4:]
    me = axis_of(lax.axis_index("group"))
    for away, out in enumerate(outs):
        at = (me + away) & 3
        total = terms[0][at]
        for term in terms[1:]:
            total += term[at]
        out[...] = total


def scatter(axis_of, terms, name, after=()):
    piece = jax.ShapeDtypeStruct(terms[0].shape[1:], F32)
    return small(
        functools.partial(scatter_kernel, axis_of, len(terms)),
        [piece] * 4,
        [*terms, *after],
        name,
        [IN_VMEM] * len(terms) + [IN_SMEM] * len(after),
    )


def sum_kernel(*rest):
    *terms, out = rest
    total = terms[0][...]
    for term in terms[1:]:
        total += term[...]
    out[...] = total


def chips_kernel(scale, mine, pair, far_one, far_two, out):
    out[...] = ((mine[...] + pair[...]) + (far_one[...] + far_two[...])) * scale


def pass_kernel(value, *rest):
    rest[-1][...] = value[...]


def gather_kernel(axis_of, *rest):
    pieces = rest[:4]
    out = rest[-1]
    me = axis_of(lax.axis_index("group"))
    for away, piece in enumerate(pieces):
        out[(me - away) & 3] = piece[...]


def gather(axis_of, pieces, name, after=()):
    whole = jax.ShapeDtypeStruct((4,) + pieces[0].shape, F32)
    specs = [IN_VMEM] * 4 + [ANYWHERE] * len(after)
    return small(functools.partial(gather_kernel, axis_of), whole, [*pieces, *after], name, specs)


def place_kernel(count_ref, target_ref, arrived, after, send, *keeps):
    del after
    core, _, _ = whereabouts()
    chip = lax.axis_index("local") >> 1
    group = lax.axis_index("group")
    sources = count_ref.shape[0]
    capacity = arrived.shape[0] // sources
    blocks = send.shape[1]
    shift = blocks.bit_length() - 1
    for out in (send, *keeps):
        out[...] = jnp.zeros_like(out)

    @pl.loop(0, sources)
    def _(source):
        count = count_ref[source, group]
        for j in range(capacity):
            target = target_ref[source, group * capacity + j]
            member = lax.shift_right_logical(target, shift)
            block = target & (blocks - 1)
            away = (lax.shift_right_logical(member, 1) - chip) & 3
            mine = (member & 1) == core

            @pl.when(j < count)
            def _():
                @pl.when(jnp.logical_not(mine))
                def _():
                    send[away, block] += arrived[source * capacity + j]

                @pl.when(mine)
                def _():
                    for k, keep in enumerate(keeps):

                        @pl.when(away == k)
                        def _():
                            keep[block] += arrived[source * capacity + j]


def place(halo_count, halo_target, arrived, after, blocks):
    keep = jax.ShapeDtypeStruct((blocks,) + arrived.shape[1:], F32)
    send = jax.ShapeDtypeStruct((4,) + keep.shape, F32)
    specs = [IN_SMEM, IN_SMEM, IN_VMEM, ANYWHERE]
    args = [halo_count, halo_target, arrived, after]
    return small(place_kernel, [send] + [keep] * 4, args, "place", specs)


def join_kernel(*rest):
    *keeps, swapped = rest[: len(rest) // 2 + 1]
    for k, out in enumerate(rest[len(rest) // 2 + 1 :]):
        out[0] = keeps[k][...]
        out[1] = swapped[k + 1]


def self_kernel(pre_grad, weight, other_local, own_local, after, out, total):
    del after
    core, _, _ = whereabouts()
    width = own_local.shape[1]
    own = pl.ds(pl.multiple_of(core * width, width), width)
    other = pl.ds(pl.multiple_of((1 - core) * width, width), width)
    contract = (((1,), (1,)), ((), ()))
    weight_high, weight_low = split(weight[...])
    rows = out.shape[0] // 4
    for i in range(4):
        at = slice(i * rows, (i + 1) * rows)
        high, low = split(pre_grad[at])
        rows_of = lax.dot_general(high, weight_high, contract, preferred_element_type=F32)
        rows_of += lax.dot_general(high, weight_low, contract, preferred_element_type=F32)
        rows_of += lax.dot_general(low, weight_high, contract, preferred_element_type=F32)
        out[at] = rows_of
    for b in range(own_local.shape[0]):
        total[b, own] = own_local[b]
        total[b, other] = other_local[b]
        out[b * BLOCK : (b + 1) * BLOCK] += total[b].T


def finish_kernel(base, keep, swapped, *rest):
    *received, out, total, rows, sems = rest
    core, _, _ = whereabouts()
    chip = lax.axis_index("local") >> 1
    blocks, share, _ = keep.shape
    pieces = [keep, swapped.at[0]] + [some.at[k] for some in received for k in range(2)]
    copies = []
    for b in range(blocks):
        for k, some in enumerate(pieces):
            source = (chip - k // 2) & 3
            side = source >> 1
            quarter = side * 2 + ((source + side) & 1)
            first = core if k % 2 == 0 else 1 - core
            start = pl.multiple_of((first * 4 + quarter) * share, share)
            total[b, pl.ds(start, share)] = some[b]
        at = slice(b * BLOCK, (b + 1) * BLOCK)
        rows[at] = base[at] + total[b].T
        copy = pltpu.make_async_copy(rows.at[at], out.at[at], sems.at[b])
        copy.start()
        copies.append(copy)
    for copy in copies:
        copy.wait()


def finish(base, keep, swapped, received):
    node_rows, feat = base.shape
    blocks = keep.shape[0]
    return pl.pallas_call(
        finish_kernel,
        out_shape=jax.ShapeDtypeStruct(base.shape, F32),
        in_specs=[IN_VMEM] * (3 + len(received)),
        out_specs=ANYWHERE,
        scratch_shapes=[
            pltpu.VMEM((blocks, feat, BLOCK), F32),
            pltpu.VMEM((node_rows, feat), F32),
            pltpu.SemaphoreType.DMA((blocks,)),
        ],
        cost_estimate=pl.CostEstimate(
            flops=2 * base.size, bytes_accessed=16 * base.size, transcendentals=0
        ),
        compiler_params=limit(8),
        name="finish",
    )(base, keep, swapped, *received)


def on_device(
    features,
    aggregated,
    preact,
    grad_out,
    w_self,
    w_neigh,
    tile_vals,
    tile_col,
    halo_count,
    halo_target,
):
    high = lax.Precision.HIGH
    node_rows, width = features.shape
    blocks = node_rows // BLOCK
    groups = lax.axis_size("group")
    members = lax.axis_size("local")
    slot_count = halo_target.shape[1]
    dead = slot_count - MAIN
    swap = [(i, i ^ 1) for i in range(members)]
    pairs = [(i, i ^ 2) for i in range(members)]
    across = [(i, members - 2 - (i - i % 2) + i % 2) for i in range(members)]
    along_x = [[(i, (i + 2 * k) % members) for i in range(members)] for k in range(4)]
    along_y = [[(i, (i + 4 * k) % groups) for i in range(groups)] for k in range(4)]
    along_z = [[(i, i // 4 * 4 + (i + k) % 4) for i in range(groups)] for k in range(4)]

    pre_grad, other_local, send, places, column = tile_sums(
        tile_col, halo_count, w_neigh, tile_vals, MAIN, dead, preact=preact, grad_out=grad_out
    )
    recv = lax.ppermute(send, "local", swap)
    own_local, flag, keep_a, send_a, keep_b, send_b = tile_sums(
        column, halo_count, w_neigh, tile_vals, MAIN, dead, pre_grad=pre_grad, recv=recv
    )
    recv_a = lax.ppermute(send_a, "local", pairs)
    recv_b = lax.ppermute(send_b, "local", across)

    contract = (((0,), (0,)), ((), ()))
    self_term = lax.dot_general(
        features, pre_grad, contract, precision=high, preferred_element_type=F32
    )
    neigh_term = lax.dot_general(
        aggregated, pre_grad, contract, precision=high, preferred_element_type=F32
    )
    pieces = jax.ShapeDtypeStruct((groups, width // BLOCK, width // groups, BLOCK), F32)
    stay, leave = small(sort_kernel, [pieces] * 2, [self_term, neigh_term], "sort_terms")
    by_y = (4, groups // 4) + pieces.shape[1:]
    stay, leave = stay.reshape(by_y), lax.ppermute(leave, "local", swap).reshape(by_y)
    mine, *sends = scatter(lambda g: g >> 2, [stay, leave], "sum_cores", [flag])
    terms = [mine] + [
        lax.ppermute(some, "group", along_y[k + 1]) for k, some in enumerate(sends)
    ]
    mine, *sends = scatter(lambda g: g & 3, terms, "sum_y")
    terms = [mine] + [
        lax.ppermute(some, "group", along_z[k + 1]) for k, some in enumerate(sends)
    ]

    base = small(
        self_kernel,
        jax.ShapeDtypeStruct(pre_grad.shape, F32),
        [pre_grad, w_self, other_local, own_local, mine],
        "self_rows",
        [IN_VMEM] * 4 + [ANYWHERE],
        scratch=[pltpu.VMEM((blocks, width, BLOCK), F32)],
        mebibytes=16,
        flops=6 * pre_grad.size * width,
    )
    keep, send_a, send_b = second_sums(keep_a, recv_a, keep_b, recv_b, [base, terms[1]])
    recv_a = lax.ppermute(send_a, "local", across)
    recv_b = lax.ppermute(send_b, "local", pairs)
    share_shape = jax.ShapeDtypeStruct(mine.shape, F32)
    share = small(sum_kernel, share_shape, terms, "sum_z")
    terms = [share] + [lax.ppermute(share, "local", p) for p in (pairs, across, along_x[2])]
    scale = float(node_rows * groups * members) ** (-0.5)
    share = small(functools.partial(chips_kernel, scale), share_shape, terms, "sum_chips")
    shares = third_sums(places, keep, recv_a, recv_b, share)
    arrived = lax.all_to_all(shares, "group", split_axis=0, concat_axis=0, tiled=True)
    terms = [share] + [lax.ppermute(share, "group", along_z[k]) for k in range(1, 4)]
    row = gather(lambda g: g & 3, terms, "gather_z")

    send, *keeps = place(halo_count, halo_target, arrived, row, blocks)
    swapped = lax.ppermute(send, "local", swap)
    joined = jax.ShapeDtypeStruct((2,) + keeps[0].shape, F32)
    joined = small(join_kernel, [joined] * 3, [*keeps[1:], swapped], "join")
    received = [lax.ppermute(joined[k - 1], "local", along_x[k]) for k in range(1, 4)]

    row = small(
        pass_kernel,
        jax.ShapeDtypeStruct(row.shape, F32),
        [row, joined[0]],
        "pass",
        [IN_VMEM, ANYWHERE],
    )
    rows = [row] + [lax.ppermute(row, "group", along_y[k]) for k in range(1, 4)]
    whole = gather(lambda g: g >> 2, rows, "gather_y", received).reshape(pieces.shape)
    other = lax.ppermute(whole, "local", swap)
    square = jax.ShapeDtypeStruct(self_term.shape, F32)
    self_grad, neigh_grad = small(grads_kernel, [square] * 2, [whole, other], "sort_grads")

    node_grad = finish(base, keeps[0], swapped, received)
    return (node_grad, self_grad, neigh_grad)


def solution(mesh):
    in_specs = (
        P(("group", "local"), None),
        P(("group", "local"), None),
        P(("group", "local"), None),
        P(("group", "local"), None),
        P(),
        P(),
        P(("group", "local"), None, None),
        P(("group", "local")),
        P(),
        P(),
    )
    out_specs = (P(("group", "local"), None), P(), P())
    return jax.shard_map(
        on_device, mesh=mesh, in_specs=in_specs, out_specs=out_specs, check_vma=False
    )
```

```python
import functools

import jax
import jax.numpy as jnp
from jax import lax
from jax.experimental import pallas as pl
from jax.experimental.pallas import tpu as pltpu
from jax.sharding import PartitionSpec as P

F32 = jnp.float32
BF16 = jnp.bfloat16
BLOCK = 128
CHUNKS = 2
MAIN = 30
LIMIT_OTHER = 55
LIMIT_OWN = 20
LIMIT_SMALL = 6


def split(x):
    high = x.astype(BF16)
    low = (x - high.astype(F32)).astype(BF16)
    return high, low


def limit(mebibytes):
    return pltpu.CompilerParams(vmem_limit_bytes=mebibytes * 1024 * 1024)


def whereabouts():
    member = lax.axis_index("local")
    chip = member >> 1
    side = chip >> 1
    return member & 1, side, (chip + side) & 1


def slot_places(count_ref, places):
    slots = places.shape[0]
    owners = count_ref.shape[1]
    capacity = slots // owners
    group = lax.axis_index("group")

    def owner(o, carry):
        live, dead = carry
        count = count_ref[group, o]
        for j in range(capacity):
            is_live = j < count
            places[o * capacity + j] = jnp.where(is_live, live, slots - 1 - dead)
            live = live + is_live.astype(jnp.int32)
            dead = dead + 1 - is_live.astype(jnp.int32)
        return live, dead

    zero = jnp.int32(0)
    lax.fori_loop(0, owners, owner, (zero, zero))


def tile_kernel(own, blocks, main, over, col_ref, count_ref, *rest):
    if own:
        pre_hbm, weight_hbm, tiles_hbm, recv_ref, local_ref, flag_ref, *rest = rest
        keep_a, send_a, keep_b, send_b, pre, weight, tiles, sums, sems = rest
        column = col_ref
    else:
        pre_hbm, grad_hbm, weight_hbm, tiles_hbm, pre_ref, local_ref, send_ref, places, column, *rest = rest
        pre, grad, weight, tiles, sums, sems = rest
    width = weight.shape[0]
    rows = pre.shape[0] // CHUNKS
    count = tiles.shape[0] // CHUNKS
    core, p, q = whereabouts()
    half = core if own else 1 - core
    some = pl.ds(pl.multiple_of(half * width, width), width)
    weight_copy = pltpu.make_async_copy(weight_hbm.at[some], weight, sems.at[0])
    weight_copy.start()
    if own:
        flag_ref[0] = core
        main_sums = sums.at[pl.ds(blocks, main)]
        recv_copy = pltpu.make_async_copy(recv_ref, main_sums, sems.at[1])
        recv_copy.start()
    chunks = []
    for i in range(CHUNKS):
        at = pl.ds(i * rows, rows)
        copies = [pltpu.make_async_copy(pre_hbm.at[at], pre.at[at], sems.at[2 + 3 * i])]
        if not own:
            copies.append(pltpu.make_async_copy(grad_hbm.at[at], grad.at[at], sems.at[3 + 3 * i]))
        some_tiles = pl.ds(i * count, count)
        copies.append(
            pltpu.make_async_copy(tiles_hbm.at[some_tiles], tiles.at[some_tiles], sems.at[4 + 3 * i])
        )
        for copy in copies:
            copy.start()
        chunks.append(copies)
    sums[0:blocks] = jnp.zeros((blocks,) + sums.shape[1:], F32)
    sums[blocks + main :] = jnp.zeros((over,) + sums.shape[1:], F32)
    if not own:
        sums[blocks : blocks + main] = jnp.zeros((main,) + sums.shape[1:], F32)
    if not own:
        slot_places(count_ref, places)

        def place_tile(t, _):
            col = col_ref[t]
            slot = jnp.maximum(col - blocks, 0)
            column[t] = jnp.where(col < blocks, col, blocks + places[slot])
            return 0

        lax.fori_loop(0, tiles.shape[0], place_tile, 0)
    weight_copy.wait()
    weight_high, weight_low = split(weight[...])
    contract = (((1,), (1,)), ((), ()))
    pre_copies = []
    for i in range(CHUNKS):
        at = pl.ds(i * rows, rows)
        *copies, tiles_copy = chunks[i]
        for copy in copies:
            copy.wait()
        if own:
            pre_grad = pre[at]
        else:
            pre_grad = jnp.where(pre[at] > 0, grad[at], 0.0)
            grad[at] = pre_grad
            pre_copy = pltpu.make_async_copy(grad.at[at], pre_ref.at[at], sems.at[2 + 3 * i])
            pre_copy.start()
            pre_copies.append(pre_copy)
        pre_high, pre_low = split(pre_grad)
        part = lax.dot_general(weight_high, pre_high, contract, preferred_element_type=F32)
        part += lax.dot_general(weight_high, pre_low, contract, preferred_element_type=F32)
        part += lax.dot_general(weight_low, pre_high, contract, preferred_element_type=F32)
        row_high, row_low = split(part)
        tiles_copy.wait()
        if own and i == 0:
            recv_copy.wait()
        for r in range(rows // BLOCK):
            mine = slice(r * BLOCK, (r + 1) * BLOCK)
            high = row_high[:, mine]
            left = jnp.concatenate([high, high, row_low[:, mine]], axis=1)
            each = count * BLOCK // rows
            for k in range(0, each, 2):
                t = i * count + r * each + k
                first_high, first_low = split(tiles[t])
                next_high, next_low = split(tiles[t + 1])
                high = jnp.concatenate([first_high, next_high], axis=1)
                low = jnp.concatenate([first_low, next_low], axis=1)
                right = jnp.concatenate([high, low, high], axis=0)
                product = jnp.dot(left, right, preferred_element_type=F32)
                sums[column[t]] += product[:, :BLOCK]
                sums[column[t + 1]] += product[:, BLOCK:]

    copies = []

    def out(source, target):
        copy = pltpu.make_async_copy(source, target, sems.at[2 + 3 * CHUNKS + len(copies)])
        copy.start()
        copies.append(copy)

    if own:
        some = main // 2
        share = width // 4

        def piece(first, p_at, q_at, target):
            share_rows = pl.ds(pl.multiple_of((p_at * 2 + q_at) * share, share), share)
            out(sums.at[pl.ds(blocks + first, some), share_rows], target)

        for k in range(2):
            piece(0, k, 1 - q, send_a.at[k])
            piece(some, 1 - p, k, send_b.at[k])
        for k in range(2):
            piece(0, k, q, keep_a.at[k])
            piece(some, p, k, keep_b.at[k])
    else:
        out(sums.at[pl.ds(blocks, main)], send_ref)
    out(sums.at[pl.ds(0, blocks)], local_ref)
    for copy in pre_copies + copies:
        copy.wait()


def tile_sums(
    tile_col, halo_count, weight, tile_vals, main, over, preact=None, grad_out=None,
    pre_grad=None, recv=None,
):
    own = recv is not None
    node_rows, feat = (pre_grad if own else preact).shape
    width = weight.shape[0] // 2
    blocks = node_rows // BLOCK
    some = main // 2
    anywhere = pl.BlockSpec(memory_space=pl.ANY)
    local = jax.ShapeDtypeStruct((blocks, width, BLOCK), F32)
    piece = jax.ShapeDtypeStruct((2, some, width // 4, BLOCK), F32)
    if own:
        args = [pre_grad, weight, tile_vals, recv]
        flag = jax.ShapeDtypeStruct((1,), jnp.int32)
        out_shape = [local, flag] + [piece] * 4
    else:
        args = [preact, grad_out, weight, tile_vals]
        out_shape = [
            jax.ShapeDtypeStruct((node_rows, feat), F32),
            local,
            jax.ShapeDtypeStruct((main, width, BLOCK), F32),
            jax.ShapeDtypeStruct((main + over,), jnp.int32),
            jax.ShapeDtypeStruct(tile_col.shape, jnp.int32),
        ]
    scratch = [pltpu.VMEM((node_rows, feat), F32)]
    if not own:
        scratch.append(pltpu.VMEM((node_rows, feat), F32))
    scratch += [
        pltpu.VMEM((width, feat), F32),
        pltpu.VMEM(tile_vals.shape, F32),
        pltpu.VMEM((blocks + main + over, width, BLOCK), F32),
        pltpu.SemaphoreType.DMA((2 + 3 * CHUNKS + 10,)),
    ]
    return pl.pallas_call(
        functools.partial(tile_kernel, own, blocks, main, over),
        out_shape=out_shape,
        in_specs=[pl.BlockSpec(memory_space=pltpu.SMEM)] * 2 + [anywhere] * len(args),
        out_specs=[
            pl.BlockSpec(memory_space=pltpu.SMEM) if x.dtype == jnp.int32 else anywhere
            for x in out_shape
        ],
        scratch_shapes=scratch,
        compiler_params=limit(LIMIT_OWN if own else LIMIT_OTHER),
        cost_estimate=pl.CostEstimate(
            flops=6 * (tile_vals.size + node_rows * feat) * width,
            bytes_accessed=14 * 1024 * 1024,
            transcendentals=0,
        ),
        name="own_tile_sums" if own else "other_tile_sums",
    )(tile_col, halo_count, *args)


IN_VMEM = pl.BlockSpec(memory_space=pltpu.VMEM)
IN_SMEM = pl.BlockSpec(memory_space=pltpu.SMEM)
ANYWHERE = pl.BlockSpec(memory_space=pl.ANY)


def second_kernel(keep_a, recv_a, keep_b, recv_b, *rest):
    keep, send_a, send_b = rest[-3:]
    _, p, q = whereabouts()
    send_a[...] = keep_a[1 - p] + recv_a[1 - p]
    send_b[...] = keep_b[1 - q] + recv_b[1 - q]
    keep[0] = keep_a[p] + recv_a[p]
    keep[1] = keep_b[q] + recv_b[q]


def second_sums(keep_a, recv_a, keep_b, recv_b, after):
    send = jax.ShapeDtypeStruct(keep_a.shape[1:], F32)
    out_shape = [jax.ShapeDtypeStruct(keep_a.shape, F32), send, send]
    return small(
        second_kernel,
        out_shape,
        [keep_a, recv_a, keep_b, recv_b, *after],
        "second_sums",
        [IN_VMEM] * 4 + [ANYWHERE] * len(after),
    )


def third_kernel(places, keep, recv_a, recv_b, *rest):
    out, total = rest[-2:]
    half = recv_a.shape[0]
    main = 2 * half
    total[0:half] = keep[0] + recv_a[...]
    total[half:main] = keep[1] + recv_b[...]
    total[main:] = jnp.zeros_like(total[main:])
    for slot in range(out.shape[0]):
        out[slot] = total[places[slot]]


def third_sums(places, keep, recv_a, recv_b, after):
    shape = (places.shape[0],) + keep.shape[2:]
    return small(
        third_kernel,
        jax.ShapeDtypeStruct(shape, F32),
        [places, keep, recv_a, recv_b, *after],
        "third_sums",
        [IN_SMEM] + [IN_VMEM] * 3 + [ANYWHERE] * len(after),
        scratch=[pltpu.VMEM(shape, F32)],
    )


def small(
    kernel, out_shape, args, name, specs=None, scratch=(), mebibytes=LIMIT_SMALL, flops=None
):
    size = max(x.size for x in args)
    return pl.pallas_call(
        kernel,
        out_shape=out_shape,
        in_specs=specs or [IN_VMEM] * len(args),
        out_specs=jax.tree.map(lambda _: IN_VMEM, out_shape),
        scratch_shapes=scratch,
        cost_estimate=pl.CostEstimate(
            flops=flops or size, bytes_accessed=12 * size, transcendentals=0
        ),
        compiler_params=limit(mebibytes),
        name=name,
    )(*args)


def sort_kernel(self_term, neigh_term, keep, send):
    core, _, _ = whereabouts()
    pieces, columns, rows, _ = keep.shape

    def copy(source, target):
        for g in range(pieces):
            for c in range(columns):
                some = (slice(g * rows, (g + 1) * rows), slice(c * BLOCK, (c + 1) * BLOCK))
                target[g, c] = source[some]

    @pl.when(core == 0)
    def _():
        copy(self_term, keep)
        copy(neigh_term, send)

    @pl.when(core != 0)
    def _():
        copy(neigh_term, keep)
        copy(self_term, send)


def grads_kernel(whole, other, self_grad, neigh_grad):
    core, _, _ = whereabouts()
    pieces, columns, rows, _ = whole.shape

    def copy(source, target):
        for g in range(pieces):
            for c in range(columns):
                some = (slice(g * rows, (g + 1) * rows), slice(c * BLOCK, (c + 1) * BLOCK))
                target[some] = source[g, c]

    @pl.when(core == 0)
    def _():
        copy(whole, self_grad)
        copy(other, neigh_grad)

    @pl.when(core != 0)
    def _():
        copy(other, self_grad)
        copy(whole, neigh_grad)


def scatter_kernel(axis_of, count, *rest):
    terms = rest[:count]
    outs = rest[-4:]
    me = axis_of(lax.axis_index("group"))
    for away, out in enumerate(outs):
        at = (me + away) & 3
        total = terms[0][at]
        for term in terms[1:]:
            total += term[at]
        out[...] = total


def scatter(axis_of, terms, name, after=()):
    piece = jax.ShapeDtypeStruct(terms[0].shape[1:], F32)
    return small(
        functools.partial(scatter_kernel, axis_of, len(terms)),
        [piece] * 4,
        [*terms, *after],
        name,
        [IN_VMEM] * len(terms) + [IN_SMEM] * len(after),
    )


def sum_kernel(*rest):
    *terms, out = rest
    total = terms[0][...]
    for term in terms[1:]:
        total += term[...]
    out[...] = total


def chips_kernel(scale, mine, pair, far_one, far_two, out):
    out[...] = ((mine[...] + pair[...]) + (far_one[...] + far_two[...])) * scale


def pass_kernel(value, *rest):
    rest[-1][...] = value[...]


def gather_kernel(axis_of, *rest):
    pieces = rest[:4]
    out = rest[-1]
    me = axis_of(lax.axis_index("group"))
    for away, piece in enumerate(pieces):
        out[(me - away) & 3] = piece[...]


def gather(axis_of, pieces, name, after=()):
    whole = jax.ShapeDtypeStruct((4,) + pieces[0].shape, F32)
    specs = [IN_VMEM] * 4 + [ANYWHERE] * len(after)
    return small(functools.partial(gather_kernel, axis_of), whole, [*pieces, *after], name, specs)


def place_kernel(count_ref, target_ref, arrived, after, send, *keeps):
    del after
    core, _, _ = whereabouts()
    chip = lax.axis_index("local") >> 1
    group = lax.axis_index("group")
    sources = count_ref.shape[0]
    capacity = arrived.shape[0] // sources
    blocks = send.shape[1]
    shift = blocks.bit_length() - 1
    for out in (send, *keeps):
        out[...] = jnp.zeros_like(out)

    @pl.loop(0, sources)
    def _(source):
        count = count_ref[source, group]
        for j in range(capacity):
            target = target_ref[source, group * capacity + j]
            member = lax.shift_right_logical(target, shift)
            block = target & (blocks - 1)
            away = (lax.shift_right_logical(member, 1) - chip) & 3
            mine = (member & 1) == core

            @pl.when(j < count)
            def _():
                @pl.when(jnp.logical_not(mine))
                def _():
                    send[away, block] += arrived[source * capacity + j]

                @pl.when(mine)
                def _():
                    for k, keep in enumerate(keeps):

                        @pl.when(away == k)
                        def _():
                            keep[block] += arrived[source * capacity + j]


def place(halo_count, halo_target, arrived, after, blocks):
    keep = jax.ShapeDtypeStruct((blocks,) + arrived.shape[1:], F32)
    send = jax.ShapeDtypeStruct((4,) + keep.shape, F32)
    specs = [IN_SMEM, IN_SMEM, IN_VMEM, ANYWHERE]
    args = [halo_count, halo_target, arrived, after]
    return small(place_kernel, [send] + [keep] * 4, args, "place", specs)


def join_kernel(*rest):
    *keeps, swapped = rest[: len(rest) // 2 + 1]
    for k, out in enumerate(rest[len(rest) // 2 + 1 :]):
        out[0] = keeps[k][...]
        out[1] = swapped[k + 1]


def self_kernel(pre_grad, weight, other_local, own_local, after, out, total):
    del after
    core, _, _ = whereabouts()
    width = own_local.shape[1]
    own = pl.ds(pl.multiple_of(core * width, width), width)
    other = pl.ds(pl.multiple_of((1 - core) * width, width), width)
    contract = (((1,), (1,)), ((), ()))
    weight_high, weight_low = split(weight[...])
    rows = out.shape[0] // 4
    for i in range(4):
        at = slice(i * rows, (i + 1) * rows)
        high, low = split(pre_grad[at])
        rows_of = lax.dot_general(high, weight_high, contract, preferred_element_type=F32)
        rows_of += lax.dot_general(high, weight_low, contract, preferred_element_type=F32)
        rows_of += lax.dot_general(low, weight_high, contract, preferred_element_type=F32)
        out[at] = rows_of
    for b in range(own_local.shape[0]):
        total[b, own] = own_local[b]
        total[b, other] = other_local[b]
        out[b * BLOCK : (b + 1) * BLOCK] += total[b].T


def finish_kernel(base, keep, swapped, *rest):
    *received, out, total, rows, sems = rest
    core, _, _ = whereabouts()
    chip = lax.axis_index("local") >> 1
    blocks, share, _ = keep.shape
    pieces = [keep, swapped.at[0]] + [some.at[k] for some in received for k in range(2)]
    copies = []
    for b in range(blocks):
        for k, some in enumerate(pieces):
            source = (chip - k // 2) & 3
            side = source >> 1
            quarter = side * 2 + ((source + side) & 1)
            first = core if k % 2 == 0 else 1 - core
            start = pl.multiple_of((first * 4 + quarter) * share, share)
            total[b, pl.ds(start, share)] = some[b]
        at = slice(b * BLOCK, (b + 1) * BLOCK)
        rows[at] = base[at] + total[b].T
        copy = pltpu.make_async_copy(rows.at[at], out.at[at], sems.at[b])
        copy.start()
        copies.append(copy)
    for copy in copies:
        copy.wait()


def finish(base, keep, swapped, received):
    node_rows, feat = base.shape
    blocks = keep.shape[0]
    return pl.pallas_call(
        finish_kernel,
        out_shape=jax.ShapeDtypeStruct(base.shape, F32),
        in_specs=[IN_VMEM] * (3 + len(received)),
        out_specs=ANYWHERE,
        scratch_shapes=[
            pltpu.VMEM((blocks, feat, BLOCK), F32),
            pltpu.VMEM((node_rows, feat), F32),
            pltpu.SemaphoreType.DMA((blocks,)),
        ],
        cost_estimate=pl.CostEstimate(
            flops=2 * base.size, bytes_accessed=16 * base.size, transcendentals=0
        ),
        compiler_params=limit(8),
        name="finish",
    )(base, keep, swapped, *received)


def on_device(
    features,
    aggregated,
    preact,
    grad_out,
    w_self,
    w_neigh,
    tile_vals,
    tile_col,
    halo_count,
    halo_target,
):
    high = lax.Precision.HIGH
    node_rows, width = features.shape
    blocks = node_rows // BLOCK
    groups = lax.axis_size("group")
    members = lax.axis_size("local")
    slot_count = halo_target.shape[1]
    dead = slot_count - MAIN
    swap = [(i, i ^ 1) for i in range(members)]
    pairs = [(i, i ^ 2) for i in range(members)]
    across = [(i, members - 2 - (i - i % 2) + i % 2) for i in range(members)]
    along_x = [[(i, (i + 2 * k) % members) for i in range(members)] for k in range(4)]
    along_y = [[(i, (i + 4 * k) % groups) for i in range(groups)] for k in range(4)]
    along_z = [[(i, i // 4 * 4 + (i + k) % 4) for i in range(groups)] for k in range(4)]

    pre_grad, other_local, send, places, column = tile_sums(
        tile_col, halo_count, w_neigh, tile_vals, MAIN, dead, preact=preact, grad_out=grad_out
    )
    recv = lax.ppermute(send, "local", swap)
    own_local, flag, keep_a, send_a, keep_b, send_b = tile_sums(
        column, halo_count, w_neigh, tile_vals, MAIN, dead, pre_grad=pre_grad, recv=recv
    )
    recv_a = lax.ppermute(send_a, "local", pairs)
    recv_b = lax.ppermute(send_b, "local", across)

    contract = (((0,), (0,)), ((), ()))
    self_term = lax.dot_general(
        features, pre_grad, contract, precision=high, preferred_element_type=F32
    )
    neigh_term = lax.dot_general(
        aggregated, pre_grad, contract, precision=high, preferred_element_type=F32
    )
    pieces = jax.ShapeDtypeStruct((groups, width // BLOCK, width // groups, BLOCK), F32)
    stay, leave = small(sort_kernel, [pieces] * 2, [self_term, neigh_term], "sort_terms")
    by_y = (4, groups // 4) + pieces.shape[1:]
    stay, leave = stay.reshape(by_y), lax.ppermute(leave, "local", swap).reshape(by_y)
    mine, *sends = scatter(lambda g: g >> 2, [stay, leave], "sum_cores", [flag])
    terms = [mine] + [
        lax.ppermute(some, "group", along_y[k + 1]) for k, some in enumerate(sends)
    ]
    mine, *sends = scatter(lambda g: g & 3, terms, "sum_y")
    terms = [mine] + [
        lax.ppermute(some, "group", along_z[k + 1]) for k, some in enumerate(sends)
    ]

    keep, send_a, send_b = second_sums(keep_a, recv_a, keep_b, recv_b, terms[1:])
    recv_a = lax.ppermute(send_a, "local", across)
    recv_b = lax.ppermute(send_b, "local", pairs)
    base = small(
        self_kernel,
        jax.ShapeDtypeStruct(pre_grad.shape, F32),
        [pre_grad, w_self, other_local, own_local, keep],
        "self_rows",
        [IN_VMEM] * 4 + [ANYWHERE],
        scratch=[pltpu.VMEM((blocks, width, BLOCK), F32)],
        mebibytes=16,
        flops=6 * pre_grad.size * width,
    )
    share_shape = jax.ShapeDtypeStruct(mine.shape, F32)
    share = small(sum_kernel, share_shape, terms, "sum_z")
    terms = [share] + [lax.ppermute(share, "local", p) for p in (pairs, across, along_x[2])]
    scale = float(node_rows * groups * members) ** (-0.5)
    share = small(functools.partial(chips_kernel, scale), share_shape, terms, "sum_chips")
    shares = third_sums(places, keep, recv_a, recv_b, [share, base])
    arrived = lax.all_to_all(shares, "group", split_axis=0, concat_axis=0, tiled=True)
    terms = [share] + [lax.ppermute(share, "group", along_z[k]) for k in range(1, 4)]
    row = gather(lambda g: g & 3, terms, "gather_z")

    send, *keeps = place(halo_count, halo_target, arrived, row, blocks)
    swapped = lax.ppermute(send, "local", swap)
    joined = jax.ShapeDtypeStruct((2,) + keeps[0].shape, F32)
    joined = small(join_kernel, [joined] * 3, [*keeps[1:], swapped], "join")
    received = [lax.ppermute(joined[k - 1], "local", along_x[k]) for k in range(1, 4)]

    row = small(
        pass_kernel,
        jax.ShapeDtypeStruct(row.shape, F32),
        [row, joined[0]],
        "pass",
        [IN_VMEM, ANYWHERE],
    )
    rows = [row] + [lax.ppermute(row, "group", along_y[k]) for k in range(1, 4)]
    whole = gather(lambda g: g >> 2, rows, "gather_y", received).reshape(pieces.shape)
    other = lax.ppermute(whole, "local", swap)
    square = jax.ShapeDtypeStruct(self_term.shape, F32)
    self_grad, neigh_grad = small(grads_kernel, [square] * 2, [whole, other], "sort_grads")

    node_grad = finish(base, keeps[0], swapped, received)
    return (node_grad, self_grad, neigh_grad)


def solution(mesh):
    in_specs = (
        P(("group", "local"), None),
        P(("group", "local"), None),
        P(("group", "local"), None),
        P(("group", "local"), None),
        P(),
        P(),
        P(("group", "local"), None, None),
        P(("group", "local")),
        P(),
        P(),
    )
    out_specs = (P(("group", "local"), None), P(), P())
    return jax.shard_map(
        on_device, mesh=mesh, in_specs=in_specs, out_specs=out_specs, check_vma=False
    )
```

```python
import functools

import jax
import jax.numpy as jnp
from jax import lax
from jax.experimental import pallas as pl
from jax.experimental.pallas import tpu as pltpu
from jax.sharding import PartitionSpec as P

F32 = jnp.float32
BF16 = jnp.bfloat16
BLOCK = 128
CHUNKS = 2
MAINS = (24, 30)
LIMIT_OTHER = 55
LIMIT_OWN = 20
LIMIT_SMALL = 6


def split(x):
    high = x.astype(BF16)
    low = (x - high.astype(F32)).astype(BF16)
    return high, low


def limit(mebibytes):
    return pltpu.CompilerParams(vmem_limit_bytes=mebibytes * 1024 * 1024)


def whereabouts():
    member = lax.axis_index("local")
    chip = member >> 1
    side = chip >> 1
    return member & 1, side, (chip + side) & 1


def slot_places(count_ref, places):
    slots = places.shape[0]
    owners = count_ref.shape[1]
    capacity = slots // owners
    group = lax.axis_index("group")

    def owner(o, carry):
        live, dead = carry
        count = count_ref[group, o]
        for j in range(capacity):
            is_live = j < count
            places[o * capacity + j] = jnp.where(is_live, live, slots - 1 - dead)
            live = live + is_live.astype(jnp.int32)
            dead = dead + 1 - is_live.astype(jnp.int32)
        return live, dead

    zero = jnp.int32(0)
    lax.fori_loop(0, owners, owner, (zero, zero))


def tile_kernel(own, blocks, main, over, col_ref, count_ref, *rest):
    if own:
        pre_hbm, weight_hbm, tiles_hbm, recv_ref, local_ref, flag_ref, *rest = rest
        keep_a, send_a, keep_b, send_b, pre, weight, tiles, sums, sems = rest
        column = col_ref
    else:
        pre_hbm, grad_hbm, weight_hbm, tiles_hbm, pre_ref, local_ref, send_ref, places, column, *rest = rest
        pre, grad, weight, tiles, sums, sems = rest
    width = weight.shape[0]
    rows = pre.shape[0] // CHUNKS
    count = tiles.shape[0] // CHUNKS
    core, p, q = whereabouts()
    half = core if own else 1 - core
    some = pl.ds(pl.multiple_of(half * width, width), width)
    weight_copy = pltpu.make_async_copy(weight_hbm.at[some], weight, sems.at[0])
    weight_copy.start()
    if own:
        flag_ref[0] = core
        main_sums = sums.at[pl.ds(blocks, main)]
        recv_copy = pltpu.make_async_copy(recv_ref, main_sums, sems.at[1])
        recv_copy.start()
    chunks = []
    for i in range(CHUNKS):
        at = pl.ds(i * rows, rows)
        copies = [pltpu.make_async_copy(pre_hbm.at[at], pre.at[at], sems.at[2 + 3 * i])]
        if not own:
            copies.append(pltpu.make_async_copy(grad_hbm.at[at], grad.at[at], sems.at[3 + 3 * i]))
        some_tiles = pl.ds(i * count, count)
        copies.append(
            pltpu.make_async_copy(tiles_hbm.at[some_tiles], tiles.at[some_tiles], sems.at[4 + 3 * i])
        )
        for copy in copies:
            copy.start()
        chunks.append(copies)
    sums[0:blocks] = jnp.zeros((blocks,) + sums.shape[1:], F32)
    sums[blocks + main :] = jnp.zeros((over,) + sums.shape[1:], F32)
    if not own:
        sums[blocks : blocks + main] = jnp.zeros((main,) + sums.shape[1:], F32)
    if not own:
        slot_places(count_ref, places)

        def place_tile(t, _):
            col = col_ref[t]
            slot = jnp.maximum(col - blocks, 0)
            column[t] = jnp.where(col < blocks, col, blocks + places[slot])
            return 0

        lax.fori_loop(0, tiles.shape[0], place_tile, 0)
    weight_copy.wait()
    weight_high, weight_low = split(weight[...])
    contract = (((1,), (1,)), ((), ()))
    pre_copies = []
    for i in range(CHUNKS):
        at = pl.ds(i * rows, rows)
        *copies, tiles_copy = chunks[i]
        for copy in copies:
            copy.wait()
        if own:
            pre_grad = pre[at]
        else:
            pre_grad = jnp.where(pre[at] > 0, grad[at], 0.0)
            grad[at] = pre_grad
            pre_copy = pltpu.make_async_copy(grad.at[at], pre_ref.at[at], sems.at[2 + 3 * i])
            pre_copy.start()
            pre_copies.append(pre_copy)
        pre_high, pre_low = split(pre_grad)
        part = lax.dot_general(weight_high, pre_high, contract, preferred_element_type=F32)
        part += lax.dot_general(weight_high, pre_low, contract, preferred_element_type=F32)
        part += lax.dot_general(weight_low, pre_high, contract, preferred_element_type=F32)
        row_high, row_low = split(part)
        tiles_copy.wait()
        if own and i == 0:
            recv_copy.wait()
        for r in range(rows // BLOCK):
            mine = slice(r * BLOCK, (r + 1) * BLOCK)
            high = row_high[:, mine]
            left = jnp.concatenate([high, high, row_low[:, mine]], axis=1)
            each = count * BLOCK // rows
            for k in range(0, each, 2):
                t = i * count + r * each + k
                first_high, first_low = split(tiles[t])
                next_high, next_low = split(tiles[t + 1])
                high = jnp.concatenate([first_high, next_high], axis=1)
                low = jnp.concatenate([first_low, next_low], axis=1)
                right = jnp.concatenate([high, low, high], axis=0)
                product = jnp.dot(left, right, preferred_element_type=F32)
                sums[column[t]] += product[:, :BLOCK]
                sums[column[t + 1]] += product[:, BLOCK:]

    copies = []

    def out(source, target):
        copy = pltpu.make_async_copy(source, target, sems.at[2 + 3 * CHUNKS + len(copies)])
        copy.start()
        copies.append(copy)

    if own:
        some = main // 2
        share = width // 4

        def piece(first, p_at, q_at, target):
            share_rows = pl.ds(pl.multiple_of((p_at * 2 + q_at) * share, share), share)
            out(sums.at[pl.ds(blocks + first, some), share_rows], target)

        for k in range(2):
            piece(0, k, 1 - q, send_a.at[k])
            piece(some, 1 - p, k, send_b.at[k])
        for k in range(2):
            piece(0, k, q, keep_a.at[k])
            piece(some, p, k, keep_b.at[k])
    else:
        out(sums.at[pl.ds(blocks, main)], send_ref)
    out(sums.at[pl.ds(0, blocks)], local_ref)
    for copy in pre_copies + copies:
        copy.wait()


def tile_sums(
    tile_col, halo_count, weight, tile_vals, main, over, preact=None, grad_out=None,
    pre_grad=None, recv=None,
):
    own = recv is not None
    node_rows, feat = (pre_grad if own else preact).shape
    width = weight.shape[0] // 2
    blocks = node_rows // BLOCK
    some = main // 2
    anywhere = pl.BlockSpec(memory_space=pl.ANY)
    local = jax.ShapeDtypeStruct((blocks, width, BLOCK), F32)
    piece = jax.ShapeDtypeStruct((2, some, width // 4, BLOCK), F32)
    if own:
        args = [pre_grad, weight, tile_vals, recv]
        flag = jax.ShapeDtypeStruct((1,), jnp.int32)
        out_shape = [local, flag] + [piece] * 4
    else:
        args = [preact, grad_out, weight, tile_vals]
        out_shape = [
            jax.ShapeDtypeStruct((node_rows, feat), F32),
            local,
            jax.ShapeDtypeStruct((main, width, BLOCK), F32),
            jax.ShapeDtypeStruct((main + over,), jnp.int32),
            jax.ShapeDtypeStruct(tile_col.shape, jnp.int32),
        ]
    scratch = [pltpu.VMEM((node_rows, feat), F32)]
    if not own:
        scratch.append(pltpu.VMEM((node_rows, feat), F32))
    scratch += [
        pltpu.VMEM((width, feat), F32),
        pltpu.VMEM(tile_vals.shape, F32),
        pltpu.VMEM((blocks + main + over, width, BLOCK), F32),
        pltpu.SemaphoreType.DMA((2 + 3 * CHUNKS + 10,)),
    ]
    return pl.pallas_call(
        functools.partial(tile_kernel, own, blocks, main, over),
        out_shape=out_shape,
        in_specs=[pl.BlockSpec(memory_space=pltpu.SMEM)] * 2 + [anywhere] * len(args),
        out_specs=[
            pl.BlockSpec(memory_space=pltpu.SMEM) if x.dtype == jnp.int32 else anywhere
            for x in out_shape
        ],
        scratch_shapes=scratch,
        compiler_params=limit(LIMIT_OWN if own else LIMIT_OTHER),
        cost_estimate=pl.CostEstimate(
            flops=6 * (tile_vals.size + node_rows * feat) * width,
            bytes_accessed=14 * 1024 * 1024,
            transcendentals=0,
        ),
        name="own_tile_sums" if own else "other_tile_sums",
    )(tile_col, halo_count, *args)


IN_VMEM = pl.BlockSpec(memory_space=pltpu.VMEM)
IN_SMEM = pl.BlockSpec(memory_space=pltpu.SMEM)
ANYWHERE = pl.BlockSpec(memory_space=pl.ANY)


def second_kernel(keep_a, recv_a, keep_b, recv_b, *rest):
    keep, send_a, send_b = rest[-3:]
    _, p, q = whereabouts()
    send_a[...] = keep_a[1 - p] + recv_a[1 - p]
    send_b[...] = keep_b[1 - q] + recv_b[1 - q]
    keep[0] = keep_a[p] + recv_a[p]
    keep[1] = keep_b[q] + recv_b[q]


def second_sums(keep_a, recv_a, keep_b, recv_b, after):
    send = jax.ShapeDtypeStruct(keep_a.shape[1:], F32)
    out_shape = [jax.ShapeDtypeStruct(keep_a.shape, F32), send, send]
    return small(
        second_kernel,
        out_shape,
        [keep_a, recv_a, keep_b, recv_b, *after],
        "second_sums",
        [IN_VMEM] * 4 + [ANYWHERE] * len(after),
    )


def third_kernel(places, keep, recv_a, recv_b, after, out, total):
    del after
    half = recv_a.shape[0]
    main = 2 * half
    total[0:half] = keep[0] + recv_a[...]
    total[half:main] = keep[1] + recv_b[...]
    total[main:] = jnp.zeros_like(total[main:])
    for slot in range(out.shape[0]):
        out[slot] = total[places[slot]]


def third_sums(places, keep, recv_a, recv_b, after):
    shape = (places.shape[0],) + keep.shape[2:]
    return small(
        third_kernel,
        jax.ShapeDtypeStruct(shape, F32),
        [places, keep, recv_a, recv_b, after],
        "third_sums",
        [IN_SMEM] + [IN_VMEM] * 3 + [ANYWHERE],
        scratch=[pltpu.VMEM(shape, F32)],
    )


def small(
    kernel, out_shape, args, name, specs=None, scratch=(), mebibytes=LIMIT_SMALL, flops=None
):
    size = max(x.size for x in args)
    return pl.pallas_call(
        kernel,
        out_shape=out_shape,
        in_specs=specs or [IN_VMEM] * len(args),
        out_specs=jax.tree.map(lambda _: IN_VMEM, out_shape),
        scratch_shapes=scratch,
        cost_estimate=pl.CostEstimate(
            flops=flops or size, bytes_accessed=12 * size, transcendentals=0
        ),
        compiler_params=limit(mebibytes),
        name=name,
    )(*args)


def sort_kernel(self_term, neigh_term, keep, send):
    core, _, _ = whereabouts()
    pieces, columns, rows, _ = keep.shape

    def copy(source, target):
        for g in range(pieces):
            for c in range(columns):
                some = (slice(g * rows, (g + 1) * rows), slice(c * BLOCK, (c + 1) * BLOCK))
                target[g, c] = source[some]

    @pl.when(core == 0)
    def _():
        copy(self_term, keep)
        copy(neigh_term, send)

    @pl.when(core != 0)
    def _():
        copy(neigh_term, keep)
        copy(self_term, send)


def grads_kernel(whole, other, self_grad, neigh_grad):
    core, _, _ = whereabouts()
    pieces, columns, rows, _ = whole.shape

    def copy(source, target):
        for g in range(pieces):
            for c in range(columns):
                some = (slice(g * rows, (g + 1) * rows), slice(c * BLOCK, (c + 1) * BLOCK))
                target[some] = source[g, c]

    @pl.when(core == 0)
    def _():
        copy(whole, self_grad)
        copy(other, neigh_grad)

    @pl.when(core != 0)
    def _():
        copy(other, self_grad)
        copy(whole, neigh_grad)


def scatter_kernel(axis_of, count, *rest):
    terms = rest[:count]
    outs = rest[-4:]
    me = axis_of(lax.axis_index("group"))
    for away, out in enumerate(outs):
        at = (me + away) & 3
        total = terms[0][at]
        for term in terms[1:]:
            total += term[at]
        out[...] = total


def scatter(axis_of, terms, name, after=()):
    piece = jax.ShapeDtypeStruct(terms[0].shape[1:], F32)
    return small(
        functools.partial(scatter_kernel, axis_of, len(terms)),
        [piece] * 4,
        [*terms, *after],
        name,
        [IN_VMEM] * len(terms) + [IN_SMEM] * len(after),
    )


def sum_kernel(*rest):
    *terms, out = rest
    total = terms[0][...]
    for term in terms[1:]:
        total += term[...]
    out[...] = total


def chips_kernel(scale, mine, pair, far_one, far_two, out):
    out[...] = ((mine[...] + pair[...]) + (far_one[...] + far_two[...])) * scale


def pass_kernel(value, *rest):
    rest[-1][...] = value[...]


def gather_kernel(axis_of, *rest):
    pieces = rest[:4]
    out = rest[-1]
    me = axis_of(lax.axis_index("group"))
    for away, piece in enumerate(pieces):
        out[(me - away) & 3] = piece[...]


def gather(axis_of, pieces, name, after=()):
    whole = jax.ShapeDtypeStruct((4,) + pieces[0].shape, F32)
    specs = [IN_VMEM] * 4 + [ANYWHERE] * len(after)
    return small(functools.partial(gather_kernel, axis_of), whole, [*pieces, *after], name, specs)


def place_kernel(count_ref, target_ref, arrived, after, send, *keeps):
    del after
    core, _, _ = whereabouts()
    chip = lax.axis_index("local") >> 1
    group = lax.axis_index("group")
    sources = count_ref.shape[0]
    capacity = arrived.shape[0] // sources
    blocks = send.shape[1]
    shift = blocks.bit_length() - 1
    for out in (send, *keeps):
        out[...] = jnp.zeros_like(out)

    @pl.loop(0, sources)
    def _(source):
        count = count_ref[source, group]
        for j in range(capacity):
            target = target_ref[source, group * capacity + j]
            member = lax.shift_right_logical(target, shift)
            block = target & (blocks - 1)
            away = (lax.shift_right_logical(member, 1) - chip) & 3
            mine = (member & 1) == core

            @pl.when(j < count)
            def _():
                @pl.when(jnp.logical_not(mine))
                def _():
                    send[away, block] += arrived[source * capacity + j]

                @pl.when(mine)
                def _():
                    for k, keep in enumerate(keeps):

                        @pl.when(away == k)
                        def _():
                            keep[block] += arrived[source * capacity + j]


def place(halo_count, halo_target, arrived, after, blocks):
    keep = jax.ShapeDtypeStruct((blocks,) + arrived.shape[1:], F32)
    send = jax.ShapeDtypeStruct((4,) + keep.shape, F32)
    specs = [IN_SMEM, IN_SMEM, IN_VMEM, ANYWHERE]
    args = [halo_count, halo_target, arrived, after]
    return small(place_kernel, [send] + [keep] * 4, args, "place", specs)


def join_kernel(*rest):
    *keeps, swapped = rest[: len(rest) // 2 + 1]
    for k, out in enumerate(rest[len(rest) // 2 + 1 :]):
        out[0] = keeps[k][...]
        out[1] = swapped[k + 1]


def self_kernel(pre_grad, weight, other_local, own_local, after, out, total):
    del after
    core, _, _ = whereabouts()
    width = own_local.shape[1]
    own = pl.ds(pl.multiple_of(core * width, width), width)
    other = pl.ds(pl.multiple_of((1 - core) * width, width), width)
    contract = (((1,), (1,)), ((), ()))
    weight_high, weight_low = split(weight[...])
    rows = out.shape[0] // 4
    for i in range(4):
        at = slice(i * rows, (i + 1) * rows)
        high, low = split(pre_grad[at])
        rows_of = lax.dot_general(high, weight_high, contract, preferred_element_type=F32)
        rows_of += lax.dot_general(high, weight_low, contract, preferred_element_type=F32)
        rows_of += lax.dot_general(low, weight_high, contract, preferred_element_type=F32)
        out[at] = rows_of
    for b in range(own_local.shape[0]):
        total[b, own] = own_local[b]
        total[b, other] = other_local[b]
        out[b * BLOCK : (b + 1) * BLOCK] += total[b].T


def finish_kernel(base, keep, swapped, *rest):
    *received, out, total, rows, sems = rest
    core, _, _ = whereabouts()
    chip = lax.axis_index("local") >> 1
    blocks, share, _ = keep.shape
    pieces = [keep, swapped.at[0]] + [some.at[k] for some in received for k in range(2)]
    copies = []
    for b in range(blocks):
        for k, some in enumerate(pieces):
            source = (chip - k // 2) & 3
            side = source >> 1
            quarter = side * 2 + ((source + side) & 1)
            first = core if k % 2 == 0 else 1 - core
            start = pl.multiple_of((first * 4 + quarter) * share, share)
            total[b, pl.ds(start, share)] = some[b]
        at = slice(b * BLOCK, (b + 1) * BLOCK)
        rows[at] = base[at] + total[b].T
        copy = pltpu.make_async_copy(rows.at[at], out.at[at], sems.at[b])
        copy.start()
        copies.append(copy)
    for copy in copies:
        copy.wait()


def finish(base, keep, swapped, received):
    node_rows, feat = base.shape
    blocks = keep.shape[0]
    return pl.pallas_call(
        finish_kernel,
        out_shape=jax.ShapeDtypeStruct(base.shape, F32),
        in_specs=[IN_VMEM] * (3 + len(received)),
        out_specs=ANYWHERE,
        scratch_shapes=[
            pltpu.VMEM((blocks, feat, BLOCK), F32),
            pltpu.VMEM((node_rows, feat), F32),
            pltpu.SemaphoreType.DMA((blocks,)),
        ],
        cost_estimate=pl.CostEstimate(
            flops=2 * base.size, bytes_accessed=16 * base.size, transcendentals=0
        ),
        compiler_params=limit(8),
        name="finish",
    )(base, keep, swapped, *received)


def body(
    main,
    features,
    aggregated,
    preact,
    grad_out,
    w_self,
    w_neigh,
    tile_vals,
    tile_col,
    halo_count,
    halo_target,
):
    high = lax.Precision.HIGH
    node_rows, width = features.shape
    blocks = node_rows // BLOCK
    groups = lax.axis_size("group")
    members = lax.axis_size("local")
    slot_count = halo_target.shape[1]
    dead = slot_count - main
    swap = [(i, i ^ 1) for i in range(members)]
    pairs = [(i, i ^ 2) for i in range(members)]
    across = [(i, members - 2 - (i - i % 2) + i % 2) for i in range(members)]
    along_x = [[(i, (i + 2 * k) % members) for i in range(members)] for k in range(4)]
    along_y = [[(i, (i + 4 * k) % groups) for i in range(groups)] for k in range(4)]
    along_z = [[(i, i // 4 * 4 + (i + k) % 4) for i in range(groups)] for k in range(4)]

    pre_grad, other_local, send, places, column = tile_sums(
        tile_col, halo_count, w_neigh, tile_vals, main, dead, preact=preact, grad_out=grad_out
    )
    recv = lax.ppermute(send, "local", swap)
    own_local, flag, keep_a, send_a, keep_b, send_b = tile_sums(
        column, halo_count, w_neigh, tile_vals, main, dead, pre_grad=pre_grad, recv=recv
    )
    recv_a = lax.ppermute(send_a, "local", pairs)
    recv_b = lax.ppermute(send_b, "local", across)

    contract = (((0,), (0,)), ((), ()))
    self_term = lax.dot_general(
        features, pre_grad, contract, precision=high, preferred_element_type=F32
    )
    neigh_term = lax.dot_general(
        aggregated, pre_grad, contract, precision=high, preferred_element_type=F32
    )
    pieces = jax.ShapeDtypeStruct((groups, width // BLOCK, width // groups, BLOCK), F32)
    stay, leave = small(sort_kernel, [pieces] * 2, [self_term, neigh_term], "sort_terms")
    by_y = (4, groups // 4) + pieces.shape[1:]
    stay, leave = stay.reshape(by_y), lax.ppermute(leave, "local", swap).reshape(by_y)
    mine, *sends = scatter(lambda g: g >> 2, [stay, leave], "sum_cores", [flag])
    terms = [mine] + [
        lax.ppermute(some, "group", along_y[k + 1]) for k, some in enumerate(sends)
    ]
    mine, *sends = scatter(lambda g: g & 3, terms, "sum_y")
    terms = [mine] + [
        lax.ppermute(some, "group", along_z[k + 1]) for k, some in enumerate(sends)
    ]

    base = small(
        self_kernel,
        jax.ShapeDtypeStruct(pre_grad.shape, F32),
        [pre_grad, w_self, other_local, own_local, mine],
        "self_rows",
        [IN_VMEM] * 4 + [ANYWHERE],
        scratch=[pltpu.VMEM((blocks, width, BLOCK), F32)],
        mebibytes=16,
        flops=6 * pre_grad.size * width,
    )
    keep, send_a, send_b = second_sums(keep_a, recv_a, keep_b, recv_b, [base, terms[1]])
    recv_a = lax.ppermute(send_a, "local", across)
    recv_b = lax.ppermute(send_b, "local", pairs)
    share_shape = jax.ShapeDtypeStruct(mine.shape, F32)
    share = small(sum_kernel, share_shape, terms, "sum_z")
    terms = [share] + [lax.ppermute(share, "local", p) for p in (pairs, across, along_x[2])]
    scale = float(node_rows * groups * members) ** (-0.5)
    share = small(functools.partial(chips_kernel, scale), share_shape, terms, "sum_chips")
    shares = third_sums(places, keep, recv_a, recv_b, share)
    arrived = lax.all_to_all(shares, "group", split_axis=0, concat_axis=0, tiled=True)
    terms = [share] + [lax.ppermute(share, "group", along_z[k]) for k in range(1, 4)]
    row = gather(lambda g: g & 3, terms, "gather_z")

    send, *keeps = place(halo_count, halo_target, arrived, row, blocks)
    swapped = lax.ppermute(send, "local", swap)
    joined = jax.ShapeDtypeStruct((2,) + keeps[0].shape, F32)
    joined = small(join_kernel, [joined] * 3, [*keeps[1:], swapped], "join")
    received = [lax.ppermute(joined[k - 1], "local", along_x[k]) for k in range(1, 4)]

    row = small(
        pass_kernel,
        jax.ShapeDtypeStruct(row.shape, F32),
        [row, joined[0]],
        "pass",
        [IN_VMEM, ANYWHERE],
    )
    rows = [row] + [lax.ppermute(row, "group", along_y[k]) for k in range(1, 4)]
    whole = gather(lambda g: g >> 2, rows, "gather_y", received).reshape(pieces.shape)
    other = lax.ppermute(whole, "local", swap)
    square = jax.ShapeDtypeStruct(self_term.shape, F32)
    self_grad, neigh_grad = small(grads_kernel, [square] * 2, [whole, other], "sort_grads")

    node_grad = finish(base, keeps[0], swapped, received)
    return (node_grad, self_grad, neigh_grad)


def on_device(*args):
    halo_count = args[8]
    most = jnp.max(jnp.sum(halo_count, axis=1))
    few, all_of_them = (functools.partial(body, main) for main in MAINS)
    return lax.cond(most <= MAINS[0], few, all_of_them, *args)


def solution(mesh):
    in_specs = (
        P(("group", "local"), None),
        P(("group", "local"), None),
        P(("group", "local"), None),
        P(("group", "local"), None),
        P(),
        P(),
        P(("group", "local"), None, None),
        P(("group", "local")),
        P(),
        P(),
    )
    out_specs = (P(("group", "local"), None), P(), P())
    return jax.shard_map(
        on_device, mesh=mesh, in_specs=in_specs, out_specs=out_specs, check_vma=False
    )
```

```python
import functools

import jax
import jax.numpy as jnp
from jax import lax
from jax.experimental import pallas as pl
from jax.experimental.pallas import tpu as pltpu
from jax.sharding import PartitionSpec as P

F32 = jnp.float32
BF16 = jnp.bfloat16
BLOCK = 128
CHUNKS = 2
MAIN = 30
LIMIT_OTHER = 55
LIMIT_OWN = 20
LIMIT_SMALL = 6


def split(x):
    high = x.astype(BF16)
    low = (x - high.astype(F32)).astype(BF16)
    return high, low


def limit(mebibytes):
    return pltpu.CompilerParams(vmem_limit_bytes=mebibytes * 1024 * 1024)


def whereabouts():
    member = lax.axis_index("local")
    chip = member >> 1
    side = chip >> 1
    return member & 1, side, (chip + side) & 1


def slot_places(count_ref, places):
    slots = places.shape[0]
    owners = count_ref.shape[1]
    capacity = slots // owners
    group = lax.axis_index("group")

    def owner(o, carry):
        live, dead = carry
        count = count_ref[group, o]
        for j in range(capacity):
            is_live = j < count
            places[o * capacity + j] = jnp.where(is_live, live, slots - 1 - dead)
            live = live + is_live.astype(jnp.int32)
            dead = dead + 1 - is_live.astype(jnp.int32)
        return live, dead

    zero = jnp.int32(0)
    lax.fori_loop(0, owners, owner, (zero, zero))


def tile_kernel(own, blocks, main, over, col_ref, count_ref, *rest):
    if own:
        pre_hbm, weight_hbm, tiles_hbm, recv_ref, local_ref, flag_ref, *rest = rest
        keep_a, send_a, keep_b, send_b, pre, weight, tiles, sums, sems = rest
        column = col_ref
    else:
        pre_hbm, grad_hbm, weight_hbm, tiles_hbm, pre_ref, local_ref, send_ref, places, column, *rest = rest
        pre, grad, weight, tiles, sums, sems = rest
    width = weight.shape[0]
    rows = pre.shape[0] // CHUNKS
    count = tiles.shape[0] // CHUNKS
    core, p, q = whereabouts()
    half = core if own else 1 - core
    some = pl.ds(pl.multiple_of(half * width, width), width)
    weight_copy = pltpu.make_async_copy(weight_hbm.at[some], weight, sems.at[0])
    weight_copy.start()
    if own:
        flag_ref[0] = core
        main_sums = sums.at[pl.ds(blocks, main)]
        recv_copy = pltpu.make_async_copy(recv_ref, main_sums, sems.at[1])
        recv_copy.start()
    chunks = []
    for i in range(CHUNKS):
        at = pl.ds(i * rows, rows)
        copies = [pltpu.make_async_copy(pre_hbm.at[at], pre.at[at], sems.at[2 + 3 * i])]
        if not own:
            copies.append(pltpu.make_async_copy(grad_hbm.at[at], grad.at[at], sems.at[3 + 3 * i]))
        some_tiles = pl.ds(i * count, count)
        copies.append(
            pltpu.make_async_copy(tiles_hbm.at[some_tiles], tiles.at[some_tiles], sems.at[4 + 3 * i])
        )
        for copy in copies:
            copy.start()
        chunks.append(copies)
    sums[0:blocks] = jnp.zeros((blocks,) + sums.shape[1:], F32)
    sums[blocks + main :] = jnp.zeros((over,) + sums.shape[1:], F32)
    if not own:
        sums[blocks : blocks + main] = jnp.zeros((main,) + sums.shape[1:], F32)
    if not own:
        slot_places(count_ref, places)

        def place_tile(t, _):
            col = col_ref[t]
            slot = jnp.maximum(col - blocks, 0)
            column[t] = jnp.where(col < blocks, col, blocks + places[slot])
            return 0

        lax.fori_loop(0, tiles.shape[0], place_tile, 0)
    weight_copy.wait()
    weight_high, weight_low = split(weight[...])
    contract = (((1,), (1,)), ((), ()))
    pre_copies = []
    for i in range(CHUNKS):
        at = pl.ds(i * rows, rows)
        *copies, tiles_copy = chunks[i]
        for copy in copies:
            copy.wait()
        if own:
            pre_grad = pre[at]
        else:
            pre_grad = jnp.where(pre[at] > 0, grad[at], 0.0)
            grad[at] = pre_grad
            pre_copy = pltpu.make_async_copy(grad.at[at], pre_ref.at[at], sems.at[2 + 3 * i])
            pre_copy.start()
            pre_copies.append(pre_copy)
        pre_high, pre_low = split(pre_grad)
        part = lax.dot_general(weight_high, pre_high, contract, preferred_element_type=F32)
        part += lax.dot_general(weight_high, pre_low, contract, preferred_element_type=F32)
        part += lax.dot_general(weight_low, pre_high, contract, preferred_element_type=F32)
        row_high, row_low = split(part)
        tiles_copy.wait()
        if own and i == 0:
            recv_copy.wait()
        for r in range(rows // BLOCK):
            mine = slice(r * BLOCK, (r + 1) * BLOCK)
            high = row_high[:, mine]
            left = jnp.concatenate([high, high, row_low[:, mine]], axis=1)
            each = count * BLOCK // rows
            for k in range(0, each, 2):
                t = i * count + r * each + k
                first_high, first_low = split(tiles[t])
                next_high, next_low = split(tiles[t + 1])
                high = jnp.concatenate([first_high, next_high], axis=1)
                low = jnp.concatenate([first_low, next_low], axis=1)
                right = jnp.concatenate([high, low, high], axis=0)
                product = jnp.dot(left, right, preferred_element_type=F32)
                sums[column[t]] += product[:, :BLOCK]
                sums[column[t + 1]] += product[:, BLOCK:]

    copies = []

    def out(source, target):
        copy = pltpu.make_async_copy(source, target, sems.at[2 + 3 * CHUNKS + len(copies)])
        copy.start()
        copies.append(copy)

    if own:
        some = main // 2
        share = width // 4

        def piece(first, p_at, q_at, target):
            share_rows = pl.ds(pl.multiple_of((p_at * 2 + q_at) * share, share), share)
            out(sums.at[pl.ds(blocks + first, some), share_rows], target)

        for k in range(2):
            piece(0, k, 1 - q, send_a.at[k])
            piece(some, 1 - p, k, send_b.at[k])
        for k in range(2):
            piece(0, k, q, keep_a.at[k])
            piece(some, p, k, keep_b.at[k])
    else:
        out(sums.at[pl.ds(blocks, main)], send_ref)
    out(sums.at[pl.ds(0, blocks)], local_ref)
    for copy in pre_copies + copies:
        copy.wait()


def tile_sums(
    tile_col, halo_count, weight, tile_vals, main, over, preact=None, grad_out=None,
    pre_grad=None, recv=None,
):
    own = recv is not None
    node_rows, feat = (pre_grad if own else preact).shape
    width = weight.shape[0] // 2
    blocks = node_rows // BLOCK
    some = main // 2
    anywhere = pl.BlockSpec(memory_space=pl.ANY)
    local = jax.ShapeDtypeStruct((blocks, width, BLOCK), F32)
    piece = jax.ShapeDtypeStruct((2, some, width // 4, BLOCK), F32)
    if own:
        args = [pre_grad, weight, tile_vals, recv]
        flag = jax.ShapeDtypeStruct((1,), jnp.int32)
        out_shape = [local, flag] + [piece] * 4
    else:
        args = [preact, grad_out, weight, tile_vals]
        out_shape = [
            jax.ShapeDtypeStruct((node_rows, feat), F32),
            local,
            jax.ShapeDtypeStruct((main, width, BLOCK), F32),
            jax.ShapeDtypeStruct((main + over,), jnp.int32),
            jax.ShapeDtypeStruct(tile_col.shape, jnp.int32),
        ]
    scratch = [pltpu.VMEM((node_rows, feat), F32)]
    if not own:
        scratch.append(pltpu.VMEM((node_rows, feat), F32))
    scratch += [
        pltpu.VMEM((width, feat), F32),
        pltpu.VMEM(tile_vals.shape, F32),
        pltpu.VMEM((blocks + main + over, width, BLOCK), F32),
        pltpu.SemaphoreType.DMA((2 + 3 * CHUNKS + 10,)),
    ]
    return pl.pallas_call(
        functools.partial(tile_kernel, own, blocks, main, over),
        out_shape=out_shape,
        in_specs=[pl.BlockSpec(memory_space=pltpu.SMEM)] * 2 + [anywhere] * len(args),
        out_specs=[
            pl.BlockSpec(memory_space=pltpu.SMEM) if x.dtype == jnp.int32 else anywhere
            for x in out_shape
        ],
        scratch_shapes=scratch,
        compiler_params=limit(LIMIT_OWN if own else LIMIT_OTHER),
        cost_estimate=pl.CostEstimate(
            flops=6 * (tile_vals.size + node_rows * feat) * width,
            bytes_accessed=14 * 1024 * 1024,
            transcendentals=0,
        ),
        name="own_tile_sums" if own else "other_tile_sums",
    )(tile_col, halo_count, *args)


IN_VMEM = pl.BlockSpec(memory_space=pltpu.VMEM)
IN_SMEM = pl.BlockSpec(memory_space=pltpu.SMEM)
ANYWHERE = pl.BlockSpec(memory_space=pl.ANY)


def second_kernel(keep_a, recv_a, keep_b, recv_b, *rest):
    keep, send_a, send_b = rest[-3:]
    _, p, q = whereabouts()
    send_a[...] = keep_a[1 - p] + recv_a[1 - p]
    send_b[...] = keep_b[1 - q] + recv_b[1 - q]
    keep[0] = keep_a[p] + recv_a[p]
    keep[1] = keep_b[q] + recv_b[q]


def second_sums(keep_a, recv_a, keep_b, recv_b, after):
    send = jax.ShapeDtypeStruct(keep_a.shape[1:], F32)
    out_shape = [jax.ShapeDtypeStruct(keep_a.shape, F32), send, send]
    return small(
        second_kernel,
        out_shape,
        [keep_a, recv_a, keep_b, recv_b, *after],
        "second_sums",
        [IN_VMEM] * 4 + [ANYWHERE] * len(after),
    )


def third_kernel(places, keep, recv_a, recv_b, after, out, total):
    del after
    half = recv_a.shape[0]
    main = 2 * half
    total[0:half] = keep[0] + recv_a[...]
    total[half:main] = keep[1] + recv_b[...]
    total[main:] = jnp.zeros_like(total[main:])
    for slot in range(out.shape[0]):
        out[slot] = total[places[slot]]


def third_sums(places, keep, recv_a, recv_b, after):
    shape = (places.shape[0],) + keep.shape[2:]
    return small(
        third_kernel,
        jax.ShapeDtypeStruct(shape, F32),
        [places, keep, recv_a, recv_b, after],
        "third_sums",
        [IN_SMEM] + [IN_VMEM] * 3 + [ANYWHERE],
        scratch=[pltpu.VMEM(shape, F32)],
    )


def small(
    kernel, out_shape, args, name, specs=None, scratch=(), mebibytes=LIMIT_SMALL, flops=None
):
    size = max(x.size for x in args)
    return pl.pallas_call(
        kernel,
        out_shape=out_shape,
        in_specs=specs or [IN_VMEM] * len(args),
        out_specs=jax.tree.map(lambda _: IN_VMEM, out_shape),
        scratch_shapes=scratch,
        cost_estimate=pl.CostEstimate(
            flops=flops or size, bytes_accessed=12 * size, transcendentals=0
        ),
        compiler_params=limit(mebibytes),
        name=name,
    )(*args)


def sort_kernel(self_term, neigh_term, keep, send):
    core, _, _ = whereabouts()
    pieces, columns, rows, _ = keep.shape

    def copy(source, target):
        for g in range(pieces):
            for c in range(columns):
                some = (slice(g * rows, (g + 1) * rows), slice(c * BLOCK, (c + 1) * BLOCK))
                target[g, c] = source[some]

    @pl.when(core == 0)
    def _():
        copy(self_term, keep)
        copy(neigh_term, send)

    @pl.when(core != 0)
    def _():
        copy(neigh_term, keep)
        copy(self_term, send)


def grads_kernel(whole, other, self_grad, neigh_grad):
    core, _, _ = whereabouts()
    pieces, columns, rows, _ = whole.shape

    def copy(source, target):
        for g in range(pieces):
            for c in range(columns):
                some = (slice(g * rows, (g + 1) * rows), slice(c * BLOCK, (c + 1) * BLOCK))
                target[some] = source[g, c]

    @pl.when(core == 0)
    def _():
        copy(whole, self_grad)
        copy(other, neigh_grad)

    @pl.when(core != 0)
    def _():
        copy(other, self_grad)
        copy(whole, neigh_grad)


def scatter_kernel(axis_of, count, *rest):
    terms = rest[:count]
    outs = rest[-4:]
    me = axis_of(lax.axis_index("group"))
    for away, out in enumerate(outs):
        at = (me + away) & 3
        total = terms[0][at]
        for term in terms[1:]:
            total += term[at]
        out[...] = total


def scatter(axis_of, terms, name, after=()):
    piece = jax.ShapeDtypeStruct(terms[0].shape[1:], F32)
    return small(
        functools.partial(scatter_kernel, axis_of, len(terms)),
        [piece] * 4,
        [*terms, *after],
        name,
        [IN_VMEM] * len(terms) + [IN_SMEM] * len(after),
    )


def sum_kernel(*rest):
    *terms, out = rest
    total = terms[0][...]
    for term in terms[1:]:
        total += term[...]
    out[...] = total


def chips_kernel(scale, mine, pair, far_one, far_two, out):
    out[...] = ((mine[...] + pair[...]) + (far_one[...] + far_two[...])) * scale


def pass_kernel(value, *rest):
    rest[-1][...] = value[...]


def gather_kernel(axis_of, *rest):
    pieces = rest[:4]
    out = rest[-1]
    me = axis_of(lax.axis_index("group"))
    for away, piece in enumerate(pieces):
        out[(me - away) & 3] = piece[...]


def gather(axis_of, pieces, name, after=()):
    whole = jax.ShapeDtypeStruct((4,) + pieces[0].shape, F32)
    specs = [IN_VMEM] * 4 + [ANYWHERE] * len(after)
    return small(functools.partial(gather_kernel, axis_of), whole, [*pieces, *after], name, specs)


def place_kernel(count_ref, target_ref, arrived, after, send, *keeps):
    del after
    core, _, _ = whereabouts()
    chip = lax.axis_index("local") >> 1
    group = lax.axis_index("group")
    sources = count_ref.shape[0]
    capacity = arrived.shape[0] // sources
    blocks = send.shape[1]
    shift = blocks.bit_length() - 1
    for out in (send, *keeps):
        out[...] = jnp.zeros_like(out)

    @pl.loop(0, sources)
    def _(source):
        count = count_ref[source, group]
        for j in range(capacity):
            target = target_ref[source, group * capacity + j]
            member = lax.shift_right_logical(target, shift)
            block = target & (blocks - 1)
            away = (lax.shift_right_logical(member, 1) - chip) & 3
            mine = (member & 1) == core

            @pl.when(j < count)
            def _():
                @pl.when(jnp.logical_not(mine))
                def _():
                    send[away, block] += arrived[source * capacity + j]

                @pl.when(mine)
                def _():
                    for k, keep in enumerate(keeps):

                        @pl.when(away == k)
                        def _():
                            keep[block] += arrived[source * capacity + j]


def place(halo_count, halo_target, arrived, after, blocks):
    keep = jax.ShapeDtypeStruct((blocks,) + arrived.shape[1:], F32)
    send = jax.ShapeDtypeStruct((4,) + keep.shape, F32)
    specs = [IN_SMEM, IN_SMEM, IN_VMEM, ANYWHERE]
    args = [halo_count, halo_target, arrived, after]
    return small(place_kernel, [send] + [keep] * 4, args, "place", specs)


def join_kernel(*rest):
    *keeps, swapped = rest[: len(rest) // 2 + 1]
    for k, out in enumerate(rest[len(rest) // 2 + 1 :]):
        out[0] = keeps[k][...]
        out[1] = swapped[k + 1]


def self_kernel(pre_grad, weight, other_local, own_local, after, out, total):
    del after
    core, _, _ = whereabouts()
    width = own_local.shape[1]
    own = pl.ds(pl.multiple_of(core * width, width), width)
    other = pl.ds(pl.multiple_of((1 - core) * width, width), width)
    contract = (((1,), (1,)), ((), ()))
    weight_high, weight_low = split(weight[...])
    rows = out.shape[0] // 4
    for i in range(4):
        at = slice(i * rows, (i + 1) * rows)
        high, low = split(pre_grad[at])
        rows_of = lax.dot_general(high, weight_high, contract, preferred_element_type=F32)
        rows_of += lax.dot_general(high, weight_low, contract, preferred_element_type=F32)
        rows_of += lax.dot_general(low, weight_high, contract, preferred_element_type=F32)
        out[at] = rows_of
    for b in range(own_local.shape[0]):
        total[b, own] = own_local[b]
        total[b, other] = other_local[b]
        out[b * BLOCK : (b + 1) * BLOCK] += total[b].T


def finish_kernel(base, keep, swapped, *rest):
    *received, out, total, rows, sems = rest
    core, _, _ = whereabouts()
    chip = lax.axis_index("local") >> 1
    blocks, share, _ = keep.shape
    pieces = [keep, swapped.at[0]] + [some.at[k] for some in received for k in range(2)]
    copies = []
    for b in range(blocks):
        for k, some in enumerate(pieces):
            source = (chip - k // 2) & 3
            side = source >> 1
            quarter = side * 2 + ((source + side) & 1)
            first = core if k % 2 == 0 else 1 - core
            start = pl.multiple_of((first * 4 + quarter) * share, share)
            total[b, pl.ds(start, share)] = some[b]
        at = slice(b * BLOCK, (b + 1) * BLOCK)
        rows[at] = base[at] + total[b].T
        copy = pltpu.make_async_copy(rows.at[at], out.at[at], sems.at[b])
        copy.start()
        copies.append(copy)
    for copy in copies:
        copy.wait()


def finish(base, keep, swapped, received):
    node_rows, feat = base.shape
    blocks = keep.shape[0]
    return pl.pallas_call(
        finish_kernel,
        out_shape=jax.ShapeDtypeStruct(base.shape, F32),
        in_specs=[IN_VMEM] * (3 + len(received)),
        out_specs=ANYWHERE,
        scratch_shapes=[
            pltpu.VMEM((blocks, feat, BLOCK), F32),
            pltpu.VMEM((node_rows, feat), F32),
            pltpu.SemaphoreType.DMA((blocks,)),
        ],
        cost_estimate=pl.CostEstimate(
            flops=2 * base.size, bytes_accessed=16 * base.size, transcendentals=0
        ),
        compiler_params=limit(8),
        name="finish",
    )(base, keep, swapped, *received)


def on_device(
    features,
    aggregated,
    preact,
    grad_out,
    w_self,
    w_neigh,
    tile_vals,
    tile_col,
    halo_count,
    halo_target,
):
    high = lax.Precision.HIGH
    node_rows, width = features.shape
    blocks = node_rows // BLOCK
    groups = lax.axis_size("group")
    members = lax.axis_size("local")
    slot_count = halo_target.shape[1]
    dead = slot_count - MAIN
    swap = [(i, i ^ 1) for i in range(members)]
    pairs = [(i, i ^ 2) for i in range(members)]
    across = [(i, members - 2 - (i - i % 2) + i % 2) for i in range(members)]
    along_x = [[(i, (i + 2 * k) % members) for i in range(members)] for k in range(4)]
    along_y = [[(i, (i + 4 * k) % groups) for i in range(groups)] for k in range(4)]
    along_z = [[(i, i // 4 * 4 + (i + k) % 4) for i in range(groups)] for k in range(4)]

    pre_grad, other_local, send, places, column = tile_sums(
        tile_col, halo_count, w_neigh, tile_vals, MAIN, dead, preact=preact, grad_out=grad_out
    )
    recv = lax.ppermute(send, "local", swap)
    own_local, flag, keep_a, send_a, keep_b, send_b = tile_sums(
        column, halo_count, w_neigh, tile_vals, MAIN, dead, pre_grad=pre_grad, recv=recv
    )
    recv_a = lax.ppermute(send_a, "local", pairs)
    recv_b = lax.ppermute(send_b, "local", across)

    contract = (((0,), (0,)), ((), ()))
    self_term = lax.dot_general(
        features, pre_grad, contract, precision=high, preferred_element_type=F32
    )
    neigh_term = lax.dot_general(
        aggregated, pre_grad, contract, precision=high, preferred_element_type=F32
    )
    pieces = jax.ShapeDtypeStruct((groups, width // BLOCK, width // groups, BLOCK), F32)
    stay, leave = small(sort_kernel, [pieces] * 2, [self_term, neigh_term], "sort_terms")
    by_y = (4, groups // 4) + pieces.shape[1:]
    stay, leave = stay.reshape(by_y), lax.ppermute(leave, "local", swap).reshape(by_y)
    mine, *sends = scatter(lambda g: g >> 2, [stay, leave], "sum_cores", [flag])
    terms = [mine] + [
        lax.ppermute(some, "group", along_y[k + 1]) for k, some in enumerate(sends)
    ]
    mine, *sends = scatter(lambda g: g & 3, terms, "sum_y")
    terms = [mine] + [
        lax.ppermute(some, "group", along_z[k + 1]) for k, some in enumerate(sends)
    ]

    base = small(
        self_kernel,
        jax.ShapeDtypeStruct(pre_grad.shape, F32),
        [pre_grad, w_self, other_local, own_local, mine],
        "self_rows",
        [IN_VMEM] * 4 + [ANYWHERE],
        scratch=[pltpu.VMEM((blocks, width, BLOCK), F32)],
        mebibytes=16,
        flops=6 * pre_grad.size * width,
    )
    keep, send_a, send_b = second_sums(keep_a, recv_a, keep_b, recv_b, [base, terms[1]])
    recv_a = lax.ppermute(send_a, "local", across)
    recv_b = lax.ppermute(send_b, "local", pairs)
    share_shape = jax.ShapeDtypeStruct(mine.shape, F32)
    share = small(sum_kernel, share_shape, terms, "sum_z")
    shares = third_sums(places, keep, recv_a, recv_b, share)
    arrived = lax.all_to_all(shares, "group", split_axis=0, concat_axis=0, tiled=True)
    share = small(pass_kernel, share_shape, [share, shares], "pass", [IN_VMEM, ANYWHERE])
    terms = [share] + [lax.ppermute(share, "local", p) for p in (pairs, across, along_x[2])]
    scale = float(node_rows * groups * members) ** (-0.5)
    share = small(functools.partial(chips_kernel, scale), share_shape, terms, "sum_chips")
    terms = [share] + [lax.ppermute(share, "group", along_z[k]) for k in range(1, 4)]
    row = gather(lambda g: g & 3, terms, "gather_z")

    send, *keeps = place(halo_count, halo_target, arrived, row, blocks)
    swapped = lax.ppermute(send, "local", swap)
    joined = jax.ShapeDtypeStruct((2,) + keeps[0].shape, F32)
    joined = small(join_kernel, [joined] * 3, [*keeps[1:], swapped], "join")
    received = [lax.ppermute(joined[k - 1], "local", along_x[k]) for k in range(1, 4)]

    row = small(
        pass_kernel,
        jax.ShapeDtypeStruct(row.shape, F32),
        [row, joined[0]],
        "pass",
        [IN_VMEM, ANYWHERE],
    )
    rows = [row] + [lax.ppermute(row, "group", along_y[k]) for k in range(1, 4)]
    whole = gather(lambda g: g >> 2, rows, "gather_y", received).reshape(pieces.shape)
    other = lax.ppermute(whole, "local", swap)
    square = jax.ShapeDtypeStruct(self_term.shape, F32)
    self_grad, neigh_grad = small(grads_kernel, [square] * 2, [whole, other], "sort_grads")

    node_grad = finish(base, keeps[0], swapped, received)
    return (node_grad, self_grad, neigh_grad)


def solution(mesh):
    in_specs = (
        P(("group", "local"), None),
        P(("group", "local"), None),
        P(("group", "local"), None),
        P(("group", "local"), None),
        P(),
        P(),
        P(("group", "local"), None, None),
        P(("group", "local")),
        P(),
        P(),
    )
    out_specs = (P(("group", "local"), None), P(), P())
    return jax.shard_map(
        on_device, mesh=mesh, in_specs=in_specs, out_specs=out_specs, check_vma=False
    )
```

```python
import functools

import jax
import jax.numpy as jnp
from jax import lax
from jax.experimental import pallas as pl
from jax.experimental.pallas import tpu as pltpu
from jax.sharding import PartitionSpec as P

F32 = jnp.float32
BF16 = jnp.bfloat16
BLOCK = 128
CHUNKS = 2
MAIN = 30
LIMIT_OTHER = 52
LIMIT_OWN = 20
LIMIT_SMALL = 6
AWAY = (0, 1, 3, 2)


def split(x):
    high = x.astype(BF16)
    low = (x - high.astype(F32)).astype(BF16)
    return high, low


def limit(mebibytes):
    return pltpu.CompilerParams(vmem_limit_bytes=mebibytes * 1024 * 1024)


def whereabouts():
    member = lax.axis_index("local")
    chip = member >> 1
    side = chip >> 1
    return member & 1, side, (chip + side) & 1


def slot_places(count_ref, places):
    slots = places.shape[0]
    owners = count_ref.shape[1]
    capacity = slots // owners
    group = lax.axis_index("group")

    def owner(o, carry):
        live, dead = carry
        count = count_ref[group, o]
        for j in range(capacity):
            is_live = j < count
            places[o * capacity + j] = jnp.where(is_live, live, slots - 1 - dead)
            live = live + is_live.astype(jnp.int32)
            dead = dead + 1 - is_live.astype(jnp.int32)
        return live, dead

    zero = jnp.int32(0)
    lax.fori_loop(0, owners, owner, (zero, zero))


def tile_kernel(own, blocks, main, over, col_ref, count_ref, *rest):
    if own:
        pre_hbm, weight_hbm, tiles_hbm, recv_ref, local_ref, flag_ref, *rest = rest
        keep_a, send_a, keep_b, send_b, pre, weight, tiles, sums, sems = rest
        column = col_ref
    else:
        pre_hbm, grad_hbm, weight_hbm, tiles_hbm, pre_ref, local_ref, send_ref, places, column, *rest = rest
        pre, grad, weight, tiles, sums, sems = rest
    width = weight.shape[0]
    rows = pre.shape[0] // CHUNKS
    count = tiles.shape[0] // CHUNKS
    core, p, q = whereabouts()
    half = core if own else 1 - core
    some = pl.ds(pl.multiple_of(half * width, width), width)
    weight_copy = pltpu.make_async_copy(weight_hbm.at[some], weight, sems.at[0])
    weight_copy.start()
    if own:
        flag_ref[0] = core
        main_sums = sums.at[pl.ds(blocks, main)]
        recv_copy = pltpu.make_async_copy(recv_ref, main_sums, sems.at[1])
        recv_copy.start()
    chunks = []
    for i in range(CHUNKS):
        at = pl.ds(i * rows, rows)
        copies = [pltpu.make_async_copy(pre_hbm.at[at], pre.at[at], sems.at[2 + 3 * i])]
        if not own:
            copies.append(pltpu.make_async_copy(grad_hbm.at[at], grad.at[at], sems.at[3 + 3 * i]))
        some_tiles = pl.ds(i * count, count)
        copies.append(
            pltpu.make_async_copy(tiles_hbm.at[some_tiles], tiles.at[some_tiles], sems.at[4 + 3 * i])
        )
        for copy in copies:
            copy.start()
        chunks.append(copies)
    sums[0:blocks] = jnp.zeros((blocks,) + sums.shape[1:], F32)
    sums[blocks + main :] = jnp.zeros((over,) + sums.shape[1:], F32)
    if not own:
        sums[blocks : blocks + main] = jnp.zeros((main,) + sums.shape[1:], F32)
    if not own:
        slot_places(count_ref, places)

        def place_tile(t, _):
            col = col_ref[t]
            slot = jnp.maximum(col - blocks, 0)
            column[t] = jnp.where(col < blocks, col, blocks + places[slot])
            return 0

        lax.fori_loop(0, tiles.shape[0], place_tile, 0)
    weight_copy.wait()
    weight_high, weight_low = split(weight[...])
    contract = (((1,), (1,)), ((), ()))
    pre_copies = []
    for i in range(CHUNKS):
        at = pl.ds(i * rows, rows)
        *copies, tiles_copy = chunks[i]
        for copy in copies:
            copy.wait()
        if own:
            pre_grad = pre[at]
        else:
            pre_grad = jnp.where(pre[at] > 0, grad[at], 0.0)
            grad[at] = pre_grad
            pre_copy = pltpu.make_async_copy(grad.at[at], pre_ref.at[at], sems.at[2 + 3 * i])
            pre_copy.start()
            pre_copies.append(pre_copy)
        pre_high, pre_low = split(pre_grad)
        part = lax.dot_general(weight_high, pre_high, contract, preferred_element_type=F32)
        part += lax.dot_general(weight_high, pre_low, contract, preferred_element_type=F32)
        part += lax.dot_general(weight_low, pre_high, contract, preferred_element_type=F32)
        row_high, row_low = split(part)
        tiles_copy.wait()
        if own and i == 0:
            recv_copy.wait()
        for r in range(rows // BLOCK):
            mine = slice(r * BLOCK, (r + 1) * BLOCK)
            high = row_high[:, mine]
            left = jnp.concatenate([high, high, row_low[:, mine]], axis=1)
            each = count * BLOCK // rows
            for k in range(0, each, 2):
                t = i * count + r * each + k
                first_high, first_low = split(tiles[t])
                next_high, next_low = split(tiles[t + 1])
                high = jnp.concatenate([first_high, next_high], axis=1)
                low = jnp.concatenate([first_low, next_low], axis=1)
                right = jnp.concatenate([high, low, high], axis=0)
                product = jnp.dot(left, right, preferred_element_type=F32)
                sums[column[t]] += product[:, :BLOCK]
                sums[column[t + 1]] += product[:, BLOCK:]

    copies = []

    def out(source, target):
        copy = pltpu.make_async_copy(source, target, sems.at[2 + 3 * CHUNKS + len(copies)])
        copy.start()
        copies.append(copy)

    if own:
        some = main // 2
        share = width // 4

        def piece(first, p_at, q_at, target):
            share_rows = pl.ds(pl.multiple_of((p_at * 2 + q_at) * share, share), share)
            out(sums.at[pl.ds(blocks + first, some), share_rows], target)

        for k in range(2):
            piece(0, k, 1 - q, send_a.at[k])
            piece(some, 1 - p, k, send_b.at[k])
        for k in range(2):
            piece(0, k, q, keep_a.at[k])
            piece(some, p, k, keep_b.at[k])
    else:
        out(sums.at[pl.ds(blocks, main)], send_ref)
    out(sums.at[pl.ds(0, blocks)], local_ref)
    for copy in pre_copies + copies:
        copy.wait()


def tile_sums(
    tile_col, halo_count, weight, tile_vals, main, over, preact=None, grad_out=None,
    pre_grad=None, recv=None,
):
    own = recv is not None
    node_rows, feat = (pre_grad if own else preact).shape
    width = weight.shape[0] // 2
    blocks = node_rows // BLOCK
    some = main // 2
    anywhere = pl.BlockSpec(memory_space=pl.ANY)
    local = jax.ShapeDtypeStruct((blocks, width, BLOCK), F32)
    piece = jax.ShapeDtypeStruct((2, some, width // 4, BLOCK), F32)
    if own:
        args = [pre_grad, weight, tile_vals, recv]
        flag = jax.ShapeDtypeStruct((1,), jnp.int32)
        out_shape = [local, flag] + [piece] * 4
    else:
        args = [preact, grad_out, weight, tile_vals]
        out_shape = [
            jax.ShapeDtypeStruct((node_rows, feat), F32),
            local,
            pltpu.VMEM((main, width, BLOCK), F32),
            jax.ShapeDtypeStruct((main + over,), jnp.int32),
            jax.ShapeDtypeStruct(tile_col.shape, jnp.int32),
        ]
    scratch = [pltpu.VMEM((node_rows, feat), F32)]
    if not own:
        scratch.append(pltpu.VMEM((node_rows, feat), F32))
    scratch += [
        pltpu.VMEM((width, feat), F32),
        pltpu.VMEM(tile_vals.shape, F32),
        pltpu.VMEM((blocks + main + over, width, BLOCK), F32),
        pltpu.SemaphoreType.DMA((2 + 3 * CHUNKS + 10,)),
    ]
    return pl.pallas_call(
        functools.partial(tile_kernel, own, blocks, main, over),
        out_shape=out_shape,
        in_specs=[pl.BlockSpec(memory_space=pltpu.SMEM)] * 2 + [anywhere] * len(args),
        out_specs=[
            pl.BlockSpec(memory_space=pltpu.SMEM) if x.dtype == jnp.int32 else anywhere
            for x in out_shape
        ],
        scratch_shapes=scratch,
        compiler_params=limit(LIMIT_OWN if own else LIMIT_OTHER),
        cost_estimate=pl.CostEstimate(
            flops=6 * (tile_vals.size + node_rows * feat) * width,
            bytes_accessed=14 * 1024 * 1024,
            transcendentals=0,
        ),
        name="own_tile_sums" if own else "other_tile_sums",
    )(tile_col, halo_count, *args)


IN_VMEM = pl.BlockSpec(memory_space=pltpu.VMEM)
IN_SMEM = pl.BlockSpec(memory_space=pltpu.SMEM)
ANYWHERE = pl.BlockSpec(memory_space=pl.ANY)


def second_kernel(keep_a, recv_a, keep_b, recv_b, *rest):
    keep, send_a, send_b = rest[-3:]
    _, p, q = whereabouts()
    send_a[...] = keep_a[1 - p] + recv_a[1 - p]
    send_b[...] = keep_b[1 - q] + recv_b[1 - q]
    keep[0] = keep_a[p] + recv_a[p]
    keep[1] = keep_b[q] + recv_b[q]


def second_sums(keep_a, recv_a, keep_b, recv_b, after):
    send = jax.ShapeDtypeStruct(keep_a.shape[1:], F32)
    out_shape = [jax.ShapeDtypeStruct(keep_a.shape, F32), send, send]
    return small(
        second_kernel,
        out_shape,
        [keep_a, recv_a, keep_b, recv_b, *after],
        "second_sums",
        [IN_VMEM] * 4 + [ANYWHERE] * len(after),
    )


def third_kernel(places, keep, recv_a, recv_b, after, out, total):
    del after
    half = recv_a.shape[0]
    main = 2 * half
    total[0:half] = keep[0] + recv_a[...]
    total[half:main] = keep[1] + recv_b[...]
    total[main:] = jnp.zeros_like(total[main:])
    for slot in range(out.shape[0]):
        out[slot] = total[places[slot]]


def third_sums(places, keep, recv_a, recv_b, after):
    shape = (places.shape[0],) + keep.shape[2:]
    return small(
        third_kernel,
        jax.ShapeDtypeStruct(shape, F32),
        [places, keep, recv_a, recv_b, after],
        "third_sums",
        [IN_SMEM] + [IN_VMEM] * 3 + [ANYWHERE],
        scratch=[pltpu.VMEM(shape, F32)],
    )


def small(
    kernel, out_shape, args, name, specs=None, scratch=(), mebibytes=LIMIT_SMALL, flops=None
):
    size = max(x.size for x in args)
    return pl.pallas_call(
        kernel,
        out_shape=out_shape,
        in_specs=specs or [IN_VMEM] * len(args),
        out_specs=jax.tree.map(lambda _: IN_VMEM, out_shape),
        scratch_shapes=scratch,
        cost_estimate=pl.CostEstimate(
            flops=flops or size, bytes_accessed=12 * size, transcendentals=0
        ),
        compiler_params=limit(mebibytes),
        name=name,
    )(*args)


def sort_kernel(self_term, neigh_term, keep, send):
    core, _, _ = whereabouts()
    pieces, columns, rows, _ = keep.shape

    def copy(source, target):
        for g in range(pieces):
            for c in range(columns):
                some = (slice(g * rows, (g + 1) * rows), slice(c * BLOCK, (c + 1) * BLOCK))
                target[g, c] = source[some]

    @pl.when(core == 0)
    def _():
        copy(self_term, keep)
        copy(neigh_term, send)

    @pl.when(core != 0)
    def _():
        copy(neigh_term, keep)
        copy(self_term, send)


def grads_kernel(whole, other, self_grad, neigh_grad):
    core, _, _ = whereabouts()
    pieces, columns, rows, _ = whole.shape

    def copy(source, target):
        for g in range(pieces):
            for c in range(columns):
                some = (slice(g * rows, (g + 1) * rows), slice(c * BLOCK, (c + 1) * BLOCK))
                target[some] = source[g, c]

    @pl.when(core == 0)
    def _():
        copy(whole, self_grad)
        copy(other, neigh_grad)

    @pl.when(core != 0)
    def _():
        copy(other, self_grad)
        copy(whole, neigh_grad)


def scatter_kernel(axis_of, count, *rest):
    terms = rest[:count]
    outs = rest[-4:]
    me = axis_of(lax.axis_index("group"))
    for away, out in enumerate(outs):
        at = (me + away) & 3
        total = terms[0][at]
        for term in terms[1:]:
            total += term[at]
        out[...] = total


def scatter(axis_of, terms, name, after=()):
    piece = jax.ShapeDtypeStruct(terms[0].shape[1:], F32)
    return small(
        functools.partial(scatter_kernel, axis_of, len(terms)),
        [piece] * 4,
        [*terms, *after],
        name,
        [IN_VMEM] * len(terms) + [IN_SMEM] * len(after),
    )


def sum_kernel(*rest):
    *terms, out = rest
    total = terms[0][...]
    for term in terms[1:]:
        total += term[...]
    out[...] = total


def chips_kernel(scale, mine, pair, far_one, far_two, after, out):
    del after
    out[...] = ((mine[...] + pair[...]) + (far_one[...] + far_two[...])) * scale


def pass_kernel(value, *rest):
    rest[-1][...] = value[...]


def gather_kernel(axis_of, *rest):
    pieces = rest[:4]
    out = rest[-1]
    me = axis_of(lax.axis_index("group"))
    for away, piece in enumerate(pieces):
        out[(me - away) & 3] = piece[...]


def gather(axis_of, pieces, name, after=()):
    whole = jax.ShapeDtypeStruct((4,) + pieces[0].shape, F32)
    specs = [IN_VMEM] * 4 + [ANYWHERE] * len(after)
    return small(functools.partial(gather_kernel, axis_of), whole, [*pieces, *after], name, specs)


def place_kernel(count_ref, target_ref, arrived, after, send, *keeps):
    del after
    core, _, _ = whereabouts()
    chip = lax.axis_index("local") >> 1
    group = lax.axis_index("group")
    sources = count_ref.shape[0]
    capacity = arrived.shape[0] // sources
    blocks = send.shape[1]
    shift = blocks.bit_length() - 1
    for out in (send, *keeps):
        out[...] = jnp.zeros_like(out)

    @pl.loop(0, sources)
    def _(source):
        count = count_ref[source, group]
        for j in range(capacity):
            target = target_ref[source, group * capacity + j]
            member = lax.shift_right_logical(target, shift)
            block = target & (blocks - 1)
            away = (lax.shift_right_logical(member, 1) - chip) & 3
            mine = (member & 1) == core

            @pl.when(j < count)
            def _():
                @pl.when(jnp.logical_not(mine))
                def _():
                    send[away, block] += arrived[source * capacity + j]

                @pl.when(mine)
                def _():
                    for k, keep in enumerate(keeps):

                        @pl.when(away == k)
                        def _():
                            keep[block] += arrived[source * capacity + j]


def place(halo_count, halo_target, arrived, after, blocks):
    keep = jax.ShapeDtypeStruct((blocks,) + arrived.shape[1:], F32)
    send = jax.ShapeDtypeStruct((4,) + keep.shape, F32)
    specs = [IN_SMEM, IN_SMEM, IN_VMEM, ANYWHERE]
    args = [halo_count, halo_target, arrived, after]
    return small(place_kernel, [send] + [keep] * 4, args, "place", specs)


def join_kernel(*rest):
    *keeps, swapped = rest[: len(rest) // 2 + 1]
    for k, out in enumerate(rest[len(rest) // 2 + 1 :]):
        out[0] = keeps[k][...]
        out[1] = swapped[k + 1]


def self_kernel(pre_grad, weight, other_local, own_local, after, out, total):
    del after
    core, _, _ = whereabouts()
    width = own_local.shape[1]
    own = pl.ds(pl.multiple_of(core * width, width), width)
    other = pl.ds(pl.multiple_of((1 - core) * width, width), width)
    contract = (((1,), (1,)), ((), ()))
    weight_high, weight_low = split(weight[...])
    rows = out.shape[0] // 4
    for i in range(4):
        at = slice(i * rows, (i + 1) * rows)
        high, low = split(pre_grad[at])
        rows_of = lax.dot_general(high, weight_high, contract, preferred_element_type=F32)
        rows_of += lax.dot_general(high, weight_low, contract, preferred_element_type=F32)
        rows_of += lax.dot_general(low, weight_high, contract, preferred_element_type=F32)
        out[at] = rows_of
    for b in range(own_local.shape[0]):
        total[b, own] = own_local[b]
        total[b, other] = other_local[b]
        out[b * BLOCK : (b + 1) * BLOCK] += total[b].T


def finish_kernel(base, keep, swapped, *rest):
    *received, out, total, rows, sems = rest
    core, _, _ = whereabouts()
    chip = lax.axis_index("local") >> 1
    blocks, share, _ = keep.shape
    pieces = [keep, swapped.at[0]] + [some.at[k] for some in received for k in range(2)]
    copies = []
    for b in range(blocks):
        for k, some in enumerate(pieces):
            source = (chip - AWAY[k // 2]) & 3
            side = source >> 1
            quarter = side * 2 + ((source + side) & 1)
            first = core if k % 2 == 0 else 1 - core
            start = pl.multiple_of((first * 4 + quarter) * share, share)
            total[b, pl.ds(start, share)] = some[b]
        at = slice(b * BLOCK, (b + 1) * BLOCK)
        rows[at] = base[at] + total[b].T
        copy = pltpu.make_async_copy(rows.at[at], out.at[at], sems.at[b])
        copy.start()
        copies.append(copy)
    for copy in copies:
        copy.wait()


def finish(base, keep, swapped, received):
    node_rows, feat = base.shape
    blocks = keep.shape[0]
    return pl.pallas_call(
        finish_kernel,
        out_shape=jax.ShapeDtypeStruct(base.shape, F32),
        in_specs=[IN_VMEM] * (3 + len(received)),
        out_specs=ANYWHERE,
        scratch_shapes=[
            pltpu.VMEM((blocks, feat, BLOCK), F32),
            pltpu.VMEM((node_rows, feat), F32),
            pltpu.SemaphoreType.DMA((blocks,)),
        ],
        cost_estimate=pl.CostEstimate(
            flops=2 * base.size, bytes_accessed=16 * base.size, transcendentals=0
        ),
        compiler_params=limit(8),
        name="finish",
    )(base, keep, swapped, *received)


def on_device(
    features,
    aggregated,
    preact,
    grad_out,
    w_self,
    w_neigh,
    tile_vals,
    tile_col,
    halo_count,
    halo_target,
):
    high = lax.Precision.HIGH
    node_rows, width = features.shape
    blocks = node_rows // BLOCK
    groups = lax.axis_size("group")
    members = lax.axis_size("local")
    slot_count = halo_target.shape[1]
    dead = slot_count - MAIN
    swap = [(i, i ^ 1) for i in range(members)]
    pairs = [(i, i ^ 2) for i in range(members)]
    across = [(i, members - 2 - (i - i % 2) + i % 2) for i in range(members)]
    along_x = [[(i, (i + 2 * k) % members) for i in range(members)] for k in range(4)]
    along_y = [[(i, (i + 4 * k) % groups) for i in range(groups)] for k in range(4)]
    along_z = [[(i, i // 4 * 4 + (i + k) % 4) for i in range(groups)] for k in range(4)]

    pre_grad, other_local, send, places, column = tile_sums(
        tile_col, halo_count, w_neigh, tile_vals, MAIN, dead, preact=preact, grad_out=grad_out
    )
    recv = lax.ppermute(send, "local", swap)
    own_local, flag, keep_a, send_a, keep_b, send_b = tile_sums(
        column, halo_count, w_neigh, tile_vals, MAIN, dead, pre_grad=pre_grad, recv=recv
    )
    recv_a = lax.ppermute(send_a, "local", pairs)
    recv_b = lax.ppermute(send_b, "local", across)

    contract = (((0,), (0,)), ((), ()))
    self_term = lax.dot_general(
        features, pre_grad, contract, precision=high, preferred_element_type=F32
    )
    neigh_term = lax.dot_general(
        aggregated, pre_grad, contract, precision=high, preferred_element_type=F32
    )
    pieces = jax.ShapeDtypeStruct((groups, width // BLOCK, width // groups, BLOCK), F32)
    stay, leave = small(sort_kernel, [pieces] * 2, [self_term, neigh_term], "sort_terms")
    by_y = (4, groups // 4) + pieces.shape[1:]
    stay, leave = stay.reshape(by_y), lax.ppermute(leave, "local", swap).reshape(by_y)
    mine, *sends = scatter(lambda g: g >> 2, [stay, leave], "sum_cores", [flag])
    terms = [mine] + [
        lax.ppermute(some, "group", along_y[k + 1]) for k, some in enumerate(sends)
    ]
    mine, *sends = scatter(lambda g: g & 3, terms, "sum_y")
    terms = [mine] + [
        lax.ppermute(some, "group", along_z[k + 1]) for k, some in enumerate(sends)
    ]

    base = small(
        self_kernel,
        jax.ShapeDtypeStruct(pre_grad.shape, F32),
        [pre_grad, w_self, other_local, own_local, mine],
        "self_rows",
        [IN_VMEM] * 4 + [ANYWHERE],
        scratch=[pltpu.VMEM((blocks, width, BLOCK), F32)],
        mebibytes=16,
        flops=6 * pre_grad.size * width,
    )
    keep, send_a, send_b = second_sums(keep_a, recv_a, keep_b, recv_b, [base, terms[1]])
    recv_a = lax.ppermute(send_a, "local", across)
    recv_b = lax.ppermute(send_b, "local", pairs)
    share_shape = jax.ShapeDtypeStruct(mine.shape, F32)
    share = small(sum_kernel, share_shape, terms, "sum_z")
    shares = third_sums(places, keep, recv_a, recv_b, share)
    arrived = lax.all_to_all(shares, "group", split_axis=0, concat_axis=0, tiled=True)
    terms = [share] + [lax.ppermute(share, "local", p) for p in (pairs, across, along_x[2])]
    scale = float(node_rows * groups * members) ** (-0.5)
    share = small(
        functools.partial(chips_kernel, scale),
        share_shape,
        [*terms, shares],
        "sum_chips",
        [IN_VMEM] * 4 + [ANYWHERE],
    )
    terms = [share] + [lax.ppermute(share, "group", along_z[k]) for k in range(1, 4)]
    row = gather(lambda g: g & 3, terms, "gather_z")

    send, *keeps = place(halo_count, halo_target, arrived, row, blocks)
    swapped = lax.ppermute(send, "local", swap)
    joined = jax.ShapeDtypeStruct((2,) + keeps[0].shape, F32)
    joined = small(join_kernel, [joined] * 3, [*keeps[1:], swapped], "join")
    received = [lax.ppermute(joined[k - 1], "local", along_x[k]) for k in AWAY[1:]]

    row = small(
        pass_kernel,
        jax.ShapeDtypeStruct(row.shape, F32),
        [row, joined[0]],
        "pass",
        [IN_VMEM, ANYWHERE],
    )
    rows = [row] + [lax.ppermute(row, "group", along_y[k]) for k in range(1, 4)]
    whole = gather(lambda g: g >> 2, rows, "gather_y", received).reshape(pieces.shape)
    other = lax.ppermute(whole, "local", swap)
    square = jax.ShapeDtypeStruct(self_term.shape, F32)
    self_grad, neigh_grad = small(grads_kernel, [square] * 2, [whole, other], "sort_grads")

    node_grad = finish(base, keeps[0], swapped, received)
    return (node_grad, self_grad, neigh_grad)


def solution(mesh):
    in_specs = (
        P(("group", "local"), None),
        P(("group", "local"), None),
        P(("group", "local"), None),
        P(("group", "local"), None),
        P(),
        P(),
        P(("group", "local"), None, None),
        P(("group", "local")),
        P(),
        P(),
    )
    out_specs = (P(("group", "local"), None), P(), P())
    return jax.shard_map(
        on_device, mesh=mesh, in_specs=in_specs, out_specs=out_specs, check_vma=False
    )
```

```python
import functools

import jax
import jax.numpy as jnp
from jax import lax
from jax.experimental import pallas as pl
from jax.experimental.pallas import tpu as pltpu
from jax.sharding import PartitionSpec as P

F32 = jnp.float32
BF16 = jnp.bfloat16
BLOCK = 128
CHUNKS = 2
MAIN = 30
LIMIT_OTHER = 51
LIMIT_OWN = 20
LIMIT_SMALL = 6
AWAY = (0, 1, 3, 2)


def split(x):
    high = x.astype(BF16)
    low = (x - high.astype(F32)).astype(BF16)
    return high, low


def limit(mebibytes):
    return pltpu.CompilerParams(vmem_limit_bytes=mebibytes * 1024 * 1024)


def whereabouts():
    member = lax.axis_index("local")
    chip = member >> 1
    side = chip >> 1
    return member & 1, side, (chip + side) & 1


def slot_places(count_ref, places):
    slots = places.shape[0]
    owners = count_ref.shape[1]
    capacity = slots // owners
    group = lax.axis_index("group")

    def owner(o, carry):
        live, dead = carry
        count = count_ref[group, o]
        for j in range(capacity):
            is_live = j < count
            places[o * capacity + j] = jnp.where(is_live, live, slots - 1 - dead)
            live = live + is_live.astype(jnp.int32)
            dead = dead + 1 - is_live.astype(jnp.int32)
        return live, dead

    zero = jnp.int32(0)
    lax.fori_loop(0, owners, owner, (zero, zero))


def tile_kernel(own, blocks, main, over, col_ref, count_ref, *rest):
    if own:
        pre_hbm, weight_hbm, tiles_hbm, recv_ref, local_ref, flag_ref, *rest = rest
        keep_a, send_a, keep_b, send_b, pre, weight, tiles, sums, sems = rest
        column = col_ref
    else:
        pre_hbm, grad_hbm, weight_hbm, tiles_hbm, pre_ref, local_ref, send_ref, places, column, *rest = rest
        pre, grad, weight, tiles, sums, sems = rest
    width = weight.shape[0]
    rows = pre.shape[0] // CHUNKS
    count = tiles.shape[0] // CHUNKS
    core, p, q = whereabouts()
    half = core if own else 1 - core
    some = pl.ds(pl.multiple_of(half * width, width), width)
    weight_copy = pltpu.make_async_copy(weight_hbm.at[some], weight, sems.at[0])
    weight_copy.start()
    if own:
        flag_ref[0] = core
        main_sums = sums.at[pl.ds(blocks, main)]
        recv_copy = pltpu.make_async_copy(recv_ref, main_sums, sems.at[1])
        recv_copy.start()
    chunks = []
    for i in range(CHUNKS):
        at = pl.ds(i * rows, rows)
        copies = [pltpu.make_async_copy(pre_hbm.at[at], pre.at[at], sems.at[2 + 3 * i])]
        if not own:
            copies.append(pltpu.make_async_copy(grad_hbm.at[at], grad.at[at], sems.at[3 + 3 * i]))
        some_tiles = pl.ds(i * count, count)
        copies.append(
            pltpu.make_async_copy(tiles_hbm.at[some_tiles], tiles.at[some_tiles], sems.at[4 + 3 * i])
        )
        for copy in copies:
            copy.start()
        chunks.append(copies)
    sums[0:blocks] = jnp.zeros((blocks,) + sums.shape[1:], F32)
    sums[blocks + main :] = jnp.zeros((over,) + sums.shape[1:], F32)
    if not own:
        sums[blocks : blocks + main] = jnp.zeros((main,) + sums.shape[1:], F32)
    if not own:
        slot_places(count_ref, places)

        def place_tile(t, _):
            col = col_ref[t]
            slot = jnp.maximum(col - blocks, 0)
            column[t] = jnp.where(col < blocks, col, blocks + places[slot])
            return 0

        lax.fori_loop(0, tiles.shape[0], place_tile, 0)
    weight_copy.wait()
    weight_high, weight_low = split(weight[...])
    contract = (((1,), (1,)), ((), ()))
    pre_copies = []
    for i in range(CHUNKS):
        at = pl.ds(i * rows, rows)
        *copies, tiles_copy = chunks[i]
        for copy in copies:
            copy.wait()
        if own:
            pre_grad = pre[at]
        else:
            pre_grad = jnp.where(pre[at] > 0, grad[at], 0.0)
            grad[at] = pre_grad
            pre_copy = pltpu.make_async_copy(grad.at[at], pre_ref.at[at], sems.at[2 + 3 * i])
            pre_copy.start()
            pre_copies.append(pre_copy)
        pre_high, pre_low = split(pre_grad)
        part = lax.dot_general(weight_high, pre_high, contract, preferred_element_type=F32)
        part += lax.dot_general(weight_high, pre_low, contract, preferred_element_type=F32)
        part += lax.dot_general(weight_low, pre_high, contract, preferred_element_type=F32)
        row_high, row_low = split(part)
        tiles_copy.wait()
        if own and i == 0:
            recv_copy.wait()
        for r in range(rows // BLOCK):
            mine = slice(r * BLOCK, (r + 1) * BLOCK)
            high = row_high[:, mine]
            left = jnp.concatenate([high, high, row_low[:, mine]], axis=1)
            each = count * BLOCK // rows
            for k in range(0, each, 2):
                t = i * count + r * each + k
                first_high, first_low = split(tiles[t])
                next_high, next_low = split(tiles[t + 1])
                high = jnp.concatenate([first_high, next_high], axis=1)
                low = jnp.concatenate([first_low, next_low], axis=1)
                right = jnp.concatenate([high, low, high], axis=0)
                product = jnp.dot(left, right, preferred_element_type=F32)
                sums[column[t]] += product[:, :BLOCK]
                sums[column[t + 1]] += product[:, BLOCK:]

    copies = []

    def out(source, target):
        copy = pltpu.make_async_copy(source, target, sems.at[2 + 3 * CHUNKS + len(copies)])
        copy.start()
        copies.append(copy)

    if own:
        some = main // 2
        share = width // 4

        def piece(first, p_at, q_at, target):
            share_rows = pl.ds(pl.multiple_of((p_at * 2 + q_at) * share, share), share)
            out(sums.at[pl.ds(blocks + first, some), share_rows], target)

        for k in range(2):
            piece(0, k, 1 - q, send_a.at[k])
            piece(some, 1 - p, k, send_b.at[k])
        for k in range(2):
            piece(0, k, q, keep_a.at[k])
            piece(some, p, k, keep_b.at[k])
    else:
        out(sums.at[pl.ds(blocks, main)], send_ref)
    out(sums.at[pl.ds(0, blocks)], local_ref)
    for copy in pre_copies + copies:
        copy.wait()


def tile_sums(
    tile_col, halo_count, weight, tile_vals, main, over, preact=None, grad_out=None,
    pre_grad=None, recv=None,
):
    own = recv is not None
    node_rows, feat = (pre_grad if own else preact).shape
    width = weight.shape[0] // 2
    blocks = node_rows // BLOCK
    some = main // 2
    anywhere = pl.BlockSpec(memory_space=pl.ANY)
    local = pltpu.VMEM((blocks, width, BLOCK), F32)
    piece = jax.ShapeDtypeStruct((2, some, width // 4, BLOCK), F32)
    if own:
        args = [pre_grad, weight, tile_vals, recv]
        flag = jax.ShapeDtypeStruct((1,), jnp.int32)
        out_shape = [local, flag] + [piece] * 4
    else:
        args = [preact, grad_out, weight, tile_vals]
        out_shape = [
            jax.ShapeDtypeStruct((node_rows, feat), F32),
            local,
            pltpu.VMEM((main, width, BLOCK), F32),
            jax.ShapeDtypeStruct((main + over,), jnp.int32),
            jax.ShapeDtypeStruct(tile_col.shape, jnp.int32),
        ]
    scratch = [pltpu.VMEM((node_rows, feat), F32)]
    if not own:
        scratch.append(pltpu.VMEM((node_rows, feat), F32))
    scratch += [
        pltpu.VMEM((width, feat), F32),
        pltpu.VMEM(tile_vals.shape, F32),
        pltpu.VMEM((blocks + main + over, width, BLOCK), F32),
        pltpu.SemaphoreType.DMA((2 + 3 * CHUNKS + 10,)),
    ]
    return pl.pallas_call(
        functools.partial(tile_kernel, own, blocks, main, over),
        out_shape=out_shape,
        in_specs=[pl.BlockSpec(memory_space=pltpu.SMEM)] * 2 + [anywhere] * len(args),
        out_specs=[
            pl.BlockSpec(memory_space=pltpu.SMEM) if x.dtype == jnp.int32 else anywhere
            for x in out_shape
        ],
        scratch_shapes=scratch,
        compiler_params=limit(LIMIT_OWN if own else LIMIT_OTHER),
        cost_estimate=pl.CostEstimate(
            flops=6 * (tile_vals.size + node_rows * feat) * width,
            bytes_accessed=14 * 1024 * 1024,
            transcendentals=0,
        ),
        name="own_tile_sums" if own else "other_tile_sums",
    )(tile_col, halo_count, *args)


IN_VMEM = pl.BlockSpec(memory_space=pltpu.VMEM)
IN_SMEM = pl.BlockSpec(memory_space=pltpu.SMEM)
ANYWHERE = pl.BlockSpec(memory_space=pl.ANY)


def second_kernel(keep_a, recv_a, keep_b, recv_b, *rest):
    keep, send_a, send_b = rest[-3:]
    _, p, q = whereabouts()
    send_a[...] = keep_a[1 - p] + recv_a[1 - p]
    send_b[...] = keep_b[1 - q] + recv_b[1 - q]
    keep[0] = keep_a[p] + recv_a[p]
    keep[1] = keep_b[q] + recv_b[q]


def second_sums(keep_a, recv_a, keep_b, recv_b, after):
    send = jax.ShapeDtypeStruct(keep_a.shape[1:], F32)
    out_shape = [jax.ShapeDtypeStruct(keep_a.shape, F32), send, send]
    return small(
        second_kernel,
        out_shape,
        [keep_a, recv_a, keep_b, recv_b, *after],
        "second_sums",
        [IN_VMEM] * 4 + [ANYWHERE] * len(after),
    )


def third_kernel(places, keep, recv_a, recv_b, after, out, total):
    del after
    half = recv_a.shape[0]
    main = 2 * half
    total[0:half] = keep[0] + recv_a[...]
    total[half:main] = keep[1] + recv_b[...]
    total[main:] = jnp.zeros_like(total[main:])
    for slot in range(out.shape[0]):
        out[slot] = total[places[slot]]


def third_sums(places, keep, recv_a, recv_b, after):
    shape = (places.shape[0],) + keep.shape[2:]
    return small(
        third_kernel,
        jax.ShapeDtypeStruct(shape, F32),
        [places, keep, recv_a, recv_b, after],
        "third_sums",
        [IN_SMEM] + [IN_VMEM] * 3 + [ANYWHERE],
        scratch=[pltpu.VMEM(shape, F32)],
    )


def small(
    kernel, out_shape, args, name, specs=None, scratch=(), mebibytes=LIMIT_SMALL, flops=None
):
    size = max(x.size for x in args)
    return pl.pallas_call(
        kernel,
        out_shape=out_shape,
        in_specs=specs or [IN_VMEM] * len(args),
        out_specs=jax.tree.map(lambda _: IN_VMEM, out_shape),
        scratch_shapes=scratch,
        cost_estimate=pl.CostEstimate(
            flops=flops or size, bytes_accessed=12 * size, transcendentals=0
        ),
        compiler_params=limit(mebibytes),
        name=name,
    )(*args)


def sort_kernel(self_term, neigh_term, keep, send):
    core, _, _ = whereabouts()
    pieces, columns, rows, _ = keep.shape

    def copy(source, target):
        for g in range(pieces):
            for c in range(columns):
                some = (slice(g * rows, (g + 1) * rows), slice(c * BLOCK, (c + 1) * BLOCK))
                target[g, c] = source[some]

    @pl.when(core == 0)
    def _():
        copy(self_term, keep)
        copy(neigh_term, send)

    @pl.when(core != 0)
    def _():
        copy(neigh_term, keep)
        copy(self_term, send)


def grads_kernel(whole, other, self_grad, neigh_grad):
    core, _, _ = whereabouts()
    pieces, columns, rows, _ = whole.shape

    def copy(source, target):
        for g in range(pieces):
            for c in range(columns):
                some = (slice(g * rows, (g + 1) * rows), slice(c * BLOCK, (c + 1) * BLOCK))
                target[some] = source[g, c]

    @pl.when(core == 0)
    def _():
        copy(whole, self_grad)
        copy(other, neigh_grad)

    @pl.when(core != 0)
    def _():
        copy(other, self_grad)
        copy(whole, neigh_grad)


def scatter_kernel(axis_of, count, *rest):
    terms = rest[:count]
    outs = rest[-4:]
    me = axis_of(lax.axis_index("group"))
    for away, out in enumerate(outs):
        at = (me + away) & 3
        total = terms[0][at]
        for term in terms[1:]:
            total += term[at]
        out[...] = total


def scatter(axis_of, terms, name, after=()):
    piece = jax.ShapeDtypeStruct(terms[0].shape[1:], F32)
    return small(
        functools.partial(scatter_kernel, axis_of, len(terms)),
        [piece] * 4,
        [*terms, *after],
        name,
        [IN_VMEM] * len(terms) + [IN_SMEM] * len(after),
    )


def sum_kernel(*rest):
    *terms, out = rest
    total = terms[0][...]
    for term in terms[1:]:
        total += term[...]
    out[...] = total


def chips_kernel(scale, mine, pair, far_one, far_two, after, out):
    del after
    out[...] = ((mine[...] + pair[...]) + (far_one[...] + far_two[...])) * scale


def pass_kernel(value, *rest):
    rest[-1][...] = value[...]


def gather_kernel(axis_of, *rest):
    pieces = rest[:4]
    out = rest[-1]
    me = axis_of(lax.axis_index("group"))
    for away, piece in enumerate(pieces):
        out[(me - away) & 3] = piece[...]


def gather(axis_of, pieces, name, after=()):
    whole = jax.ShapeDtypeStruct((4,) + pieces[0].shape, F32)
    specs = [IN_VMEM] * 4 + [ANYWHERE] * len(after)
    return small(functools.partial(gather_kernel, axis_of), whole, [*pieces, *after], name, specs)


def place_kernel(count_ref, target_ref, arrived, after, send, *keeps):
    del after
    core, _, _ = whereabouts()
    chip = lax.axis_index("local") >> 1
    group = lax.axis_index("group")
    sources = count_ref.shape[0]
    capacity = arrived.shape[0] // sources
    blocks = send.shape[1]
    shift = blocks.bit_length() - 1
    for out in (send, *keeps):
        out[...] = jnp.zeros_like(out)

    @pl.loop(0, sources)
    def _(source):
        count = count_ref[source, group]
        for j in range(capacity):
            target = target_ref[source, group * capacity + j]
            member = lax.shift_right_logical(target, shift)
            block = target & (blocks - 1)
            away = (lax.shift_right_logical(member, 1) - chip) & 3
            mine = (member & 1) == core

            @pl.when(j < count)
            def _():
                @pl.when(jnp.logical_not(mine))
                def _():
                    send[away, block] += arrived[source * capacity + j]

                @pl.when(mine)
                def _():
                    for k, keep in enumerate(keeps):

                        @pl.when(away == k)
                        def _():
                            keep[block] += arrived[source * capacity + j]


def place(halo_count, halo_target, arrived, after, blocks):
    keep = jax.ShapeDtypeStruct((blocks,) + arrived.shape[1:], F32)
    send = jax.ShapeDtypeStruct((4,) + keep.shape, F32)
    specs = [IN_SMEM, IN_SMEM, IN_VMEM, ANYWHERE]
    args = [halo_count, halo_target, arrived, after]
    return small(place_kernel, [send] + [keep] * 4, args, "place", specs)


def join_kernel(*rest):
    *keeps, swapped = rest[: len(rest) // 2 + 1]
    for k, out in enumerate(rest[len(rest) // 2 + 1 :]):
        out[0] = keeps[k][...]
        out[1] = swapped[k + 1]


def self_kernel(pre_grad, weight, other_local, own_local, after, out, total):
    del after
    core, _, _ = whereabouts()
    width = own_local.shape[1]
    own = pl.ds(pl.multiple_of(core * width, width), width)
    other = pl.ds(pl.multiple_of((1 - core) * width, width), width)
    contract = (((1,), (1,)), ((), ()))
    weight_high, weight_low = split(weight[...])
    rows = out.shape[0] // 4
    for i in range(4):
        at = slice(i * rows, (i + 1) * rows)
        high, low = split(pre_grad[at])
        rows_of = lax.dot_general(high, weight_high, contract, preferred_element_type=F32)
        rows_of += lax.dot_general(high, weight_low, contract, preferred_element_type=F32)
        rows_of += lax.dot_general(low, weight_high, contract, preferred_element_type=F32)
        out[at] = rows_of
    for b in range(own_local.shape[0]):
        total[b, own] = own_local[b]
        total[b, other] = other_local[b]
        out[b * BLOCK : (b + 1) * BLOCK] += total[b].T


def finish_kernel(base, keep, swapped, *rest):
    *received, out, total, rows, sems = rest
    core, _, _ = whereabouts()
    chip = lax.axis_index("local") >> 1
    blocks, share, _ = keep.shape
    pieces = [keep, swapped.at[0]] + [some.at[k] for some in received for k in range(2)]
    copies = []
    for b in range(blocks):
        for k, some in enumerate(pieces):
            source = (chip - AWAY[k // 2]) & 3
            side = source >> 1
            quarter = side * 2 + ((source + side) & 1)
            first = core if k % 2 == 0 else 1 - core
            start = pl.multiple_of((first * 4 + quarter) * share, share)
            total[b, pl.ds(start, share)] = some[b]
        at = slice(b * BLOCK, (b + 1) * BLOCK)
        rows[at] = base[at] + total[b].T
        copy = pltpu.make_async_copy(rows.at[at], out.at[at], sems.at[b])
        copy.start()
        copies.append(copy)
    for copy in copies:
        copy.wait()


def finish(base, keep, swapped, received):
    node_rows, feat = base.shape
    blocks = keep.shape[0]
    return pl.pallas_call(
        finish_kernel,
        out_shape=jax.ShapeDtypeStruct(base.shape, F32),
        in_specs=[IN_VMEM] * (3 + len(received)),
        out_specs=ANYWHERE,
        scratch_shapes=[
            pltpu.VMEM((blocks, feat, BLOCK), F32),
            pltpu.VMEM((node_rows, feat), F32),
            pltpu.SemaphoreType.DMA((blocks,)),
        ],
        cost_estimate=pl.CostEstimate(
            flops=2 * base.size, bytes_accessed=16 * base.size, transcendentals=0
        ),
        compiler_params=limit(8),
        name="finish",
    )(base, keep, swapped, *received)


def on_device(
    features,
    aggregated,
    preact,
    grad_out,
    w_self,
    w_neigh,
    tile_vals,
    tile_col,
    halo_count,
    halo_target,
):
    high = lax.Precision.HIGH
    node_rows, width = features.shape
    blocks = node_rows // BLOCK
    groups = lax.axis_size("group")
    members = lax.axis_size("local")
    slot_count = halo_target.shape[1]
    dead = slot_count - MAIN
    swap = [(i, i ^ 1) for i in range(members)]
    pairs = [(i, i ^ 2) for i in range(members)]
    across = [(i, members - 2 - (i - i % 2) + i % 2) for i in range(members)]
    along_x = [[(i, (i + 2 * k) % members) for i in range(members)] for k in range(4)]
    along_y = [[(i, (i + 4 * k) % groups) for i in range(groups)] for k in range(4)]
    along_z = [[(i, i // 4 * 4 + (i + k) % 4) for i in range(groups)] for k in range(4)]

    pre_grad, other_local, send, places, column = tile_sums(
        tile_col, halo_count, w_neigh, tile_vals, MAIN, dead, preact=preact, grad_out=grad_out
    )
    recv = lax.ppermute(send, "local", swap)
    own_local, flag, keep_a, send_a, keep_b, send_b = tile_sums(
        column, halo_count, w_neigh, tile_vals, MAIN, dead, pre_grad=pre_grad, recv=recv
    )
    recv_a = lax.ppermute(send_a, "local", pairs)
    recv_b = lax.ppermute(send_b, "local", across)

    contract = (((0,), (0,)), ((), ()))
    self_term = lax.dot_general(
        features, pre_grad, contract, precision=high, preferred_element_type=F32
    )
    neigh_term = lax.dot_general(
        aggregated, pre_grad, contract, precision=high, preferred_element_type=F32
    )
    pieces = jax.ShapeDtypeStruct((groups, width // BLOCK, width // groups, BLOCK), F32)
    stay, leave = small(sort_kernel, [pieces] * 2, [self_term, neigh_term], "sort_terms")
    by_y = (4, groups // 4) + pieces.shape[1:]
    stay, leave = stay.reshape(by_y), lax.ppermute(leave, "local", swap).reshape(by_y)
    mine, *sends = scatter(lambda g: g >> 2, [stay, leave], "sum_cores", [flag])
    terms = [mine] + [
        lax.ppermute(some, "group", along_y[k + 1]) for k, some in enumerate(sends)
    ]
    mine, *sends = scatter(lambda g: g & 3, terms, "sum_y")
    terms = [mine] + [
        lax.ppermute(some, "group", along_z[k + 1]) for k, some in enumerate(sends)
    ]

    base = small(
        self_kernel,
        jax.ShapeDtypeStruct(pre_grad.shape, F32),
        [pre_grad, w_self, other_local, own_local, mine],
        "self_rows",
        [IN_VMEM] * 4 + [ANYWHERE],
        scratch=[pltpu.VMEM((blocks, width, BLOCK), F32)],
        mebibytes=16,
        flops=6 * pre_grad.size * width,
    )
    keep, send_a, send_b = second_sums(keep_a, recv_a, keep_b, recv_b, [base, terms[1]])
    recv_a = lax.ppermute(send_a, "local", across)
    recv_b = lax.ppermute(send_b, "local", pairs)
    share_shape = jax.ShapeDtypeStruct(mine.shape, F32)
    share = small(sum_kernel, share_shape, terms, "sum_z")
    terms = [share] + [lax.ppermute(share, "local", p) for p in (pairs, across, along_x[2])]
    shares = third_sums(places, keep, recv_a, recv_b, terms[1])
    arrived = lax.all_to_all(shares, "group", split_axis=0, concat_axis=0, tiled=True)
    scale = float(node_rows * groups * members) ** (-0.5)
    share = small(
        functools.partial(chips_kernel, scale),
        share_shape,
        [*terms, shares],
        "sum_chips",
        [IN_VMEM] * 4 + [ANYWHERE],
    )
    terms = [share] + [lax.ppermute(share, "group", along_z[k]) for k in range(1, 4)]
    row = gather(lambda g: g & 3, terms, "gather_z")

    send, *keeps = place(halo_count, halo_target, arrived, row, blocks)
    swapped = lax.ppermute(send, "local", swap)
    joined = jax.ShapeDtypeStruct((2,) + keeps[0].shape, F32)
    joined = small(join_kernel, [joined] * 3, [*keeps[1:], swapped], "join")
    received = [lax.ppermute(joined[k - 1], "local", along_x[k]) for k in AWAY[1:]]

    row = small(
        pass_kernel,
        jax.ShapeDtypeStruct(row.shape, F32),
        [row, joined[0]],
        "pass",
        [IN_VMEM, ANYWHERE],
    )
    rows = [row] + [lax.ppermute(row, "group", along_y[k]) for k in range(1, 4)]
    whole = gather(lambda g: g >> 2, rows, "gather_y", received).reshape(pieces.shape)
    other = lax.ppermute(whole, "local", swap)
    square = jax.ShapeDtypeStruct(self_term.shape, F32)
    self_grad, neigh_grad = small(grads_kernel, [square] * 2, [whole, other], "sort_grads")

    node_grad = finish(base, keeps[0], swapped, received)
    return (node_grad, self_grad, neigh_grad)


def solution(mesh):
    in_specs = (
        P(("group", "local"), None),
        P(("group", "local"), None),
        P(("group", "local"), None),
        P(("group", "local"), None),
        P(),
        P(),
        P(("group", "local"), None, None),
        P(("group", "local")),
        P(),
        P(),
    )
    out_specs = (P(("group", "local"), None), P(), P())
    return jax.shard_map(
        on_device, mesh=mesh, in_specs=in_specs, out_specs=out_specs, check_vma=False
    )
```

```python
import functools

import jax
import jax.numpy as jnp
from jax import lax
from jax.experimental import pallas as pl
from jax.experimental.pallas import tpu as pltpu
from jax.sharding import PartitionSpec as P

F32 = jnp.float32
BF16 = jnp.bfloat16
BLOCK = 128
CHUNKS = 2
MAIN = 30
LIMIT_OTHER = 52
LIMIT_OWN = 20
LIMIT_SMALL = 6
AWAY = (0, 1, 3, 2)


def split(x):
    high = x.astype(BF16)
    low = (x - high.astype(F32)).astype(BF16)
    return high, low


def limit(mebibytes):
    return pltpu.CompilerParams(vmem_limit_bytes=mebibytes * 1024 * 1024)


def whereabouts():
    member = lax.axis_index("local")
    chip = member >> 1
    side = chip >> 1
    return member & 1, side, (chip + side) & 1


def slot_places(count_ref, places):
    slots = places.shape[0]
    owners = count_ref.shape[1]
    capacity = slots // owners
    group = lax.axis_index("group")

    def owner(o, carry):
        live, dead = carry
        count = count_ref[group, o]
        for j in range(capacity):
            is_live = j < count
            places[o * capacity + j] = jnp.where(is_live, live, slots - 1 - dead)
            live = live + is_live.astype(jnp.int32)
            dead = dead + 1 - is_live.astype(jnp.int32)
        return live, dead

    zero = jnp.int32(0)
    lax.fori_loop(0, owners, owner, (zero, zero))


def tile_kernel(own, blocks, main, over, col_ref, count_ref, *rest):
    if own:
        pre_hbm, weight_hbm, tiles_hbm, recv_ref, local_ref, flag_ref, *rest = rest
        keep_a, send_a, keep_b, send_b, pre, weight, tiles, sums, sems = rest
        column = col_ref
    else:
        pre_hbm, grad_hbm, weight_hbm, tiles_hbm, pre_ref, local_ref, send_ref, places, column, *rest = rest
        pre, grad, weight, tiles, sums, sems = rest
    width = weight.shape[0]
    rows = pre.shape[0] // CHUNKS
    count = tiles.shape[0] // CHUNKS
    core, p, q = whereabouts()
    half = core if own else 1 - core
    some = pl.ds(pl.multiple_of(half * width, width), width)
    weight_copy = pltpu.make_async_copy(weight_hbm.at[some], weight, sems.at[0])
    weight_copy.start()
    if own:
        flag_ref[0] = core
        main_sums = sums.at[pl.ds(blocks, main)]
        recv_copy = pltpu.make_async_copy(recv_ref, main_sums, sems.at[1])
        recv_copy.start()
    chunks = []
    for i in range(CHUNKS):
        at = pl.ds(i * rows, rows)
        copies = [pltpu.make_async_copy(pre_hbm.at[at], pre.at[at], sems.at[2 + 3 * i])]
        if not own:
            copies.append(pltpu.make_async_copy(grad_hbm.at[at], grad.at[at], sems.at[3 + 3 * i]))
        some_tiles = pl.ds(i * count, count)
        copies.append(
            pltpu.make_async_copy(tiles_hbm.at[some_tiles], tiles.at[some_tiles], sems.at[4 + 3 * i])
        )
        for copy in copies:
            copy.start()
        chunks.append(copies)
    sums[0:blocks] = jnp.zeros((blocks,) + sums.shape[1:], F32)
    sums[blocks + main :] = jnp.zeros((over,) + sums.shape[1:], F32)
    if not own:
        sums[blocks : blocks + main] = jnp.zeros((main,) + sums.shape[1:], F32)
    if not own:
        slot_places(count_ref, places)

        def place_tile(t, _):
            col = col_ref[t]
            slot = jnp.maximum(col - blocks, 0)
            column[t] = jnp.where(col < blocks, col, blocks + places[slot])
            return 0

        lax.fori_loop(0, tiles.shape[0], place_tile, 0)
    weight_copy.wait()
    weight_high, weight_low = split(weight[...])
    contract = (((1,), (1,)), ((), ()))
    pre_copies = []
    for i in range(CHUNKS):
        at = pl.ds(i * rows, rows)
        *copies, tiles_copy = chunks[i]
        for copy in copies:
            copy.wait()
        if own:
            pre_grad = pre[at]
        else:
            pre_grad = jnp.where(pre[at] > 0, grad[at], 0.0)
            grad[at] = pre_grad
            pre_copy = pltpu.make_async_copy(grad.at[at], pre_ref.at[at], sems.at[2 + 3 * i])
            pre_copy.start()
            pre_copies.append(pre_copy)
        pre_high, pre_low = split(pre_grad)
        part = lax.dot_general(weight_high, pre_high, contract, preferred_element_type=F32)
        part += lax.dot_general(weight_high, pre_low, contract, preferred_element_type=F32)
        part += lax.dot_general(weight_low, pre_high, contract, preferred_element_type=F32)
        row_high, row_low = split(part)
        tiles_copy.wait()
        if own and i == 0:
            recv_copy.wait()
        for r in range(rows // BLOCK):
            mine = slice(r * BLOCK, (r + 1) * BLOCK)
            high = row_high[:, mine]
            left = jnp.concatenate([high, high, row_low[:, mine]], axis=1)
            each = count * BLOCK // rows
            for k in range(0, each, 2):
                t = i * count + r * each + k
                first_high, first_low = split(tiles[t])
                next_high, next_low = split(tiles[t + 1])
                high = jnp.concatenate([first_high, next_high], axis=1)
                low = jnp.concatenate([first_low, next_low], axis=1)
                right = jnp.concatenate([high, low, high], axis=0)
                product = jnp.dot(left, right, preferred_element_type=F32)
                sums[column[t]] += product[:, :BLOCK]
                sums[column[t + 1]] += product[:, BLOCK:]

    copies = []

    def out(source, target):
        copy = pltpu.make_async_copy(source, target, sems.at[2 + 3 * CHUNKS + len(copies)])
        copy.start()
        copies.append(copy)

    if own:
        some = main // 2
        share = width // 4

        def piece(first, p_at, q_at, target):
            share_rows = pl.ds(pl.multiple_of((p_at * 2 + q_at) * share, share), share)
            out(sums.at[pl.ds(blocks + first, some), share_rows], target)

        for k in range(2):
            piece(0, k, 1 - q, send_a.at[k])
            piece(some, 1 - p, k, send_b.at[k])
        for k in range(2):
            piece(0, k, q, keep_a.at[k])
            piece(some, p, k, keep_b.at[k])
    else:
        out(sums.at[pl.ds(blocks, main)], send_ref)
    out(sums.at[pl.ds(0, blocks)], local_ref)
    for copy in pre_copies + copies:
        copy.wait()


def tile_sums(
    tile_col, halo_count, weight, tile_vals, main, over, preact=None, grad_out=None,
    pre_grad=None, recv=None,
):
    own = recv is not None
    node_rows, feat = (pre_grad if own else preact).shape
    width = weight.shape[0] // 2
    blocks = node_rows // BLOCK
    some = main // 2
    anywhere = pl.BlockSpec(memory_space=pl.ANY)
    local = jax.ShapeDtypeStruct((blocks, width, BLOCK), F32)
    piece = jax.ShapeDtypeStruct((2, some, width // 4, BLOCK), F32)
    if own:
        args = [pre_grad, weight, tile_vals, recv]
        flag = jax.ShapeDtypeStruct((1,), jnp.int32)
        out_shape = [local, flag] + [piece] * 4
    else:
        args = [preact, grad_out, weight, tile_vals]
        out_shape = [
            jax.ShapeDtypeStruct((node_rows, feat), F32),
            local,
            pltpu.VMEM((main, width, BLOCK), F32),
            jax.ShapeDtypeStruct((main + over,), jnp.int32),
            jax.ShapeDtypeStruct(tile_col.shape, jnp.int32),
        ]
    scratch = [pltpu.VMEM((node_rows, feat), F32)]
    if not own:
        scratch.append(pltpu.VMEM((node_rows, feat), F32))
    scratch += [
        pltpu.VMEM((width, feat), F32),
        pltpu.VMEM(tile_vals.shape, F32),
        pltpu.VMEM((blocks + main + over, width, BLOCK), F32),
        pltpu.SemaphoreType.DMA((2 + 3 * CHUNKS + 10,)),
    ]
    return pl.pallas_call(
        functools.partial(tile_kernel, own, blocks, main, over),
        out_shape=out_shape,
        in_specs=[pl.BlockSpec(memory_space=pltpu.SMEM)] * 2 + [anywhere] * len(args),
        out_specs=[
            pl.BlockSpec(memory_space=pltpu.SMEM) if x.dtype == jnp.int32 else anywhere
            for x in out_shape
        ],
        scratch_shapes=scratch,
        compiler_params=limit(LIMIT_OWN if own else LIMIT_OTHER),
        cost_estimate=pl.CostEstimate(
            flops=6 * (tile_vals.size + node_rows * feat) * width,
            bytes_accessed=14 * 1024 * 1024,
            transcendentals=0,
        ),
        name="own_tile_sums" if own else "other_tile_sums",
    )(tile_col, halo_count, *args)


IN_VMEM = pl.BlockSpec(memory_space=pltpu.VMEM)
IN_SMEM = pl.BlockSpec(memory_space=pltpu.SMEM)
ANYWHERE = pl.BlockSpec(memory_space=pl.ANY)


def second_kernel(keep_a, recv_a, keep_b, recv_b, *rest):
    keep, send_a, send_b = rest[-3:]
    _, p, q = whereabouts()
    send_a[...] = keep_a[1 - p] + recv_a[1 - p]
    send_b[...] = keep_b[1 - q] + recv_b[1 - q]
    keep[0] = keep_a[p] + recv_a[p]
    keep[1] = keep_b[q] + recv_b[q]


def second_sums(keep_a, recv_a, keep_b, recv_b, after):
    send = jax.ShapeDtypeStruct(keep_a.shape[1:], F32)
    out_shape = [jax.ShapeDtypeStruct(keep_a.shape, F32), send, send]
    return small(
        second_kernel,
        out_shape,
        [keep_a, recv_a, keep_b, recv_b, *after],
        "second_sums",
        [IN_VMEM] * 4 + [ANYWHERE] * len(after),
    )


def third_kernel(places, keep, recv_a, recv_b, after, out, total):
    del after
    half = recv_a.shape[0]
    main = 2 * half
    total[0:half] = keep[0] + recv_a[...]
    total[half:main] = keep[1] + recv_b[...]
    total[main:] = jnp.zeros_like(total[main:])
    for slot in range(out.shape[0]):
        out[slot] = total[places[slot]]


def third_sums(places, keep, recv_a, recv_b, after):
    shape = (places.shape[0],) + keep.shape[2:]
    return small(
        third_kernel,
        jax.ShapeDtypeStruct(shape, F32),
        [places, keep, recv_a, recv_b, after],
        "third_sums",
        [IN_SMEM] + [IN_VMEM] * 3 + [ANYWHERE],
        scratch=[pltpu.VMEM(shape, F32)],
    )


def small(
    kernel, out_shape, args, name, specs=None, scratch=(), mebibytes=LIMIT_SMALL, flops=None
):
    size = max(x.size for x in args)
    return pl.pallas_call(
        kernel,
        out_shape=out_shape,
        in_specs=specs or [IN_VMEM] * len(args),
        out_specs=jax.tree.map(lambda _: IN_VMEM, out_shape),
        scratch_shapes=scratch,
        cost_estimate=pl.CostEstimate(
            flops=flops or size, bytes_accessed=12 * size, transcendentals=0
        ),
        compiler_params=limit(mebibytes),
        name=name,
    )(*args)


def sort_kernel(self_term, neigh_term, keep, send):
    core, _, _ = whereabouts()
    pieces, columns, rows, _ = keep.shape

    def copy(source, target):
        for g in range(pieces):
            for c in range(columns):
                some = (slice(g * rows, (g + 1) * rows), slice(c * BLOCK, (c + 1) * BLOCK))
                target[g, c] = source[some]

    @pl.when(core == 0)
    def _():
        copy(self_term, keep)
        copy(neigh_term, send)

    @pl.when(core != 0)
    def _():
        copy(neigh_term, keep)
        copy(self_term, send)


def grads_kernel(whole, other, self_grad, neigh_grad):
    core, _, _ = whereabouts()
    pieces, columns, rows, _ = whole.shape

    def copy(source, target):
        for g in range(pieces):
            for c in range(columns):
                some = (slice(g * rows, (g + 1) * rows), slice(c * BLOCK, (c + 1) * BLOCK))
                target[some] = source[g, c]

    @pl.when(core == 0)
    def _():
        copy(whole, self_grad)
        copy(other, neigh_grad)

    @pl.when(core != 0)
    def _():
        copy(other, self_grad)
        copy(whole, neigh_grad)


def scatter_kernel(axis_of, count, *rest):
    terms = rest[:count]
    outs = rest[-4:]
    me = axis_of(lax.axis_index("group"))
    for away, out in enumerate(outs):
        at = (me + away) & 3
        total = terms[0][at]
        for term in terms[1:]:
            total += term[at]
        out[...] = total


def scatter(axis_of, terms, name, after=()):
    piece = jax.ShapeDtypeStruct(terms[0].shape[1:], F32)
    return small(
        functools.partial(scatter_kernel, axis_of, len(terms)),
        [piece] * 4,
        [*terms, *after],
        name,
        [IN_VMEM] * len(terms) + [IN_SMEM] * len(after),
    )


def sum_kernel(*rest):
    *terms, out = rest
    total = terms[0][...]
    for term in terms[1:]:
        total += term[...]
    out[...] = total


def chips_kernel(scale, mine, pair, far_one, far_two, after, out):
    del after
    out[...] = ((mine[...] + pair[...]) + (far_one[...] + far_two[...])) * scale


def pass_kernel(value, *rest):
    rest[-1][...] = value[...]


def gather_kernel(axis_of, *rest):
    pieces = rest[:4]
    out = rest[-1]
    me = axis_of(lax.axis_index("group"))
    for away, piece in enumerate(pieces):
        out[(me - away) & 3] = piece[...]


def gather(axis_of, pieces, name, after=()):
    whole = jax.ShapeDtypeStruct((4,) + pieces[0].shape, F32)
    specs = [IN_VMEM] * 4 + [ANYWHERE] * len(after)
    return small(functools.partial(gather_kernel, axis_of), whole, [*pieces, *after], name, specs)


def place_kernel(count_ref, target_ref, arrived, after, send, *keeps):
    del after
    core, _, _ = whereabouts()
    chip = lax.axis_index("local") >> 1
    group = lax.axis_index("group")
    sources = count_ref.shape[0]
    capacity = arrived.shape[0] // sources
    blocks = send.shape[1]
    shift = blocks.bit_length() - 1
    for out in (send, *keeps):
        out[...] = jnp.zeros_like(out)

    @pl.loop(0, sources)
    def _(source):
        count = count_ref[source, group]
        for j in range(capacity):
            target = target_ref[source, group * capacity + j]
            member = lax.shift_right_logical(target, shift)
            block = target & (blocks - 1)
            away = (lax.shift_right_logical(member, 1) - chip) & 3
            mine = (member & 1) == core

            @pl.when(j < count)
            def _():
                @pl.when(jnp.logical_not(mine))
                def _():
                    send[away, block] += arrived[source * capacity + j]

                @pl.when(mine)
                def _():
                    for k, keep in enumerate(keeps):

                        @pl.when(away == k)
                        def _():
                            keep[block] += arrived[source * capacity + j]


def place(halo_count, halo_target, arrived, after, blocks):
    keep = jax.ShapeDtypeStruct((blocks,) + arrived.shape[1:], F32)
    send = jax.ShapeDtypeStruct((4,) + keep.shape, F32)
    specs = [IN_SMEM, IN_SMEM, IN_VMEM, ANYWHERE]
    args = [halo_count, halo_target, arrived, after]
    return small(place_kernel, [send] + [keep] * 4, args, "place", specs)


def join_kernel(*rest):
    *keeps, swapped = rest[: len(rest) // 2 + 1]
    for k, out in enumerate(rest[len(rest) // 2 + 1 :]):
        out[0] = keeps[k][...]
        out[1] = swapped[k + 1]


def self_kernel(pre_grad, weight, other_local, own_local, after, out, total):
    del after
    core, _, _ = whereabouts()
    width = own_local.shape[1]
    own = pl.ds(pl.multiple_of(core * width, width), width)
    other = pl.ds(pl.multiple_of((1 - core) * width, width), width)
    contract = (((1,), (1,)), ((), ()))
    weight_high, weight_low = split(weight[...])
    rows = out.shape[0] // 4
    for i in range(4):
        at = slice(i * rows, (i + 1) * rows)
        high, low = split(pre_grad[at])
        rows_of = lax.dot_general(high, weight_high, contract, preferred_element_type=F32)
        rows_of += lax.dot_general(high, weight_low, contract, preferred_element_type=F32)
        rows_of += lax.dot_general(low, weight_high, contract, preferred_element_type=F32)
        out[at] = rows_of
    for b in range(own_local.shape[0]):
        total[b, own] = own_local[b]
        total[b, other] = other_local[b]
        out[b * BLOCK : (b + 1) * BLOCK] += total[b].T


def finish_kernel(base, keep, swapped, *rest):
    *received, out, total, rows, sems = rest
    core, _, _ = whereabouts()
    chip = lax.axis_index("local") >> 1
    blocks, share, _ = keep.shape
    pieces = [keep, swapped.at[0]] + [some.at[k] for some in received for k in range(2)]
    copies = []
    for b in range(blocks):
        for k, some in enumerate(pieces):
            source = (chip - AWAY[k // 2]) & 3
            side = source >> 1
            quarter = side * 2 + ((source + side) & 1)
            first = core if k % 2 == 0 else 1 - core
            start = pl.multiple_of((first * 4 + quarter) * share, share)
            total[b, pl.ds(start, share)] = some[b]
        at = slice(b * BLOCK, (b + 1) * BLOCK)
        rows[at] = base[at] + total[b].T
        copy = pltpu.make_async_copy(rows.at[at], out.at[at], sems.at[b])
        copy.start()
        copies.append(copy)
    for copy in copies:
        copy.wait()


def finish(base, keep, swapped, received):
    node_rows, feat = base.shape
    blocks = keep.shape[0]
    return pl.pallas_call(
        finish_kernel,
        out_shape=jax.ShapeDtypeStruct(base.shape, F32),
        in_specs=[IN_VMEM] * (3 + len(received)),
        out_specs=ANYWHERE,
        scratch_shapes=[
            pltpu.VMEM((blocks, feat, BLOCK), F32),
            pltpu.VMEM((node_rows, feat), F32),
            pltpu.SemaphoreType.DMA((blocks,)),
        ],
        cost_estimate=pl.CostEstimate(
            flops=2 * base.size, bytes_accessed=16 * base.size, transcendentals=0
        ),
        compiler_params=limit(8),
        name="finish",
    )(base, keep, swapped, *received)


def on_device(
    features,
    aggregated,
    preact,
    grad_out,
    w_self,
    w_neigh,
    tile_vals,
    tile_col,
    halo_count,
    halo_target,
):
    high = lax.Precision.HIGH
    node_rows, width = features.shape
    blocks = node_rows // BLOCK
    groups = lax.axis_size("group")
    members = lax.axis_size("local")
    slot_count = halo_target.shape[1]
    dead = slot_count - MAIN
    swap = [(i, i ^ 1) for i in range(members)]
    pairs = [(i, i ^ 2) for i in range(members)]
    across = [(i, members - 2 - (i - i % 2) + i % 2) for i in range(members)]
    along_x = [[(i, (i + 2 * k) % members) for i in range(members)] for k in range(4)]
    along_y = [[(i, (i + 4 * k) % groups) for i in range(groups)] for k in range(4)]
    along_z = [[(i, i // 4 * 4 + (i + k) % 4) for i in range(groups)] for k in range(4)]

    pre_grad, other_local, send, places, column = tile_sums(
        tile_col, halo_count, w_neigh, tile_vals, MAIN, dead, preact=preact, grad_out=grad_out
    )
    recv = lax.ppermute(send, "local", swap)
    own_local, flag, keep_a, send_a, keep_b, send_b = tile_sums(
        column, halo_count, w_neigh, tile_vals, MAIN, dead, pre_grad=pre_grad, recv=recv
    )
    recv_a = lax.ppermute(send_a, "local", pairs)
    recv_b = lax.ppermute(send_b, "local", across)

    contract = (((0,), (0,)), ((), ()))
    self_term = lax.dot_general(
        features, pre_grad, contract, precision=high, preferred_element_type=F32
    )
    neigh_term = lax.dot_general(
        aggregated, pre_grad, contract, precision=high, preferred_element_type=F32
    )
    pieces = jax.ShapeDtypeStruct((groups, width // BLOCK, width // groups, BLOCK), F32)
    stay, leave = small(sort_kernel, [pieces] * 2, [self_term, neigh_term], "sort_terms")
    by_y = (4, groups // 4) + pieces.shape[1:]
    stay, leave = stay.reshape(by_y), lax.ppermute(leave, "local", swap).reshape(by_y)
    mine, *sends = scatter(lambda g: g >> 2, [stay, leave], "sum_cores", [flag])
    terms = [mine] + [
        lax.ppermute(some, "group", along_y[k + 1]) for k, some in enumerate(sends)
    ]
    mine, *sends = scatter(lambda g: g & 3, terms, "sum_y")
    terms = [mine] + [
        lax.ppermute(some, "group", along_z[k + 1]) for k, some in enumerate(sends)
    ]

    base = small(
        self_kernel,
        jax.ShapeDtypeStruct(pre_grad.shape, F32),
        [pre_grad, w_self, other_local, own_local, mine],
        "self_rows",
        [IN_VMEM] * 4 + [ANYWHERE],
        scratch=[pltpu.VMEM((blocks, width, BLOCK), F32)],
        mebibytes=16,
        flops=6 * pre_grad.size * width,
    )
    keep, send_a, send_b = second_sums(keep_a, recv_a, keep_b, recv_b, [base])
    recv_a = lax.ppermute(send_a, "local", across)
    recv_b = lax.ppermute(send_b, "local", pairs)
    share_shape = jax.ShapeDtypeStruct(mine.shape, F32)
    share = small(sum_kernel, share_shape, terms, "sum_z")
    shares = third_sums(places, keep, recv_a, recv_b, share)
    arrived = lax.all_to_all(shares, "group", split_axis=0, concat_axis=0, tiled=True)
    terms = [share] + [lax.ppermute(share, "local", p) for p in (pairs, across, along_x[2])]
    scale = float(node_rows * groups * members) ** (-0.5)
    share = small(
        functools.partial(chips_kernel, scale),
        share_shape,
        [*terms, shares],
        "sum_chips",
        [IN_VMEM] * 4 + [ANYWHERE],
    )
    terms = [share] + [lax.ppermute(share, "group", along_z[k]) for k in range(1, 4)]
    row = gather(lambda g: g & 3, terms, "gather_z")

    send, *keeps = place(halo_count, halo_target, arrived, row, blocks)
    swapped = lax.ppermute(send, "local", swap)
    joined = jax.ShapeDtypeStruct((2,) + keeps[0].shape, F32)
    joined = small(join_kernel, [joined] * 3, [*keeps[1:], swapped], "join")
    received = [lax.ppermute(joined[k - 1], "local", along_x[k]) for k in AWAY[1:]]

    row = small(
        pass_kernel,
        jax.ShapeDtypeStruct(row.shape, F32),
        [row, joined[0]],
        "pass",
        [IN_VMEM, ANYWHERE],
    )
    rows = [row] + [lax.ppermute(row, "group", along_y[k]) for k in range(1, 4)]
    whole = gather(lambda g: g >> 2, rows, "gather_y", received).reshape(pieces.shape)
    other = lax.ppermute(whole, "local", swap)
    square = jax.ShapeDtypeStruct(self_term.shape, F32)
    self_grad, neigh_grad = small(grads_kernel, [square] * 2, [whole, other], "sort_grads")

    node_grad = finish(base, keeps[0], swapped, received)
    return (node_grad, self_grad, neigh_grad)


def solution(mesh):
    in_specs = (
        P(("group", "local"), None),
        P(("group", "local"), None),
        P(("group", "local"), None),
        P(("group", "local"), None),
        P(),
        P(),
        P(("group", "local"), None, None),
        P(("group", "local")),
        P(),
        P(),
    )
    out_specs = (P(("group", "local"), None), P(), P())
    return jax.shard_map(
        on_device, mesh=mesh, in_specs=in_specs, out_specs=out_specs, check_vma=False
    )
```
